32 devices in a mesh: parts: 2 (over x), blk: 8 (over z, y), helper: 2 (over core).
Axes of the slice: x: 2, y: 2, z: 4, core: 2. Of those that a mesh axis runs over, the one named last changes fastest.
Arguments:
- queries: bfloat16 [16384, 768], P(('parts', 'blk', 'helper')), parts along dimension 0, may hold values from -6 to 6
- query_block_cluster: int32 [128], P(('parts', 'blk', 'helper')), parts along dimension 0, may hold values from 0 to 63
- block_count: int32 [32], P(('parts', 'blk', 'helper')), parts along dimension 0, may hold values from 1 to 4, 40 in all
- references: bfloat16 [8192, 768], P(('parts', 'blk')), parts along dimension 0, may hold values from -6 to 6
- ref_cluster: int32 [8192], P(('parts', 'blk')), parts along dimension 0, may hold values from 0 to 63
- ref_rows: int32 [16], P(('parts', 'blk')), parts along dimension 0, may hold values from 1 to 512, 3072 in all
- cluster_beta: float32 [128], P('parts'), parts along dimension 0, may hold values from 0.5 to 2
- cluster_member_count: int32 [128], P('parts'), parts along dimension 0, may hold values from 24 to 97
Outputs:
- log_density: float32 [16384], P(('parts', 'blk', 'helper')), parts along dimension 0
The draws below stay inside these ranges and needn't reach their ends.
There are 2 independent parts, one for each index of `parts`. The reference program is written for one: setup_inputs(seed, part) draws one part's arguments, and reference() takes and returns one part's arrays. A program takes and returns all parts, laid end to end along the dimension named above; each array names one. Nothing has to cross between parts.
All inputs are finite; a program needn't handle non-finite values. No bound on the sum of `block_count` or of `ref_rows` on one device may be relied on, other than what follows from the above.
Results may differ from the reference program's by a relative error of at most 0.0003.
Values may be sent and summed in bfloat16 or wider, within the bound.
No kernel may reach another device: no remote copies, remote signals or barrier semaphores. Data moves between devices by JAX's collectives and lax.ppermute only.
A program may use at most 64 MiB of HBM per device.

```python
import math
import jax
import jax.numpy as jnp
import numpy as np
from jax import lax

D = 768
QB = 4
QBLK = 128
R_DEV = 512
C = 64
QROWS = 8192
QBLOCKS = 64
REFS = 4096
N_BLK = 8
N_HELPER = 2


def with_ends(array, stream_key, smallest, top_value):
    extent = array.shape
    spot = [jax.random.randint(jax.random.fold_in(stream_key, axis), (), 0, extent[axis]) for axis in range(len(extent))]
    array = array.at[tuple(spot)].set(smallest)
    longest = extent.index(max(extent))
    spot[longest] = (spot[longest] + 1) % extent[longest]
    return array.at[tuple(spot)].set(top_value)


def shard_levels(key, dims, shards, smallest, top_value):
    def one(axis_at, blocks):
        heights = jax.random.uniform(jax.random.fold_in(jax.random.fold_in(key, 6), axis_at), (blocks,), jnp.float32, smallest / len(shards), top_value / len(shards))
        return jnp.repeat(jnp.exp(heights), dims[axis_at] // blocks).reshape((-1,) + (1,) * (len(dims) - axis_at - 1))

    factor_of = one(*shards[0])
    for cut in shards[1:]:
        factor_of = factor_of * one(*cut)
    return factor_of


def split_up(number_of, total, bound, skew):
    weights = [(1 << 20) // math.isqrt(grade ** skew) + 1 for grade in range(2, number_of + 1)]
    surplus, given = total - bound - (number_of - 1), [1] * (number_of - 1)
    while surplus > 0:
        free = [i for i in range(number_of - 1) if given[i] < bound]
        whole, remaining = sum([weights[i] for i in free]), surplus
        for i in free:
            extra = min(bound - given[i], max(1, remaining * weights[i] // whole), surplus)
            given[i] = given[i] + extra
            surplus = surplus - extra
    return np.array([bound] + given)


def uneven_parts(own_key, count, total, reach, slope):
    if count == 2:
        one = jax.random.randint(own_key, (), max(1, total - reach), min(reach, total - 1) + 1)
        return jnp.stack([one, total - one])
    sizes = jnp.asarray(split_up(count, total, reach, slope), jnp.int32)
    twos = (count - 1) // 2
    donor, taker = sizes[1:1 + 2 * twos:2], sizes[2:2 + 2 * twos:2]
    slack = jnp.minimum(donor - 1, reach - taker)
    moved = jax.random.randint(jax.random.fold_in(own_key, 1), (twos,), 0, 1 << 20) % (slack + 1)
    sizes = sizes.at[1:1 + 2 * twos:2].set(donor - moved).at[2:2 + 2 * twos:2].set(taker + moved)
    return sizes[jax.random.permutation(jax.random.fold_in(own_key, 2), count)]


def bell_draw(rng, dims, scale, limit, cuts=(), kind=jnp.bfloat16):
    loudness = shard_levels(rng, dims, cuts, -0.22, 0.18) if cuts else 1.0
    values = jax.random.normal(rng, dims, jnp.float32) * scale * loudness
    return jnp.minimum(jnp.maximum(values, -limit), limit).astype(kind)


def setup_inputs(seed: int = 0, part: int = 0) -> dict:
    arg_keys = jax.random.split(jax.random.key(seed), 9)
    part_splits = jax.random.split(jax.random.fold_in(arg_keys[8], part), 9)
    queries = bell_draw(part_splits[0], (QROWS, D), 1.0, 6.0, ((0, 16),))
    query_block_cluster = with_ends(jax.random.randint(part_splits[1], (QBLOCKS,), 0, C), jax.random.fold_in(part_splits[1], 1), 0, C - 1).astype(jnp.int32)
    block_count = uneven_parts(part_splits[2], N_BLK * N_HELPER, N_BLK * N_HELPER * QB * 5 // 8, QB, 2).astype(jnp.int32)
    references = bell_draw(part_splits[3], (REFS, D), 1.0, 6.0, ((0, 8),))
    ref_cluster = with_ends(jax.random.randint(part_splits[4], (REFS,), 0, C), jax.random.fold_in(part_splits[4], 1), 0, C - 1).astype(jnp.int32)
    ref_rows = uneven_parts(part_splits[5], N_BLK, N_BLK * R_DEV * 3 // 4, R_DEV, 1).astype(jnp.int32)
    cluster_beta = jnp.clip(jnp.exp(jax.random.uniform(part_splits[6], (C,), jnp.float32, math.log(0.5), math.log(2.0))), 0.5, 2.0)
    cluster_member_count = with_ends(jax.random.randint(part_splits[7], (C,), max(1, N_BLK * R_DEV * 3 // (8 * C)), N_BLK * R_DEV * 3 // (2 * C) + 2), jax.random.fold_in(part_splits[7], 1), max(1, N_BLK * R_DEV * 3 // (8 * C)), (N_BLK * R_DEV * 3 // (2 * C) + 2) - 1).astype(jnp.int32)
    return {"queries": queries, "query_block_cluster": query_block_cluster, "block_count": block_count, "references": references, "ref_cluster": ref_cluster, "ref_rows": ref_rows, "cluster_beta": cluster_beta, "cluster_member_count": cluster_member_count}


def reference(queries, query_block_cluster, block_count, references, ref_cluster, ref_rows, cluster_beta, cluster_member_count):
    refs_all = references.shape[0]
    position = jnp.arange(refs_all, dtype=jnp.int32)
    shard_of = position // R_DEV
    live_rows = position % R_DEV < ref_rows[shard_of]
    live_ids = jnp.where(live_rows, ref_cluster, -1)
    nblocks = query_block_cluster.shape[0]
    block_index = jnp.arange(nblocks, dtype=jnp.int32)
    block_live = block_index % QB < block_count[block_index // QB]
    query_blocks = queries.reshape(nblocks, QBLK, D)
    factor = 1.0 / math.sqrt(D)

    def one_block(item):
        block, cluster, alive = item
        score = jnp.dot(block, references.T, preferred_element_type=jnp.float32) * factor
        beta = cluster_beta[cluster]
        weights = jnp.where(live_ids < 0, 0.0, jnp.where(live_ids == cluster, 1.0, 0.0625))
        gaussian_kernel = weights[None, :] * jnp.exp(beta * score - 0.5 * beta * beta)
        total = jnp.where(alive, lax.optimization_barrier(jnp.sum(gaussian_kernel, axis=1)), 0.0)
        return jnp.log1p(total / cluster_member_count[cluster].astype(jnp.float32))
    result = lax.map(one_block, (query_blocks, query_block_cluster, block_live))
    return result.reshape(nblocks * QBLK)
```

```python
import functools
import math

import jax
import jax.numpy as jnp
from jax import lax
from jax.experimental import pallas as pl
from jax.experimental.pallas import tpu as pltpu
from jax.sharding import PartitionSpec as P

LANES = 128
LOG2E = 1.4426950408889634
DEAD = -1.0e30


def shift(value, axis, by):
    length = lax.axis_size(axis)
    pairs = [(i, i + by) for i in range(length) if 0 <= i + by < length]
    return lax.ppermute(value, axis, pairs)


def swap(value, axis):
    length = lax.axis_size(axis)
    return lax.ppermute(value, axis, [(i, i ^ 1) for i in range(length)])


def score_kernel(
    tile_plan,
    nblk,
    nhelper,
    qblocks,
    with_prev,
    me_ref,
    meta_ref,
    beta_ref,
    ids_ref,
    *refs,
):
    ntiles = len(tile_plan)
    q_refs, refs = refs[:4], refs[4:]
    r_refs, refs = refs[:ntiles], refs[ntiles:]
    if with_prev:
        prev_ref, refs = refs[0], refs[1:]
    out_ref, qv, rv, q_list, r_list, q_sem, r_sem = refs
    blk, helper = me_ref[0], me_ref[1]
    width = qv.shape[1]
    id_rows = meta_ref.shape[1] - 1

    def r_copy(operand, slot):
        rows = pl.ds(pl.multiple_of(slot * LANES, LANES), LANES)
        return pltpu.make_async_copy(r_refs[operand], rv.at[rows], r_sem.at[slot])

    def q_copy(source, block, slot):
        rows = pl.ds(pl.multiple_of(slot * LANES, LANES), LANES)
        return pltpu.make_async_copy(
            q_refs[source].at[pl.ds(block * LANES, LANES)], qv.at[rows], q_sem.at[slot]
        )

    count = jnp.int32(0)
    for operand, (distance, chunk) in enumerate(tile_plan):
        shard = blk + distance
        inside = jnp.logical_and(shard >= 0, shard < nblk)
        shard = jnp.where(inside, shard, 0)
        tile = helper + nhelper * chunk
        rows = meta_ref[shard * nhelper, id_rows, qblocks + 1]
        live = jnp.logical_and(inside, rows > tile * LANES)

        @pl.when(live)
        def _(operand=operand, count=count, shard=shard, tile=tile, rows=rows):
            r_copy(operand, count).start()
            r_list[count, 0] = shard
            r_list[count, 1] = tile
            r_list[count, 2] = rows - tile * LANES

        count = count + live.astype(jnp.int32)
    odd = lax.rem(count, 2)

    @pl.when(odd == 1)
    def _(count=count):
        r_copy(0, count).start()
        r_list[count, 0] = 0
        r_list[count, 1] = 0
        r_list[count, 2] = 0

    r_count = count + odd

    partner = blk + 1 - 2 * lax.rem(blk, 2)
    other = 1 - helper
    sources = ((blk, helper), (blk, other), (partner, helper), (partner, other))
    count = jnp.int32(0)
    for source, (b, h) in enumerate(sources):
        row = b * nhelper + h
        blocks = meta_ref[row, id_rows, qblocks]
        for block in range(qblocks):
            live = blocks > block

            @pl.when(live)
            def _(source=source, block=block, count=count, row=row):
                q_copy(source, block, count).start()
                q_list[count, 0] = source * qblocks + block
                q_list[count, 1] = meta_ref[row, id_rows, block]

            count = count + live.astype(jnp.int32)
    q_count = count

    if with_prev:
        out_ref[...] = prev_ref[...]
    else:
        out_ref[...] = jnp.zeros_like(out_ref)

    def wait_r(slot, carry):
        r_copy(0, slot).wait()
        return carry

    lax.fori_loop(0, r_count, wait_r, 0)
    lane = lax.broadcasted_iota(jnp.int32, (1, LANES), 1)
    factor = LOG2E / math.sqrt(width)

    def one_query_block(q, carry):
        q_copy(0, 0, q).wait()
        slot, cluster = q_list[q, 0], q_list[q, 1]
        beta = beta_ref[cluster]
        scale = beta * factor
        offset = beta * beta * (0.5 * LOG2E)
        block = qv[pl.ds(pl.multiple_of(q * LANES, LANES), LANES), :]

        def bias(r):
            ids = ids_ref[r_list[r, 0] * nhelper, pl.ds(r_list[r, 1], 1), :]
            weight = jnp.where(ids == cluster, 0.0, -4.0)
            return jnp.where(lane < r_list[r, 2], weight, DEAD) - offset

        def two_tiles(pair, acc):
            start = pl.multiple_of(pair * (2 * LANES), 2 * LANES)
            score = lax.dot_general(
                block,
                rv[pl.ds(start, 2 * LANES), :],
                (((1,), (1,)), ((), ())),
                preferred_element_type=jnp.float32,
            )
            for side in range(2):
                part = score[:, side * LANES : (side + 1) * LANES]
                acc = acc + jnp.exp2(part * scale + bias(2 * pair + side))
            return acc

        acc = lax.fori_loop(
            0, r_count // 2, two_tiles, jnp.zeros((LANES, LANES), jnp.float32)
        )
        total = jnp.sum(acc.T, axis=0, keepdims=True)
        out_ref[pl.ds(slot, 1), :] = out_ref[pl.ds(slot, 1), :] + total
        return carry

    lax.fori_loop(0, q_count, one_query_block, 0)


def score_call(tile_plan, nblk, nhelper, qblocks, me, meta, beta, queries, tiles, prev):
    width = queries[0].shape[1]
    slots = len(queries) * qblocks
    ntiles = len(tiles)
    pad = ntiles + ntiles % 2
    smem = pl.BlockSpec(memory_space=pltpu.SMEM)
    vmem = pl.BlockSpec(memory_space=pltpu.VMEM)
    anywhere = pl.BlockSpec(memory_space=pl.ANY)
    extra = () if prev is None else (prev,)
    flops = 2 * slots * LANES * ntiles * LANES * width
    return pl.pallas_call(
        functools.partial(
            score_kernel, tile_plan, nblk, nhelper, qblocks, prev is not None
        ),
        out_shape=jax.ShapeDtypeStruct((slots, LANES), jnp.float32),
        in_specs=[smem, smem, smem, vmem]
        + [anywhere] * (len(queries) + ntiles)
        + [vmem] * len(extra),
        out_specs=vmem,
        scratch_shapes=[
            pltpu.VMEM((slots * LANES, width), jnp.bfloat16),
            pltpu.VMEM((pad * LANES, width), jnp.bfloat16),
            pltpu.SMEM((slots, 2), jnp.int32),
            pltpu.SMEM((pad, 3), jnp.int32),
            pltpu.SemaphoreType.DMA((slots,)),
            pltpu.SemaphoreType.DMA((pad,)),
        ],
        compiler_params=pltpu.CompilerParams(vmem_limit_bytes=24 * 1024 * 1024),
        cost_estimate=pl.CostEstimate(
            flops=flops,
            bytes_accessed=2 * (slots + ntiles) * LANES * width,
            transcendentals=slots * ntiles * LANES * LANES,
        ),
    )(me, meta, beta, meta, *queries, *tiles, *extra)


def per_device(
    queries,
    query_block_cluster,
    block_count,
    references,
    ref_cluster,
    ref_rows,
    cluster_beta,
    cluster_member_count,
):
    nblk, nhelper = lax.axis_size("blk"), lax.axis_size("helper")
    blk, helper = lax.axis_index("blk"), lax.axis_index("helper")
    qblocks = query_block_cluster.shape[0]
    rows, width = references.shape
    tiles = rows // LANES
    chunks = tiles // nhelper
    hops = nblk // 2 - 1
    me = jnp.stack([blk, helper]).astype(jnp.int32)

    by_tile = references.reshape(tiles, LANES, width)
    own = [
        lax.dynamic_index_in_dim(by_tile, helper + nhelper * c, 0, keepdims=False)
        for c in range(chunks)
    ]
    up, down = [own], [own]
    up.append([shift(x, "blk", 2) for x in own])
    down.append([shift(x, "blk", -2) for x in own])

    scalars = jnp.concatenate([query_block_cluster, block_count, ref_rows])
    scalars = jnp.pad(scalars, (0, LANES - scalars.shape[0]))
    meta = jnp.concatenate([ref_cluster, scalars]).reshape(1, tiles + 1, LANES)
    meta = lax.all_gather(meta, ("blk", "helper"), axis=0, tiled=True)

    q_helper = swap(queries, "helper")
    q_partner = swap(queries, "blk")
    for _ in range(1, hops):
        up.append([shift(x, "blk", 2) for x in up[-1]])
        down.append([shift(x, "blk", -2) for x in down[-1]])
    q_both = swap(q_partner, "helper")
    all_queries = (queries, q_helper, q_partner, q_both)

    def totals_of(steps, prev):
        plan, operands = [], []
        for step in steps:
            for distance, held in ((-2 * step, up), (2 * step, down)):
                if step == 0 and held is down:
                    continue
                for c in range(chunks):
                    plan.append((distance, c))
                    operands.append(held[step][c])
        return score_call(
            tuple(plan), nblk, nhelper, qblocks, me, meta, cluster_beta, all_queries, operands, prev
        )

    totals = totals_of(range(hops), None)
    totals = totals_of([hops], totals)
    totals = totals.reshape(4, qblocks, LANES)
    total = (
        totals[0]
        + swap(totals[1], "helper")
        + swap(totals[2], "blk")
        + lax.ppermute(
            totals[3],
            ("blk", "helper"),
            [(i, (i ^ nhelper) ^ 1) for i in range(nblk * nhelper)],
        )
    )
    columns = jnp.arange(cluster_member_count.shape[0], dtype=jnp.int32)
    onehot = query_block_cluster[:, None] == columns[None, :]
    sizes = jnp.sum(jnp.where(onehot, cluster_member_count[None, :], 0), axis=1)
    density = jnp.log1p(total / sizes.astype(jnp.float32)[:, None])
    return density.reshape(queries.shape[0])


def solution(mesh):
    in_specs = (
        P(("parts", "blk", "helper"), None),
        P(("parts", "blk", "helper")),
        P(("parts", "blk", "helper")),
        P(("parts", "blk"), None),
        P(("parts", "blk")),
        P(("parts", "blk")),
        P("parts"),
        P("parts"),
    )
    out_specs = P(("parts", "blk", "helper"))
    return jax.shard_map(
        per_device, mesh=mesh, in_specs=in_specs, out_specs=out_specs, check_vma=False
    )
```

```python
import functools
import math

import jax
import jax.numpy as jnp
from jax import lax
from jax.experimental import pallas as pl
from jax.experimental.pallas import tpu as pltpu
from jax.sharding import PartitionSpec as P

LANES = 128
LOG2E = 1.4426950408889634
DEAD = -1.0e30


def turn(value, by):
    length = lax.axis_size("blk")
    return lax.ppermute(value, "blk", [(i, (i + by) % length) for i in range(length)])


def swap(value, axis):
    length = lax.axis_size(axis)
    return lax.ppermute(value, axis, [(i, i ^ 1) for i in range(length)])


def swap_both(value):
    nblk, nhelper = lax.axis_size("blk"), lax.axis_size("helper")
    pairs = [(i, (i ^ nhelper) ^ 1) for i in range(nblk * nhelper)]
    return lax.ppermute(value, ("blk", "helper"), pairs)


def rows_of(index, count=1):
    return pl.ds(pl.multiple_of(index * LANES, LANES), count * LANES)


def score_kernel(plan, chunks, qblocks, first, info_ref, beta_ref, ids_ref, *refs):
    ntiles = len(plan)
    if first:
        q_refs, refs = refs[:4], refs[4:]
        r_refs, (out_ref, qv, rv, q_list, r_list) = refs[:ntiles], refs[ntiles:]
    else:
        (qv, prev_ref), refs = refs[:2], refs[2:]
        r_refs, (out_ref, rv, q_list, r_list) = refs[:ntiles], refs[ntiles:]
    width = qv.shape[1]
    slots = 4 * qblocks
    helper = info_ref[slots + 4]

    q_count = jnp.int32(0)
    for source in range(4):
        blocks = info_ref[slots + source]

        def one_block(block, carry, source=source, q_count=q_count):
            if first:
                qv[rows_of(q_count + block), :] = q_refs[source][rows_of(block), :]
            q_list[q_count + block] = source * qblocks + block
            return carry

        lax.fori_loop(0, blocks, one_block, 0)
        q_count = q_count + blocks

    r_count = jnp.int32(0)
    for operand, (source, chunk) in enumerate(plan):
        tile = helper + 2 * chunk
        live = info_ref[slots + 5 + source] > tile * LANES

        @pl.when(live)
        def _(operand=operand, source=source, chunk=chunk, r_count=r_count):
            rv[rows_of(r_count), :] = r_refs[operand][...]
            r_list[r_count] = source * chunks + chunk

        r_count = r_count + live.astype(jnp.int32)
    odd = lax.rem(r_count, 2)

    @pl.when(odd == 1)
    def _():
        rv[rows_of(r_count), :] = r_refs[0][...]
        r_list[r_count] = ids_ref.shape[0] - 1

    r_pairs = (r_count + odd) // 2
    factor = LOG2E / math.sqrt(width)
    if first:
        out_ref[...] = jnp.zeros_like(out_ref)
    else:
        out_ref[...] = prev_ref[...]

    def two_query_blocks(group, carry):
        parts = []
        for side in range(2):
            slot = q_list[jnp.minimum(2 * group + side, q_count - 1)]
            cluster = info_ref[slot]
            beta = beta_ref[cluster]
            parts.append((slot, cluster, beta * factor, beta * beta * (0.5 * LOG2E)))
        blocks = qv[rows_of(2 * group, 2), :]

        def two_tiles(pair, accs):
            score = lax.dot_general(
                blocks,
                rv[rows_of(2 * pair, 2), :],
                (((1,), (1,)), ((), ())),
                preferred_element_type=jnp.float32,
            )
            accs = list(accs)
            for t in range(2):
                ids = ids_ref[pl.ds(r_list[2 * pair + t], 1), :]
                for side, (_, cluster, scale, offset) in enumerate(parts):
                    weight = jnp.where(ids == cluster, 0.0, -4.0)
                    bias = jnp.where(ids < 0, DEAD, weight) - offset
                    part = score[
                        side * LANES : (side + 1) * LANES, t * LANES : (t + 1) * LANES
                    ]
                    accs[side] = accs[side] + jnp.exp2(part * scale + bias)
            return tuple(accs)

        zero = jnp.zeros((LANES, LANES), jnp.float32)
        accs = lax.fori_loop(0, r_pairs, two_tiles, (zero, zero))
        for side in range(2):
            total = jnp.sum(accs[side].T, axis=0, keepdims=True)

            @pl.when(2 * group + side < q_count)
            def _(side=side, total=total):
                row = pl.ds(parts[side][0], 1)
                out_ref[row, :] = out_ref[row, :] + total

        return carry

    @pl.when(r_pairs > 0)
    def _():
        lax.fori_loop(0, (q_count + 1) // 2, two_query_blocks, 0)


def score_call(plan, chunks, qblocks, info, beta, ids, queries, packed, prev, tiles):
    first = packed is None
    width = tiles[0].shape[1]
    slots = 4 * qblocks
    ntiles = len(tiles)
    pad = ntiles + ntiles % 2
    smem = pl.BlockSpec(memory_space=pltpu.SMEM)
    vmem = pl.BlockSpec(memory_space=pltpu.VMEM)
    totals_shape = jax.ShapeDtypeStruct((slots, LANES), jnp.float32)
    packed_shape = jax.ShapeDtypeStruct((slots * LANES, width), jnp.bfloat16)
    given = queries if first else (packed, prev)
    return pl.pallas_call(
        functools.partial(score_kernel, plan, chunks, qblocks, first),
        out_shape=(totals_shape, packed_shape) if first else totals_shape,
        in_specs=[smem, smem] + [vmem] * (1 + len(given) + ntiles),
        out_specs=(vmem, vmem) if first else vmem,
        scratch_shapes=[
            pltpu.VMEM((pad * LANES, width), jnp.bfloat16),
            pltpu.SMEM((slots,), jnp.int32),
            pltpu.SMEM((pad,), jnp.int32),
        ],
        compiler_params=pltpu.CompilerParams(vmem_limit_bytes=24 * 1024 * 1024),
        cost_estimate=pl.CostEstimate(flops=1, bytes_accessed=1, transcendentals=0),
    )(info, beta, ids, *given, *tiles)


def per_device(
    queries,
    query_block_cluster,
    block_count,
    references,
    ref_cluster,
    ref_rows,
    cluster_beta,
    cluster_member_count,
):
    nblk, nhelper = lax.axis_size("blk"), lax.axis_size("helper")
    helper = lax.axis_index("helper").astype(jnp.int32)
    qblocks = query_block_cluster.shape[0]
    rows, width = references.shape
    tiles = rows // LANES
    chunks = tiles // nhelper
    sources = nblk // 2

    by_tile = references.reshape(tiles, LANES, width)
    own = [
        lax.dynamic_index_in_dim(by_tile, helper + nhelper * c, 0, keepdims=False)
        for c in range(chunks)
    ]
    own, queries, ref_cluster, query_block_cluster, block_count, ref_rows = (
        lax.optimization_barrier(
            (own, queries, ref_cluster, query_block_cluster, block_count, ref_rows)
        )
    )
    held = [own, [turn(x, 2) for x in own]]
    q_partner = swap(queries, "blk")
    q_helper = swap(queries, "helper")

    live = jnp.arange(rows, dtype=jnp.int32) < ref_rows[0]
    ids = jnp.where(live, ref_cluster, -1).reshape(chunks, nhelper, LANES)
    ids = lax.dynamic_index_in_dim(ids, helper, 1, keepdims=False)
    scalars = jnp.concatenate([query_block_cluster, block_count, ref_rows])
    scalars = jnp.pad(scalars, (0, LANES - scalars.shape[0]))
    meta = jnp.concatenate([ids, scalars[None, :]])
    along = [meta] + [turn(meta, 2 * s) for s in range(1, sources)]
    around = [meta, swap(meta, "helper"), swap(meta, "blk"), swap_both(meta)]
    none = jnp.full((1, LANES), -1, jnp.int32)
    all_ids = jnp.concatenate([m[:chunks] for m in along] + [none])
    info = jnp.concatenate(
        [m[chunks, :qblocks] for m in around]
        + [m[chunks, qblocks : qblocks + 1] for m in around]
        + [helper[None]]
        + [m[chunks, qblocks + 1 : qblocks + 2] for m in along]
    )

    for _ in range(2, sources):
        held.append([turn(x, 2) for x in held[-1]])
    q_partner, held[-2] = lax.optimization_barrier((q_partner, held[-2]))
    q_both = swap(q_partner, "helper")
    all_queries = (queries, q_helper, q_partner, q_both)

    def operands(steps):
        plan = tuple((s, c) for s in steps for c in range(chunks))
        return plan, [held[s][c] for s, c in plan]

    plan, operand = operands(range(sources - 1))
    totals, packed = score_call(
        plan, chunks, qblocks, info, cluster_beta, all_ids, all_queries, None, None, operand
    )
    plan, operand = operands([sources - 1])
    totals = score_call(
        plan, chunks, qblocks, info, cluster_beta, all_ids, None, packed, totals, operand
    )
    totals = totals.reshape(4, qblocks, LANES)
    total = totals[0] + swap(totals[1], "helper") + swap(totals[2], "blk") + swap_both(totals[3])
    columns = jnp.arange(cluster_member_count.shape[0], dtype=jnp.int32)
    onehot = query_block_cluster[:, None] == columns[None, :]
    sizes = jnp.sum(jnp.where(onehot, cluster_member_count[None, :], 0), axis=1)
    density = jnp.log1p(total / sizes.astype(jnp.float32)[:, None])
    return density.reshape(queries.shape[0])


def solution(mesh):
    in_specs = (
        P(("parts", "blk", "helper"), None),
        P(("parts", "blk", "helper")),
        P(("parts", "blk", "helper")),
        P(("parts", "blk"), None),
        P(("parts", "blk")),
        P(("parts", "blk")),
        P("parts"),
        P("parts"),
    )
    out_specs = P(("parts", "blk", "helper"))
    return jax.shard_map(
        per_device, mesh=mesh, in_specs=in_specs, out_specs=out_specs, check_vma=False
    )
```

```python
import functools
import math

import jax
import jax.numpy as jnp
from jax import lax
from jax.experimental import pallas as pl
from jax.experimental.pallas import tpu as pltpu
from jax.sharding import PartitionSpec as P

LANES = 128
LOG2E = 1.4426950408889634
DEAD = -1.0e30
SMEM = pl.BlockSpec(memory_space=pltpu.SMEM)
VMEM = pl.BlockSpec(memory_space=pltpu.VMEM)
PARAMS = pltpu.CompilerParams(vmem_limit_bytes=24 * 1024 * 1024)
COST = pl.CostEstimate(flops=1, bytes_accessed=1, transcendentals=0)


def turn(value, by):
    length = lax.axis_size("blk")
    return lax.ppermute(value, "blk", [(i, (i + by) % length) for i in range(length)])


def swap(value, axis):
    length = lax.axis_size(axis)
    return lax.ppermute(value, axis, [(i, i ^ 1) for i in range(length)])


def swap_both(value):
    nblk, nhelper = lax.axis_size("blk"), lax.axis_size("helper")
    pairs = [(i, (i ^ nhelper) ^ 1) for i in range(nblk * nhelper)]
    return lax.ppermute(value, ("blk", "helper"), pairs)


def rows_of(index, count=1):
    return pl.ds(pl.multiple_of(index * LANES, LANES), count * LANES)


def table_kernel(
    nhelper, chunks, helper_ref, clusters_ref, count_ref, rows_ref, ids_ref, out_ref
):
    lane = lax.broadcasted_iota(jnp.int32, (1, LANES), 1)
    live_rows = rows_ref[0]
    out_ref[...] = jnp.zeros_like(out_ref)
    for c in range(chunks):
        tile = helper_ref[0] + nhelper * c
        ids = ids_ref[pl.ds(tile, 1), :]
        out_ref[c : c + 1, :] = jnp.where(tile * LANES + lane < live_rows, ids, -1)
    qblocks = clusters_ref.shape[0]
    row = jnp.where(lane == qblocks, count_ref[0], 0)
    for k in range(qblocks):
        row = jnp.where(lane == k, clusters_ref[k], row)
    out_ref[chunks : chunks + 1, :] = row


def spread_kernel(chunks, nalong, *refs):
    tables, (info_ref, ids_ref, weight_ref) = refs[:-3], refs[-3:]
    info_ref[...] = jnp.zeros_like(info_ref)
    for k, table in enumerate((tables[0],) + tables[nalong:]):
        info_ref[k : k + 1, :] = table[chunks : chunks + 1, :]
    for s in range(nalong):
        for c in range(chunks):
            ids = jnp.broadcast_to(tables[s][c : c + 1, :], (LANES, LANES)).T
            rows = pl.ds((s * chunks + c) * LANES, LANES)
            ids_ref[rows, :] = ids
            weight_ref[rows, :] = jnp.where(ids < 0, DEAD, -4.0)


def score_kernel(
    chunks, base, qblocks, first, info_ref, beta_ref, ids_ref, weight_ref, *refs
):
    if first:
        q_refs, r_refs, (out_ref, qv, q_list) = refs[:4], refs[4:-3], refs[-3:]
    else:
        (qv, prev_ref), r_refs, (out_ref, q_list) = refs[:2], refs[2:-2], refs[-2:]
    width = qv.shape[1]

    q_count = jnp.int32(0)
    for source in range(4):
        blocks = info_ref[source, qblocks]

        def one_block(block, carry, source=source, q_count=q_count):
            if first:
                qv[rows_of(q_count + block), :] = q_refs[source][rows_of(block), :]
            q_list[q_count + block, 0] = source * qblocks + block
            q_list[q_count + block, 1] = info_ref[source, block]
            return carry

        lax.fori_loop(0, blocks, one_block, 0)
        q_count = q_count + blocks

    factor = LOG2E / math.sqrt(width)
    out_ref[...] = jnp.zeros_like(out_ref) if first else prev_ref[...]

    def two_query_blocks(group, carry):
        parts = []
        for side in range(2):
            entry = jnp.minimum(2 * group + side, q_count - 1)
            slot, cluster = q_list[entry, 0], q_list[entry, 1]
            beta = beta_ref[cluster]
            parts.append((slot, cluster, beta * factor, beta * beta * (0.5 * LOG2E)))
        blocks = qv[rows_of(2 * group, 2), :]
        accs = [jnp.zeros((8, LANES), jnp.float32) for _ in range(2)]
        for s in range(len(r_refs) // chunks):
            held = r_refs[s * chunks : (s + 1) * chunks]
            tile = jnp.concatenate([r[...] for r in held], axis=0)
            score = lax.dot_general(
                tile,
                blocks,
                (((1,), (1,)), ((), ())),
                preferred_element_type=jnp.float32,
            )
            height = tile.shape[0]
            rows = pl.ds((base + s) * height, height)
            ids, other = ids_ref[rows, :], weight_ref[rows, :]
            for side, (_, cluster, scale, offset) in enumerate(parts):
                part = score[:, side * LANES : (side + 1) * LANES]
                weight = jnp.where(ids == cluster, 0.0, other)
                value = jnp.exp2((part * scale - offset) + weight)
                accs[side] = accs[side] + jnp.sum(value.reshape(height // 8, 8, LANES), axis=0)
        for side in range(2):
            total = jnp.sum(accs[side], axis=0, keepdims=True)

            @pl.when(2 * group + side < q_count)
            def _(side=side, total=total):
                row = pl.ds(parts[side][0], 1)
                out_ref[row, :] = out_ref[row, :] + total

        return carry

    lax.fori_loop(0, (q_count + 1) // 2, two_query_blocks, 0)


def score_call(chunks, base, qblocks, info, beta, spread, queries, packed, prev, tiles):
    first = packed is None
    width = tiles[0].shape[1]
    slots = 4 * qblocks
    totals_shape = jax.ShapeDtypeStruct((slots, LANES), jnp.float32)
    packed_shape = jax.ShapeDtypeStruct((slots * LANES, width), jnp.bfloat16)
    given = queries if first else (packed, prev)
    return pl.pallas_call(
        functools.partial(score_kernel, chunks, base, qblocks, first),
        out_shape=(totals_shape, packed_shape) if first else totals_shape,
        in_specs=[SMEM, SMEM] + [VMEM] * (2 + len(given) + len(tiles)),
        out_specs=(VMEM, VMEM) if first else VMEM,
        scratch_shapes=[pltpu.SMEM((slots, 2), jnp.int32)],
        compiler_params=PARAMS,
        cost_estimate=COST,
    )(info, beta, *spread, *given, *tiles)


def per_device(
    queries,
    query_block_cluster,
    block_count,
    references,
    ref_cluster,
    ref_rows,
    cluster_beta,
    cluster_member_count,
):
    nblk, nhelper = lax.axis_size("blk"), lax.axis_size("helper")
    helper = lax.axis_index("helper").astype(jnp.int32)
    qblocks = query_block_cluster.shape[0]
    rows, width = references.shape
    tiles = rows // LANES
    chunks = tiles // nhelper
    sources = nblk // 2

    by_tile = references.reshape(tiles, LANES, width)
    own = [
        lax.dynamic_index_in_dim(by_tile, helper + nhelper * c, 0, keepdims=False)
        for c in range(chunks)
    ]
    own, queries, ref_cluster = lax.optimization_barrier((own, queries, ref_cluster))
    held = [own, [turn(x, 2) for x in own]]
    q_partner = swap(queries, "blk")
    q_helper = swap(queries, "helper")

    table = pl.pallas_call(
        functools.partial(table_kernel, nhelper, chunks),
        out_shape=jax.ShapeDtypeStruct((8 * ((chunks + 8) // 8), LANES), jnp.int32),
        in_specs=[SMEM] * 4 + [VMEM],
        out_specs=VMEM,
        compiler_params=PARAMS,
        cost_estimate=COST,
    )(
        helper[None],
        query_block_cluster,
        block_count,
        ref_rows,
        ref_cluster.reshape(tiles, LANES),
    )
    along = [table] + [turn(table, 2 * s) for s in range(1, sources)]
    around = [swap(table, "helper"), swap(table, "blk"), swap_both(table)]
    spread_shape = (sources * rows // nhelper, LANES)
    info, *spread = pl.pallas_call(
        functools.partial(spread_kernel, chunks, sources),
        out_shape=(
            jax.ShapeDtypeStruct((8, LANES), jnp.int32),
            jax.ShapeDtypeStruct(spread_shape, jnp.int32),
            jax.ShapeDtypeStruct(spread_shape, jnp.float32),
        ),
        in_specs=[VMEM] * (sources + 3),
        out_specs=(VMEM, VMEM, VMEM),
        compiler_params=PARAMS,
        cost_estimate=COST,
    )(*along, *around)

    for step in range(2, sources):
        ready = table if step == 2 else info
        if step == 2 or step == sources - 1:
            held[-1][0], ready = lax.optimization_barrier((held[-1][0], ready))
        if step == sources - 1:
            info = ready
        held.append([turn(x, 2) for x in held[-1]])
    q_partner, held[-2][-1] = lax.optimization_barrier((q_partner, held[-2][-1]))
    q_both = swap(q_partner, "helper")
    all_queries = (queries, q_helper, q_partner, q_both)

    early = [x for step in held[:-1] for x in step]
    totals, packed = score_call(
        chunks, 0, qblocks, info, cluster_beta, spread, all_queries, None, None, early
    )
    totals = score_call(
        chunks, sources - 1, qblocks, info, cluster_beta, spread, None, packed, totals, held[-1]
    )
    totals = totals.reshape(4, qblocks, LANES)
    total = totals[0] + swap(totals[1], "helper") + swap(totals[2], "blk") + swap_both(totals[3])
    columns = jnp.arange(cluster_member_count.shape[0], dtype=jnp.int32)
    onehot = query_block_cluster[:, None] == columns[None, :]
    sizes = jnp.sum(jnp.where(onehot, cluster_member_count[None, :], 0), axis=1)
    density = jnp.log1p(total / sizes.astype(jnp.float32)[:, None])
    return density.reshape(queries.shape[0])


def solution(mesh):
    in_specs = (
        P(("parts", "blk", "helper"), None),
        P(("parts", "blk", "helper")),
        P(("parts", "blk", "helper")),
        P(("parts", "blk"), None),
        P(("parts", "blk")),
        P(("parts", "blk")),
        P("parts"),
        P("parts"),
    )
    out_specs = P(("parts", "blk", "helper"))
    return jax.shard_map(
        per_device, mesh=mesh, in_specs=in_specs, out_specs=out_specs, check_vma=False
    )
```

```python
import functools
import math

import jax
import jax.numpy as jnp
from jax import lax
from jax.experimental import pallas as pl
from jax.experimental.pallas import tpu as pltpu
from jax.sharding import PartitionSpec as P

LANES = 128
TABLE = 16
LOG2E = 1.4426950408889634
DEAD = -1.0e30
SMEM = pl.BlockSpec(memory_space=pltpu.SMEM)
VMEM = pl.BlockSpec(memory_space=pltpu.VMEM)
HBM = pl.BlockSpec(memory_space=pltpu.HBM)
WHOLE = pltpu.CompilerParams(vmem_limit_bytes=60 * 1024 * 1024)
PARAMS = pltpu.CompilerParams(vmem_limit_bytes=24 * 1024 * 1024)
COST = pl.CostEstimate(flops=1, bytes_accessed=1, transcendentals=0)


def turn(value, by):
    length = lax.axis_size("blk")
    return lax.ppermute(value, "blk", [(i, (i + by) % length) for i in range(length)])


def swap(value, axis):
    length = lax.axis_size(axis)
    return lax.ppermute(value, axis, [(i, i ^ 1) for i in range(length)])


def swap_both(value):
    nblk, nhelper = lax.axis_size("blk"), lax.axis_size("helper")
    pairs = [(i, (i ^ nhelper) ^ 1) for i in range(nblk * nhelper)]
    return lax.ppermute(value, ("blk", "helper"), pairs)


def after(value, *others):
    return lax.optimization_barrier((value, *others))[0]


def rows_of(index, count=1):
    return pl.ds(pl.multiple_of(index * LANES, LANES), count * LANES)


def pack_refs_kernel(nhelper, helper_ref, r_ref, ids_ref, live_ref, *refs):
    outs, (ids, live, sem) = refs[:-3], refs[-3:]
    n = len(outs)
    copies = [
        pltpu.make_async_copy(ids_ref, ids, sem.at[n]),
        pltpu.make_async_copy(live_ref, live, sem.at[n + 1]),
    ]
    for c, out in enumerate(outs):
        rows = rows_of(helper_ref[0] + nhelper * c)
        copies.append(pltpu.make_async_copy(r_ref.at[rows], out.at[pl.ds(0, LANES)], sem.at[c]))
    for copy in copies:
        copy.start()
    copies[0].wait()
    copies[1].wait()
    lane = lax.broadcasted_iota(jnp.int32, (TABLE, LANES), 1)
    row = lax.broadcasted_iota(jnp.int32, (TABLE, LANES), 0)
    table = jnp.full((TABLE, LANES), -1, jnp.int32)
    for c in range(n):
        tile = helper_ref[0] + nhelper * c
        here = jnp.where(tile * LANES + lane < live[0], ids[pl.ds(tile, 1), :], -1)
        table = jnp.where(row == c, here, table)
    outs[0][pl.ds(LANES, TABLE), pl.ds(0, LANES)] = table.astype(jnp.float32).astype(jnp.bfloat16)
    for copy in copies[2:]:
        copy.wait()


def pack_queries_kernel(q_ref, clusters_ref, count_ref, out, clusters, count, sem):
    copies = (
        pltpu.make_async_copy(clusters_ref, clusters, sem.at[0]),
        pltpu.make_async_copy(count_ref, count, sem.at[1]),
        pltpu.make_async_copy(q_ref, out.at[pl.ds(0, q_ref.shape[0])], sem.at[2]),
    )
    for copy in copies:
        copy.start()
    copies[0].wait()
    copies[1].wait()
    lane = lax.broadcasted_iota(jnp.int32, (TABLE, LANES), 1)
    qblocks = clusters_ref.shape[0]
    table = jnp.where(lane == qblocks, count[0], 0)
    for k in range(qblocks):
        table = jnp.where(lane == k, clusters[k], table)
    out[pl.ds(q_ref.shape[0], TABLE), pl.ds(0, LANES)] = table.astype(jnp.float32).astype(
        jnp.bfloat16
    )
    copies[2].wait()


def score_kernel(chunks, qblocks, first, wide, beta_ref, *refs):
    if first:
        q_refs, refs = refs[:4], refs[4:]
        r_refs, (out_ref, qv, info_out, q_list, info, ids_ref, other_ref, sem) = refs[:-8], refs[-8:]
    else:
        (info, qv, prev_ref), refs = refs[:3], refs[3:]
        r_refs, (out_ref, q_list, ids_ref, other_ref) = refs[:-4], refs[-4:]
    width = qv.shape[1]
    sources = len(r_refs) // chunks
    if first:
        for s, q_ref in enumerate(q_refs):
            table = q_ref[pl.ds(qblocks * LANES, TABLE), pl.ds(0, LANES)].astype(jnp.float32)
            info_out[s : s + 1, :] = table[0:1, :].astype(jnp.int32)
        copy = pltpu.make_async_copy(info_out, info, sem)
        copy.start()

    for s in range(sources):
        table = r_refs[s * chunks][pl.ds(LANES, TABLE), pl.ds(0, LANES)].astype(jnp.float32)
        for c in range(chunks):
            ids = jnp.broadcast_to(table[c : c + 1, :], (LANES, LANES)).T
            rows = pl.ds((s * chunks + c) * LANES, LANES)
            ids_ref[rows, :] = ids
            other_ref[rows, :] = jnp.where(ids < 0.0, DEAD, -4.0)
    if first:
        copy.wait()

    q_count = jnp.int32(0)
    for source in range(4):
        blocks = info[source, qblocks]

        def one_block(block, carry, source=source, q_count=q_count):
            if first:
                qv[rows_of(q_count + block), :] = q_refs[source][rows_of(block), :]
            q_list[q_count + block, 0] = source * qblocks + block
            q_list[q_count + block, 1] = info[source, block]
            return carry

        lax.fori_loop(0, blocks, one_block, 0)
        q_count = q_count + blocks

    factor = LOG2E / math.sqrt(width)
    out_ref[...] = jnp.zeros_like(out_ref) if first else prev_ref[...]

    def query_blocks(group, carry):
        parts = []
        for side in range(wide):
            entry = jnp.minimum(wide * group + side, q_count - 1)
            slot, cluster = q_list[entry, 0], q_list[entry, 1]
            beta = beta_ref[cluster]
            parts.append(
                (slot, cluster.astype(jnp.float32), beta * factor, beta * beta * (0.5 * LOG2E))
            )
        accs = [jnp.zeros((8, LANES), jnp.float32) for _ in range(wide)]
        for s in range(sources):
            held = r_refs[s * chunks : (s + 1) * chunks]
            tile = jnp.concatenate([r[pl.ds(0, LANES), :] for r in held], axis=0)
            height = tile.shape[0]
            rows = pl.ds(s * height, height)
            for pair in range(wide // 2):
                score = lax.dot_general(
                    tile,
                    qv[rows_of(wide * group + 2 * pair, 2), :],
                    (((1,), (1,)), ((), ())),
                    preferred_element_type=jnp.float32,
                )
                for half in range(2):
                    side = 2 * pair + half
                    _, cluster, scale, offset = parts[side]
                    part = score[:, half * LANES : (half + 1) * LANES]
                    weight = jnp.where(ids_ref[rows, :] == cluster, 0.0, other_ref[rows, :])
                    value = jnp.exp2((part * scale - offset) + weight)
                    accs[side] += jnp.sum(value.reshape(height // 8, 8, LANES), axis=0)
        for side in range(wide):
            total = jnp.sum(accs[side], axis=0, keepdims=True)

            @pl.when(wide * group + side < q_count)
            def _(side=side, total=total):
                row = pl.ds(parts[side][0], 1)
                out_ref[row, :] = out_ref[row, :] + total

        return carry

    lax.fori_loop(0, (q_count + wide - 1) // wide, query_blocks, 0)


def score_call(chunks, qblocks, wide, beta, given, tiles, first):
    width = tiles[0].shape[1]
    slots = 4 * qblocks
    totals_shape = jax.ShapeDtypeStruct((slots, LANES), jnp.float32)
    packed_shape = jax.ShapeDtypeStruct((slots * LANES, width), jnp.bfloat16)
    info_shape = jax.ShapeDtypeStruct((8, LANES), jnp.int32)
    q_list = pltpu.SMEM((slots, 2), jnp.int32)
    spread = pltpu.VMEM((len(tiles) * LANES, LANES), jnp.float32)
    info = pltpu.SMEM((8, LANES), jnp.int32)
    return pl.pallas_call(
        functools.partial(score_kernel, chunks, qblocks, first, wide),
        out_shape=(totals_shape, packed_shape, info_shape) if first else totals_shape,
        in_specs=[SMEM, VMEM if first else SMEM] + [VMEM] * (len(given) - 1 + len(tiles)),
        out_specs=(VMEM, VMEM, VMEM) if first else VMEM,
        scratch_shapes=[q_list, info, spread, spread, pltpu.SemaphoreType.DMA]
        if first
        else [q_list, spread, spread],
        compiler_params=PARAMS,
        cost_estimate=COST,
    )(beta, *given, *tiles)


def per_device(
    queries,
    query_block_cluster,
    block_count,
    references,
    ref_cluster,
    ref_rows,
    cluster_beta,
    cluster_member_count,
):
    nblk, nhelper = lax.axis_size("blk"), lax.axis_size("helper")
    helper = lax.axis_index("helper").astype(jnp.int32)
    qblocks = query_block_cluster.shape[0]
    q_rows, (rows, width) = queries.shape[0], references.shape
    tiles = rows // LANES
    chunks = tiles // nhelper
    sources = nblk // 2

    own = pl.pallas_call(
        functools.partial(pack_refs_kernel, nhelper),
        out_shape=[
            jax.ShapeDtypeStruct((LANES + (TABLE if c == 0 else 0), width), jnp.bfloat16)
            for c in range(chunks)
        ],
        in_specs=[SMEM] + [HBM] * 3,
        out_specs=[VMEM] * chunks,
        scratch_shapes=[
            pltpu.VMEM((tiles, LANES), jnp.int32),
            pltpu.SMEM((1,), jnp.int32),
            pltpu.SemaphoreType.DMA((chunks + 2,)),
        ],
        compiler_params=WHOLE,
        cost_estimate=COST,
    )(helper[None], references, ref_cluster.reshape(tiles, LANES), ref_rows)
    q_own = pl.pallas_call(
        pack_queries_kernel,
        out_shape=jax.ShapeDtypeStruct((q_rows + TABLE, width), jnp.bfloat16),
        in_specs=[HBM] * 3,
        out_specs=VMEM,
        scratch_shapes=[
            pltpu.SMEM((qblocks,), jnp.int32),
            pltpu.SMEM((1,), jnp.int32),
            pltpu.SemaphoreType.DMA((3,)),
        ],
        compiler_params=WHOLE,
        cost_estimate=COST,
    )(after(queries, *own), query_block_cluster, block_count)
    q_partner = swap(q_own, "blk")
    q_helper = swap(q_own, "helper")
    held = [own]
    for step in range(1, sources):
        sent = []
        for c in range(chunks):
            if c > 0 and step > 1:
                waits = [held[step - 1][c - 1]]
            elif c == 0 and step > 2:
                waits = [held[step - 2][-1]]
            else:
                waits = []
            sent.append(turn(after(held[step - 1][c], *waits), 2))
        held.append(sent)
    q_both = swap(after(q_partner, *held[-2]), "helper")

    early = [x for step in held[:-1] for x in step]
    totals, packed, info = score_call(
        chunks, qblocks, 2, cluster_beta, (q_own, q_helper, q_partner, q_both), early, True
    )
    totals = score_call(
        chunks, qblocks, 4, cluster_beta, (info, packed, totals), held[-1], False
    )
    totals = totals.reshape(4, qblocks, LANES)
    total = totals[0] + swap(totals[1], "helper") + swap(totals[2], "blk") + swap_both(totals[3])
    columns = jnp.arange(cluster_member_count.shape[0], dtype=jnp.int32)
    onehot = query_block_cluster[:, None] == columns[None, :]
    sizes = jnp.sum(jnp.where(onehot, cluster_member_count[None, :], 0), axis=1)
    density = jnp.log1p(total / sizes.astype(jnp.float32)[:, None])
    return density.reshape(queries.shape[0])


def solution(mesh):
    in_specs = (
        P(("parts", "blk", "helper"), None),
        P(("parts", "blk", "helper")),
        P(("parts", "blk", "helper")),
        P(("parts", "blk"), None),
        P(("parts", "blk")),
        P(("parts", "blk")),
        P("parts"),
        P("parts"),
    )
    out_specs = P(("parts", "blk", "helper"))
    return jax.shard_map(
        per_device, mesh=mesh, in_specs=in_specs, out_specs=out_specs, check_vma=False
    )
```

```python
import functools
import math

import jax
import jax.numpy as jnp
from jax import lax
from jax.experimental import pallas as pl
from jax.experimental.pallas import tpu as pltpu
from jax.sharding import PartitionSpec as P

LANES = 128
TABLE = 16
LOG2E = 1.4426950408889634
DEAD = -1.0e30
SMEM = pl.BlockSpec(memory_space=pltpu.SMEM)
VMEM = pl.BlockSpec(memory_space=pltpu.VMEM)
HBM = pl.BlockSpec(memory_space=pltpu.HBM)
WHOLE = pltpu.CompilerParams(vmem_limit_bytes=60 * 1024 * 1024)
PARAMS = pltpu.CompilerParams(vmem_limit_bytes=24 * 1024 * 1024)


def turn(value, by):
    length = lax.axis_size("blk")
    return lax.ppermute(value, "blk", [(i, (i + by) % length) for i in range(length)])


def swap(value, axis):
    length = lax.axis_size(axis)
    return lax.ppermute(value, axis, [(i, i ^ 1) for i in range(length)])


def swap_both(value):
    nblk, nhelper = lax.axis_size("blk"), lax.axis_size("helper")
    pairs = [(i, (i ^ nhelper) ^ 1) for i in range(nblk * nhelper)]
    return lax.ppermute(value, ("blk", "helper"), pairs)


def after(value, *others):
    return lax.optimization_barrier((value, *others))[0]


def cost(flops, moved):
    return pl.CostEstimate(flops=flops, bytes_accessed=moved, transcendentals=0)


def rows_of(index, count=1):
    return pl.ds(pl.multiple_of(index * LANES, LANES), count * LANES)


def pack_refs_kernel(nhelper, helper_ref, r_ref, ids_ref, live_ref, *refs):
    outs, (ids, live, sem) = refs[:-3], refs[-3:]
    n = len(outs)
    copies = [
        pltpu.make_async_copy(ids_ref, ids, sem.at[n]),
        pltpu.make_async_copy(live_ref, live, sem.at[n + 1]),
    ]
    for c, out in enumerate(outs):
        rows = rows_of(helper_ref[0] + nhelper * c)
        copies.append(pltpu.make_async_copy(r_ref.at[rows], out.at[pl.ds(0, LANES)], sem.at[c]))
    for copy in copies:
        copy.start()
    copies[0].wait()
    copies[1].wait()
    lane = lax.broadcasted_iota(jnp.int32, (TABLE, LANES), 1)
    row = lax.broadcasted_iota(jnp.int32, (TABLE, LANES), 0)
    table = jnp.full((TABLE, LANES), -1, jnp.int32)
    for c in range(n):
        tile = helper_ref[0] + nhelper * c
        here = jnp.where(tile * LANES + lane < live[0, 0], ids[pl.ds(tile, 1), :], -1)
        table = jnp.where(row == c, here, table)
    outs[0][pl.ds(LANES, TABLE), pl.ds(0, LANES)] = table.astype(jnp.float32).astype(jnp.bfloat16)
    for copy in copies[2:]:
        copy.wait()


def pack_queries_kernel(q_ref, clusters_ref, count_ref, out, clusters, count, sem):
    copies = (
        pltpu.make_async_copy(clusters_ref, clusters, sem.at[0]),
        pltpu.make_async_copy(count_ref, count, sem.at[1]),
        pltpu.make_async_copy(q_ref, out.at[pl.ds(0, q_ref.shape[0])], sem.at[2]),
    )
    for copy in copies:
        copy.start()
    copies[0].wait()
    copies[1].wait()
    lane = lax.broadcasted_iota(jnp.int32, (TABLE, LANES), 1)
    qblocks = clusters_ref.shape[0]
    table = jnp.where(lane == qblocks, count[0, 0], 0)
    for k in range(qblocks):
        table = jnp.where(lane == k, clusters[k], table)
    out[pl.ds(q_ref.shape[0], TABLE), pl.ds(0, LANES)] = table.astype(jnp.float32).astype(
        jnp.bfloat16
    )
    copies[2].wait()


def score_kernel(chunks, qblocks, first, wide, beta_ref, *refs):
    if first:
        q_refs, refs = refs[:4], refs[4:]
        r_refs, (out_ref, qv, info_out, q_list, info, ids_ref, other_ref, sem) = refs[:-8], refs[-8:]
    else:
        (info, qv, prev_ref), refs = refs[:3], refs[3:]
        r_refs, (out_ref, q_list, ids_ref, other_ref) = refs[:-4], refs[-4:]
    width = qv.shape[1]
    sources = len(r_refs) // chunks
    if first:
        for s, q_ref in enumerate(q_refs):
            table = q_ref[pl.ds(qblocks * LANES, TABLE), pl.ds(0, LANES)].astype(jnp.float32)
            info_out[s : s + 1, :] = table[0:1, :].astype(jnp.int32)
        copy = pltpu.make_async_copy(info_out, info, sem)
        copy.start()

    for s in range(sources):
        table = r_refs[s * chunks][pl.ds(LANES, TABLE), pl.ds(0, LANES)].astype(jnp.float32)
        for c in range(chunks):
            ids = jnp.broadcast_to(table[c : c + 1, :], (LANES, LANES)).T
            rows = pl.ds((s * chunks + c) * LANES, LANES)
            ids_ref[rows, :] = ids
            other_ref[rows, :] = jnp.where(ids < 0.0, DEAD, -4.0)
    if first:
        copy.wait()

    q_count = jnp.int32(0)
    for source in range(4):
        blocks = info[source, qblocks]

        def one_block(block, carry, source=source, q_count=q_count):
            if first:
                qv[rows_of(q_count + block), :] = q_refs[source][rows_of(block), :]
            q_list[q_count + block, 0] = source * qblocks + block
            q_list[q_count + block, 1] = info[source, block]
            return carry

        lax.fori_loop(0, blocks, one_block, 0)
        q_count = q_count + blocks

    factor = LOG2E / math.sqrt(width)
    out_ref[...] = jnp.zeros_like(out_ref) if first else prev_ref[...]

    def query_blocks(group, carry):
        parts = []
        for side in range(wide):
            entry = jnp.minimum(wide * group + side, q_count - 1)
            slot, cluster = q_list[entry, 0], q_list[entry, 1]
            beta = beta_ref[cluster]
            parts.append(
                (slot, cluster.astype(jnp.float32), beta * factor, beta * beta * (0.5 * LOG2E))
            )
        accs = [jnp.zeros((8, LANES), jnp.float32) for _ in range(wide)]
        for s in range(sources):
            held = r_refs[s * chunks : (s + 1) * chunks]
            tile = jnp.concatenate([r[pl.ds(0, LANES), :] for r in held], axis=0)
            height = tile.shape[0]
            rows = pl.ds(s * height, height)
            for pair in range(wide // 2):
                score = lax.dot_general(
                    tile,
                    qv[rows_of(wide * group + 2 * pair, 2), :],
                    (((1,), (1,)), ((), ())),
                    preferred_element_type=jnp.float32,
                )
                for half in range(2):
                    side = 2 * pair + half
                    _, cluster, scale, offset = parts[side]
                    part = score[:, half * LANES : (half + 1) * LANES]
                    weight = jnp.where(ids_ref[rows, :] == cluster, 0.0, other_ref[rows, :])
                    value = jnp.exp2((part * scale - offset) + weight)
                    accs[side] += jnp.sum(value.reshape(height // 8, 8, LANES), axis=0)
        for side in range(wide):
            total = jnp.sum(accs[side], axis=0, keepdims=True)

            @pl.when(wide * group + side < q_count)
            def _(side=side, total=total):
                row = pl.ds(parts[side][0], 1)
                out_ref[row, :] = out_ref[row, :] + total

        return carry

    lax.fori_loop(0, (q_count + wide - 1) // wide, query_blocks, 0)


def score_call(chunks, qblocks, wide, beta, given, tiles, first):
    width = tiles[0].shape[1]
    slots = 4 * qblocks
    totals_shape = jax.ShapeDtypeStruct((slots, LANES), jnp.float32)
    packed_shape = jax.ShapeDtypeStruct((slots * LANES, width), jnp.bfloat16)
    info_shape = jax.ShapeDtypeStruct((8, LANES), jnp.int32)
    q_list = pltpu.SMEM((slots, 2), jnp.int32)
    spread = pltpu.VMEM((len(tiles) * LANES, LANES), jnp.float32)
    info = pltpu.SMEM((8, LANES), jnp.int32)
    return pl.pallas_call(
        functools.partial(score_kernel, chunks, qblocks, first, wide),
        out_shape=(totals_shape, packed_shape, info_shape) if first else totals_shape,
        in_specs=[SMEM, VMEM if first else SMEM] + [VMEM] * (len(given) - 1 + len(tiles)),
        out_specs=(VMEM, VMEM, VMEM) if first else VMEM,
        scratch_shapes=[q_list, info, spread, spread, pltpu.SemaphoreType.DMA]
        if first
        else [q_list, spread, spread],
        compiler_params=PARAMS,
        cost_estimate=cost(2 * slots * len(tiles) * LANES**2 * width, 2 * slots * LANES * width),
    )(beta, *given, *tiles)


def per_device(
    queries,
    query_block_cluster,
    block_count,
    references,
    ref_cluster,
    ref_rows,
    cluster_beta,
    cluster_member_count,
):
    nblk, nhelper = lax.axis_size("blk"), lax.axis_size("helper")
    helper = lax.axis_index("helper").astype(jnp.int32)
    qblocks = query_block_cluster.shape[0]
    q_rows, (rows, width) = queries.shape[0], references.shape
    tiles = rows // LANES
    chunks = tiles // nhelper
    sources = nblk // 2

    own = pl.pallas_call(
        functools.partial(pack_refs_kernel, nhelper),
        out_shape=[
            jax.ShapeDtypeStruct((LANES + (TABLE if c == 0 else 0), width), jnp.bfloat16)
            for c in range(chunks)
        ],
        in_specs=[SMEM] + [HBM] * 3,
        out_specs=[VMEM] * chunks,
        scratch_shapes=[
            pltpu.VMEM((tiles, LANES), jnp.int32),
            pltpu.SMEM((1, 1), jnp.int32),
            pltpu.SemaphoreType.DMA((chunks + 2,)),
        ],
        compiler_params=WHOLE,
        cost_estimate=cost(1, 4 * rows * width),
    )(helper[None], references, ref_cluster.reshape(tiles, LANES), ref_rows.reshape(1, 1))
    q_own = pl.pallas_call(
        pack_queries_kernel,
        out_shape=jax.ShapeDtypeStruct((q_rows + TABLE, width), jnp.bfloat16),
        in_specs=[HBM] * 3,
        out_specs=VMEM,
        scratch_shapes=[
            pltpu.SMEM((qblocks,), jnp.int32),
            pltpu.SMEM((1, 1), jnp.int32),
            pltpu.SemaphoreType.DMA((3,)),
        ],
        compiler_params=WHOLE,
        cost_estimate=cost(1, 8 * q_rows * width),
    )(after(queries, *own), query_block_cluster, block_count.reshape(1, 1))
    q_partner = swap(q_own, "blk")
    q_helper = swap(q_own, "helper")

    above, below = [own], [own]
    for step in range(1, (sources + 1) // 2):
        above.append([turn(x, 2) for x in above[-1]])
        below.append([turn(x, -2) for x in below[-1]])
    early = [x for step in [own] + above[1:] + below[1:] for x in step]
    half = chunks // 2
    last = [turn(x, 2) for x in above[-1][:half]] + [turn(x, -2) for x in below[-1][half:]]
    q_both = swap(after(q_partner, *above[-1], *below[-1]), "helper")

    totals, packed, info = score_call(
        chunks, qblocks, 2, cluster_beta, (q_own, q_helper, q_partner, q_both), early, True
    )
    totals = score_call(
        chunks, qblocks, 4, cluster_beta, (info, packed, totals), last, False
    )
    totals = totals.reshape(4, qblocks, LANES)
    total = totals[0] + swap(totals[1], "helper") + swap(totals[2], "blk") + swap_both(totals[3])
    columns = jnp.arange(cluster_member_count.shape[0], dtype=jnp.int32)
    onehot = query_block_cluster[:, None] == columns[None, :]
    sizes = jnp.sum(jnp.where(onehot, cluster_member_count[None, :], 0), axis=1)
    density = jnp.log1p(total / sizes.astype(jnp.float32)[:, None])
    return density.reshape(queries.shape[0])


def solution(mesh):
    in_specs = (
        P(("parts", "blk", "helper"), None),
        P(("parts", "blk", "helper")),
        P(("parts", "blk", "helper")),
        P(("parts", "blk"), None),
        P(("parts", "blk")),
        P(("parts", "blk")),
        P("parts"),
        P("parts"),
    )
    out_specs = P(("parts", "blk", "helper"))
    return jax.shard_map(
        per_device, mesh=mesh, in_specs=in_specs, out_specs=out_specs, check_vma=False
    )
```

```python
import functools
import math

import jax
import jax.numpy as jnp
from jax import lax
from jax.experimental import pallas as pl
from jax.experimental.pallas import tpu as pltpu
from jax.sharding import PartitionSpec as P

LANES = 128
TABLE = 16
LOG2E = 1.4426950408889634
DEAD = -1.0e30
SMEM = pl.BlockSpec(memory_space=pltpu.SMEM)
VMEM = pl.BlockSpec(memory_space=pltpu.VMEM)
PARAMS = pltpu.CompilerParams(vmem_limit_bytes=24 * 1024 * 1024)


def turn(value, by):
    length = lax.axis_size("blk")
    return lax.ppermute(value, "blk", [(i, (i + by) % length) for i in range(length)])


def swap(value, axis):
    length = lax.axis_size(axis)
    return lax.ppermute(value, axis, [(i, i ^ 1) for i in range(length)])


def swap_both(value):
    nblk, nhelper = lax.axis_size("blk"), lax.axis_size("helper")
    pairs = [(i, (i ^ nhelper) ^ 1) for i in range(nblk * nhelper)]
    return lax.ppermute(value, ("blk", "helper"), pairs)


def after(value, *others):
    return lax.optimization_barrier((value, *others))[0]


def cost(flops, moved):
    return pl.CostEstimate(flops=flops, bytes_accessed=moved, transcendentals=0)


def rows_of(index, count=1):
    return pl.ds(pl.multiple_of(index * LANES, LANES), count * LANES)


def cut_kernel(nhelper, helper_ref, live_ref, ids_ref, r_ref, *outs):
    lane = lax.broadcasted_iota(jnp.int32, (TABLE, LANES), 1)
    row = lax.broadcasted_iota(jnp.int32, (TABLE, LANES), 0)
    table = jnp.full((TABLE, LANES), -1, jnp.int32)
    for c, out in enumerate(outs):
        tile = helper_ref[0] + nhelper * c
        here = jnp.where(tile * LANES + lane < live_ref[0], ids_ref[pl.ds(tile, 1), :], -1)
        table = jnp.where(row == c, here, table)
        out[pl.ds(0, LANES), :] = r_ref[rows_of(tile), :]
    outs[-1][pl.ds(LANES, TABLE), pl.ds(0, LANES)] = table.astype(jnp.float32).astype(jnp.bfloat16)


def table_kernel(clusters_ref, count_ref, out):
    qblocks = clusters_ref.shape[0]
    lane = lax.broadcasted_iota(jnp.int32, out.shape, 1)
    table = jnp.where(lane == qblocks, count_ref[0], 0)
    for k in range(qblocks):
        table = jnp.where(lane == k, clusters_ref[k], table)
    out[...] = table


def score_kernel(chunks, qblocks, first, wide, beta_ref, *refs):
    if first:
        q_refs, t_refs, refs = refs[:4], refs[4:8], refs[8:]
        r_refs, (out_ref, qv, info_out, q_list, info, ids_ref, other_ref, sem) = refs[:-8], refs[-8:]
    else:
        (info, qv, prev_ref), refs = refs[:3], refs[3:]
        r_refs, (out_ref, q_list, ids_ref, other_ref) = refs[:-4], refs[-4:]
    width = qv.shape[1]
    sources = len(r_refs) // chunks
    if first:
        for s, t_ref in enumerate(t_refs):
            info_out[s : s + 1, :] = t_ref[0:1, :]
        copy = pltpu.make_async_copy(info_out, info, sem)
        copy.start()

    for s in range(sources):
        last = r_refs[(s + 1) * chunks - 1]
        table = last[pl.ds(LANES, TABLE), pl.ds(0, LANES)].astype(jnp.float32)
        for c in range(chunks):
            ids = jnp.broadcast_to(table[c : c + 1, :], (LANES, LANES)).T
            rows = pl.ds((s * chunks + c) * LANES, LANES)
            ids_ref[rows, :] = ids
            other_ref[rows, :] = jnp.where(ids < 0.0, DEAD, -4.0)
    if first:
        copy.wait()

    q_count = jnp.int32(0)
    for source in range(4):
        blocks = info[source, qblocks]

        def one_block(block, carry, source=source, q_count=q_count):
            if first:
                qv[rows_of(q_count + block), :] = q_refs[source][rows_of(block), :]
            q_list[q_count + block, 0] = source * qblocks + block
            q_list[q_count + block, 1] = info[source, block]
            return carry

        lax.fori_loop(0, blocks, one_block, 0)
        q_count = q_count + blocks

    factor = LOG2E / math.sqrt(width)
    out_ref[...] = jnp.zeros_like(out_ref) if first else prev_ref[...]

    def query_blocks(group, carry):
        parts = []
        for side in range(wide):
            entry = jnp.minimum(wide * group + side, q_count - 1)
            slot, cluster = q_list[entry, 0], q_list[entry, 1]
            beta = beta_ref[cluster]
            parts.append(
                (slot, cluster.astype(jnp.float32), beta * factor, beta * beta * (0.5 * LOG2E))
            )
        accs = [jnp.zeros((8, LANES), jnp.float32) for _ in range(wide)]
        for s in range(sources):
            held = r_refs[s * chunks : (s + 1) * chunks]
            tile = jnp.concatenate([r[pl.ds(0, LANES), :] for r in held], axis=0)
            height = tile.shape[0]
            rows = pl.ds(s * height, height)
            for pair in range(wide // 2):
                score = lax.dot_general(
                    tile,
                    qv[rows_of(wide * group + 2 * pair, 2), :],
                    (((1,), (1,)), ((), ())),
                    preferred_element_type=jnp.float32,
                )
                for half in range(2):
                    side = 2 * pair + half
                    _, cluster, scale, offset = parts[side]
                    part = score[:, half * LANES : (half + 1) * LANES]
                    weight = jnp.where(ids_ref[rows, :] == cluster, 0.0, other_ref[rows, :])
                    value = jnp.exp2((part * scale - offset) + weight)
                    accs[side] += jnp.sum(value.reshape(height // 8, 8, LANES), axis=0)
        for side in range(wide):
            total = jnp.sum(accs[side], axis=0, keepdims=True)

            @pl.when(wide * group + side < q_count)
            def _(side=side, total=total):
                row = pl.ds(parts[side][0], 1)
                out_ref[row, :] = out_ref[row, :] + total

        return carry

    lax.fori_loop(0, (q_count + wide - 1) // wide, query_blocks, 0)


def score_call(chunks, qblocks, wide, beta, given, tiles, first):
    width = tiles[0].shape[1]
    slots = 4 * qblocks
    totals_shape = jax.ShapeDtypeStruct((slots, LANES), jnp.float32)
    packed_shape = jax.ShapeDtypeStruct((slots * LANES, width), jnp.bfloat16)
    info_shape = jax.ShapeDtypeStruct((8, LANES), jnp.int32)
    q_list = pltpu.SMEM((slots, 2), jnp.int32)
    spread = pltpu.VMEM((len(tiles) * LANES, LANES), jnp.float32)
    info = pltpu.SMEM((8, LANES), jnp.int32)
    return pl.pallas_call(
        functools.partial(score_kernel, chunks, qblocks, first, wide),
        out_shape=(totals_shape, packed_shape, info_shape) if first else totals_shape,
        in_specs=[SMEM, VMEM if first else SMEM] + [VMEM] * (len(given) - 1 + len(tiles)),
        out_specs=(VMEM, VMEM, VMEM) if first else VMEM,
        scratch_shapes=[q_list, info, spread, spread, pltpu.SemaphoreType.DMA]
        if first
        else [q_list, spread, spread],
        compiler_params=PARAMS,
        cost_estimate=cost(2 * slots * len(tiles) * LANES**2 * width, 2 * slots * LANES * width),
    )(beta, *given, *tiles)


def per_device(
    queries,
    query_block_cluster,
    block_count,
    references,
    ref_cluster,
    ref_rows,
    cluster_beta,
    cluster_member_count,
):
    nblk, nhelper = lax.axis_size("blk"), lax.axis_size("helper")
    helper = lax.axis_index("helper").astype(jnp.int32)
    qblocks = query_block_cluster.shape[0]
    rows, width = references.shape
    tiles = rows // LANES
    chunks = tiles // nhelper
    sources = nblk // 2

    q_partner = swap(queries, "blk")
    own = pl.pallas_call(
        functools.partial(cut_kernel, nhelper),
        out_shape=[
            jax.ShapeDtypeStruct((LANES + (TABLE if c == chunks - 1 else 0), width), jnp.bfloat16)
            for c in range(chunks)
        ],
        in_specs=[SMEM] * 2 + [VMEM] * 2,
        out_specs=[VMEM] * chunks,
        compiler_params=PARAMS,
        cost_estimate=cost(1, 4 * LANES * width),
    )(helper[None], ref_rows, ref_cluster.reshape(tiles, LANES), references)
    table = pl.pallas_call(
        table_kernel,
        out_shape=jax.ShapeDtypeStruct((8, LANES), jnp.int32),
        in_specs=[SMEM] * 2,
        out_specs=VMEM,
        compiler_params=PARAMS,
        cost_estimate=cost(1, 4 * LANES * width),
    )(after(query_block_cluster, *own), block_count)
    q_helper = swap(queries, "helper")
    tables = (table, swap(table, "helper"), swap(table, "blk"), swap_both(table))

    above, below = [own], [own]
    for step in range(1, (sources + 1) // 2):
        above.append([turn(x, 2) for x in above[-1]])
        below.append([turn(x, -2) for x in below[-1]])
    early = [x for step in [own] + above[1:] + below[1:] for x in step]
    half = chunks // 2
    last = [turn(x, 2) for x in above[-1][:half]] + [turn(x, -2) for x in below[-1][half:]]
    q_both = swap(after(q_partner, *above[-1], *below[-1], *tables), "helper")

    totals, packed, info = score_call(
        chunks, qblocks, 2, cluster_beta, (queries, q_helper, q_partner, q_both, *tables), early, True
    )
    totals = score_call(
        chunks, qblocks, 4, cluster_beta, (info, packed, totals), last, False
    )
    totals = totals.reshape(4, qblocks, LANES)
    total = totals[0] + swap(totals[1], "helper") + swap(totals[2], "blk") + swap_both(totals[3])
    columns = jnp.arange(cluster_member_count.shape[0], dtype=jnp.int32)
    onehot = query_block_cluster[:, None] == columns[None, :]
    sizes = jnp.sum(jnp.where(onehot, cluster_member_count[None, :], 0), axis=1)
    density = jnp.log1p(total / sizes.astype(jnp.float32)[:, None])
    return density.reshape(queries.shape[0])


def solution(mesh):
    in_specs = (
        P(("parts", "blk", "helper"), None),
        P(("parts", "blk", "helper")),
        P(("parts", "blk", "helper")),
        P(("parts", "blk"), None),
        P(("parts", "blk")),
        P(("parts", "blk")),
        P("parts"),
        P("parts"),
    )
    out_specs = P(("parts", "blk", "helper"))
    return jax.shard_map(
        per_device, mesh=mesh, in_specs=in_specs, out_specs=out_specs, check_vma=False
    )
```

```python
import functools
import math

import jax
import jax.numpy as jnp
from jax import lax
from jax.experimental import pallas as pl
from jax.experimental.pallas import tpu as pltpu
from jax.sharding import PartitionSpec as P

LANES = 128
TABLE = 16
LOG2E = 1.4426950408889634
DEAD = -1.0e30
SMEM = pl.BlockSpec(memory_space=pltpu.SMEM)
VMEM = pl.BlockSpec(memory_space=pltpu.VMEM)
ANY = pl.BlockSpec(memory_space=pl.ANY)
WHOLE = pltpu.CompilerParams(vmem_limit_bytes=60 * 1024 * 1024)
PARAMS = pltpu.CompilerParams(vmem_limit_bytes=24 * 1024 * 1024)


def turn(value, by):
    length = lax.axis_size("blk")
    return lax.ppermute(value, "blk", [(i, (i + by) % length) for i in range(length)])


def swap(value, axis):
    length = lax.axis_size(axis)
    return lax.ppermute(value, axis, [(i, i ^ 1) for i in range(length)])


def swap_both(value):
    nblk, nhelper = lax.axis_size("blk"), lax.axis_size("helper")
    pairs = [(i, (i ^ nhelper) ^ 1) for i in range(nblk * nhelper)]
    return lax.ppermute(value, ("blk", "helper"), pairs)


def after(value, *others):
    return lax.optimization_barrier((value, *others))[0]


def cost(flops, moved):
    return pl.CostEstimate(flops=flops, bytes_accessed=moved, transcendentals=0)


def rows_of(index, count=1):
    return pl.ds(pl.multiple_of(index * LANES, LANES), count * LANES)


def pack_kernel(
    nhelper, helper_ref, r_ref, q_ref, ids_ref, clusters_ref, live_ref, count_ref, r_out, q_out, *scratch
):
    ids, clusters, live, count, sem = scratch
    chunks = ids_ref.shape[0] // nhelper
    qblocks = clusters_ref.shape[0]
    small = [
        pltpu.make_async_copy(ids_ref, ids, sem.at[0]),
        pltpu.make_async_copy(clusters_ref, clusters, sem.at[1]),
        pltpu.make_async_copy(live_ref, live, sem.at[2]),
        pltpu.make_async_copy(count_ref, count, sem.at[3]),
    ]
    large = [pltpu.make_async_copy(q_ref, q_out.at[pl.ds(0, qblocks * LANES)], sem.at[4])]
    for c in range(chunks):
        rows = rows_of(helper_ref[0] + nhelper * c)
        large.append(pltpu.make_async_copy(r_ref.at[rows], r_out.at[rows_of(c)], sem.at[5 + c]))
    for copy in small + large:
        copy.start()
    for copy in small:
        copy.wait()
    lane = lax.broadcasted_iota(jnp.int32, (TABLE, LANES), 1)
    row = lax.broadcasted_iota(jnp.int32, (TABLE, LANES), 0)
    table = jnp.full((TABLE, LANES), -1, jnp.int32)
    for c in range(chunks):
        tile = helper_ref[0] + nhelper * c
        here = jnp.where(tile * LANES + lane < live[0], ids[pl.ds(tile, 1), :], -1)
        table = jnp.where(row == c, here, table)
    columns = pl.ds(0, LANES)
    r_out[pl.ds(chunks * LANES, TABLE), columns] = table.astype(jnp.float32).astype(jnp.bfloat16)
    table = jnp.where(lane == qblocks, count[0], 0)
    for k in range(qblocks):
        table = jnp.where(lane == k, clusters[k], table)
    q_out[pl.ds(qblocks * LANES, TABLE), columns] = table.astype(jnp.float32).astype(jnp.bfloat16)
    for copy in large:
        copy.wait()


def score_kernel(chunks, qblocks, first, wide, beta_ref, *refs):
    if first:
        q_refs, r_refs, refs = list(refs[:4]), list(refs[4:-11]), refs[-11:]
        out_ref, qv, info_out, q_list, ids_ref, other_ref, info, q_own, r_own, sem, info_sem = refs
        fetch = (
            pltpu.make_async_copy(r_refs[0], r_own, sem.at[0]),
            pltpu.make_async_copy(q_refs[0], q_own, sem.at[1]),
        )
        q_refs[0], r_refs[0] = q_own, r_own
    else:
        info, qv, prev_ref, *r_refs, out_ref, q_list, ids_ref, other_ref = refs
        fetch = ()
    width = qv.shape[1]
    height = chunks * LANES
    for copy in fetch:
        copy.start()

    def spread(s):
        table = r_refs[s][pl.ds(height, TABLE), pl.ds(0, LANES)].astype(jnp.float32)
        for c in range(chunks):
            ids = jnp.broadcast_to(table[c : c + 1, :], (LANES, LANES)).T
            rows = pl.ds(s * height + c * LANES, LANES)
            ids_ref[rows, :] = ids
            other_ref[rows, :] = jnp.where(ids < 0.0, DEAD, -4.0)

    for s in range(len(fetch) // 2, len(r_refs)):
        spread(s)
    for copy in fetch:
        copy.wait()
    if first:
        spread(0)
        for s, q_ref in enumerate(q_refs):
            table = q_ref[pl.ds(qblocks * LANES, TABLE), pl.ds(0, LANES)].astype(jnp.float32)
            info_out[s : s + 1, :] = table[0:1, :].astype(jnp.int32)
        copy = pltpu.make_async_copy(info_out, info, info_sem)
        copy.start()
        copy.wait()

    q_count = jnp.int32(0)
    for source in range(4):
        blocks = info[source, qblocks]

        def one_block(block, carry, source=source, q_count=q_count):
            if first:
                qv[rows_of(q_count + block), :] = q_refs[source][rows_of(block), :]
            q_list[q_count + block, 0] = source * qblocks + block
            q_list[q_count + block, 1] = info[source, block]
            return carry

        lax.fori_loop(0, blocks, one_block, 0)
        q_count = q_count + blocks

    factor = LOG2E / math.sqrt(width)
    out_ref[...] = jnp.zeros_like(out_ref) if first else prev_ref[...]

    def query_blocks(group, carry):
        parts = []
        for side in range(wide):
            entry = jnp.minimum(wide * group + side, q_count - 1)
            slot, cluster = q_list[entry, 0], q_list[entry, 1]
            beta = beta_ref[cluster]
            parts.append(
                (slot, cluster.astype(jnp.float32), beta * factor, beta * beta * (0.5 * LOG2E))
            )
        accs = [jnp.zeros((8, LANES), jnp.float32) for _ in range(wide)]
        for s, r_ref in enumerate(r_refs):
            tile = r_ref[pl.ds(0, height), :]
            rows = pl.ds(s * height, height)
            for pair in range(wide // 2):
                score = lax.dot_general(
                    tile,
                    qv[rows_of(wide * group + 2 * pair, 2), :],
                    (((1,), (1,)), ((), ())),
                    preferred_element_type=jnp.float32,
                )
                for half in range(2):
                    side = 2 * pair + half
                    _, cluster, scale, offset = parts[side]
                    part = score[:, half * LANES : (half + 1) * LANES]
                    weight = jnp.where(ids_ref[rows, :] == cluster, 0.0, other_ref[rows, :])
                    value = jnp.exp2((part * scale - offset) + weight)
                    accs[side] += jnp.sum(value.reshape(height // 8, 8, LANES), axis=0)
        for side in range(wide):
            total = jnp.sum(accs[side], axis=0, keepdims=True)

            @pl.when(wide * group + side < q_count)
            def _(side=side, total=total):
                row = pl.ds(parts[side][0], 1)
                out_ref[row, :] = out_ref[row, :] + total

        return carry

    lax.fori_loop(0, (q_count + wide - 1) // wide, query_blocks, 0)


def score_call(chunks, qblocks, wide, beta, given, payloads, first):
    width = payloads[0].shape[1]
    slots = 4 * qblocks
    height = chunks * LANES
    totals_shape = jax.ShapeDtypeStruct((slots, LANES), jnp.float32)
    packed_shape = jax.ShapeDtypeStruct((slots * LANES, width), jnp.bfloat16)
    info_shape = jax.ShapeDtypeStruct((8, LANES), jnp.int32)
    spread = pltpu.VMEM((len(payloads) * height, LANES), jnp.float32)
    scratch = [pltpu.SMEM((slots, 2), jnp.int32), spread, spread]
    specs = [VMEM] * (len(given) + len(payloads))
    if first:
        specs[0] = specs[len(given)] = ANY
        scratch += [
            pltpu.SMEM((8, LANES), jnp.int32),
            pltpu.VMEM(given[0].shape, jnp.bfloat16),
            pltpu.VMEM(payloads[0].shape, jnp.bfloat16),
            pltpu.SemaphoreType.DMA((2,)),
            pltpu.SemaphoreType.DMA,
        ]
    else:
        specs[0] = SMEM
    return pl.pallas_call(
        functools.partial(score_kernel, chunks, qblocks, first, wide),
        out_shape=(totals_shape, packed_shape, info_shape) if first else totals_shape,
        in_specs=[SMEM] + specs,
        out_specs=(VMEM, VMEM, VMEM) if first else VMEM,
        scratch_shapes=scratch,
        compiler_params=PARAMS,
        cost_estimate=cost(
            2 * slots * LANES * len(payloads) * height * width, 2 * slots * LANES * width
        ),
    )(beta, *given, *payloads)


def per_device(
    queries,
    query_block_cluster,
    block_count,
    references,
    ref_cluster,
    ref_rows,
    cluster_beta,
    cluster_member_count,
):
    nblk, nhelper = lax.axis_size("blk"), lax.axis_size("helper")
    helper = lax.axis_index("helper").astype(jnp.int32)
    qblocks = query_block_cluster.shape[0]
    rows, width = references.shape
    tiles = rows // LANES
    chunks = tiles // nhelper
    sources = nblk // 2

    own, q_own = pl.pallas_call(
        functools.partial(pack_kernel, nhelper),
        out_shape=(
            jax.ShapeDtypeStruct((chunks * LANES + TABLE, width), jnp.bfloat16),
            jax.ShapeDtypeStruct((queries.shape[0] + TABLE, width), jnp.bfloat16),
        ),
        in_specs=[SMEM] + [ANY] * 6,
        out_specs=(VMEM, VMEM),
        scratch_shapes=[
            pltpu.VMEM((tiles, LANES), jnp.int32),
            pltpu.SMEM((qblocks,), jnp.int32),
            pltpu.SMEM((1,), jnp.int32),
            pltpu.SMEM((1,), jnp.int32),
            pltpu.SemaphoreType.DMA((5 + chunks,)),
        ],
        compiler_params=WHOLE,
        cost_estimate=cost(1, 4 * rows * width),
    )(
        helper[None],
        references,
        queries,
        ref_cluster.reshape(tiles, LANES),
        query_block_cluster,
        ref_rows,
        block_count,
    )
    q_partner = swap(q_own, "blk")
    q_helper = swap(q_own, "helper")

    above, below = [own], [own]
    for step in range(1, sources // 2 + 1):
        above.append(turn(above[-1], 2))
        if step < (sources + 1) // 2:
            below.append(turn(below[-1], -2))
    early = [own] + above[1:-1] + below[1:]
    q_both = swap(after(q_partner, above[-2], below[-1]), "helper")

    totals, packed, info = score_call(
        chunks, qblocks, 2, cluster_beta, (q_own, q_helper, q_partner, q_both), early, True
    )
    totals = score_call(
        chunks, qblocks, 4, cluster_beta, (info, packed, totals), above[-1:], False
    )
    totals = totals.reshape(4, qblocks, LANES)
    total = totals[0] + swap(totals[1], "helper") + swap(totals[2], "blk") + swap_both(totals[3])
    columns = jnp.arange(cluster_member_count.shape[0], dtype=jnp.int32)
    onehot = query_block_cluster[:, None] == columns[None, :]
    sizes = jnp.sum(jnp.where(onehot, cluster_member_count[None, :], 0), axis=1)
    density = jnp.log1p(total / sizes.astype(jnp.float32)[:, None])
    return density.reshape(queries.shape[0])


def solution(mesh):
    in_specs = (
        P(("parts", "blk", "helper"), None),
        P(("parts", "blk", "helper")),
        P(("parts", "blk", "helper")),
        P(("parts", "blk"), None),
        P(("parts", "blk")),
        P(("parts", "blk")),
        P("parts"),
        P("parts"),
    )
    out_specs = P(("parts", "blk", "helper"))
    return jax.shard_map(
        per_device, mesh=mesh, in_specs=in_specs, out_specs=out_specs, check_vma=False
    )
```

```python
import functools
import math

import jax
import jax.numpy as jnp
from jax import lax
from jax.experimental import pallas as pl
from jax.experimental.pallas import tpu as pltpu
from jax.sharding import PartitionSpec as P

LANES = 128
TABLE = 16
LOG2E = 1.4426950408889634
DEAD = -1.0e30
SMEM = pl.BlockSpec(memory_space=pltpu.SMEM)
VMEM = pl.BlockSpec(memory_space=pltpu.VMEM)
ANY = pl.BlockSpec(memory_space=pl.ANY)
WHOLE = pltpu.CompilerParams(vmem_limit_bytes=60 * 1024 * 1024)
PARAMS = pltpu.CompilerParams(vmem_limit_bytes=24 * 1024 * 1024)


def turn(value, by):
    length = lax.axis_size("blk")
    return lax.ppermute(value, "blk", [(i, (i + by) % length) for i in range(length)])


def swap(value, axis):
    length = lax.axis_size(axis)
    return lax.ppermute(value, axis, [(i, i ^ 1) for i in range(length)])


def swap_both(value):
    nblk, nhelper = lax.axis_size("blk"), lax.axis_size("helper")
    pairs = [(i, (i ^ nhelper) ^ 1) for i in range(nblk * nhelper)]
    return lax.ppermute(value, ("blk", "helper"), pairs)


def after(value, *others):
    return lax.optimization_barrier((value, *others))[0]


def cost(flops, moved):
    return pl.CostEstimate(flops=flops, bytes_accessed=moved, transcendentals=0)


def rows_of(index, count=1):
    return pl.ds(pl.multiple_of(index * LANES, LANES), count * LANES)


def pack_kernel(
    nhelper, helper_ref, r_ref, q_ref, ids_ref, clusters_ref, live_ref, count_ref, r_out, *outs
):
    q_outs, (ids, clusters, live, count, sem) = outs[:-5], outs[-5:]
    chunks = ids_ref.shape[0] // nhelper
    qblocks = clusters_ref.shape[0]
    small = [
        pltpu.make_async_copy(ids_ref, ids, sem.at[0]),
        pltpu.make_async_copy(clusters_ref, clusters, sem.at[1]),
        pltpu.make_async_copy(live_ref, live, sem.at[2]),
        pltpu.make_async_copy(count_ref, count, sem.at[3]),
    ]
    large, height = [], qblocks * LANES // len(q_outs)
    for p, q_out in enumerate(q_outs):
        source = q_ref.at[pl.ds(p * height, height)]
        large.append(
            pltpu.make_async_copy(source, q_out.at[pl.ds(0, height)], sem.at[4 + chunks + p])
        )
    for c in range(chunks):
        rows = rows_of(helper_ref[0] + nhelper * c)
        large.append(pltpu.make_async_copy(r_ref.at[rows], r_out.at[rows_of(c)], sem.at[4 + c]))
    for copy in small + large:
        copy.start()
    for copy in small:
        copy.wait()
    lane = lax.broadcasted_iota(jnp.int32, (TABLE, LANES), 1)
    row = lax.broadcasted_iota(jnp.int32, (TABLE, LANES), 0)
    table = jnp.full((TABLE, LANES), -1, jnp.int32)
    for c in range(chunks):
        tile = helper_ref[0] + nhelper * c
        here = jnp.where(tile * LANES + lane < live[0], ids[pl.ds(tile, 1), :], -1)
        table = jnp.where(row == c, here, table)
    columns = pl.ds(0, LANES)
    r_out[pl.ds(chunks * LANES, TABLE), columns] = table.astype(jnp.float32).astype(jnp.bfloat16)
    table = jnp.where(lane == qblocks, count[0], 0)
    for k in range(qblocks):
        table = jnp.where(lane == k, clusters[k], table)
    q_outs[0][pl.ds(height, TABLE), columns] = table.astype(jnp.float32).astype(jnp.bfloat16)
    for copy in large:
        copy.wait()


def score_kernel(chunks, qblocks, parts, first, wide, beta_ref, *refs):
    if first:
        q_refs = [list(refs[i : i + parts]) for i in range(0, 4 * parts, parts)]
        r_refs, refs = list(refs[4 * parts : -10 - parts]), refs[-10 - parts :]
        out_ref, qv, info_out, q_list, ids_ref, other_ref, info, sem, info_sem, r_own, *q_own = refs
        fetch = [pltpu.make_async_copy(r_refs[0], r_own, sem.at[parts])]
        for p in range(parts):
            fetch.append(pltpu.make_async_copy(q_refs[0][p], q_own[p], sem.at[p]))
        q_refs[0], r_refs[0] = q_own, r_own
    else:
        info, qv, prev_ref, *r_refs, out_ref, q_list, ids_ref, other_ref = refs
        fetch = ()
    width = qv.shape[1]
    height = chunks * LANES
    for copy in fetch:
        copy.start()

    def spread(s):
        table = r_refs[s][pl.ds(height, TABLE), pl.ds(0, LANES)].astype(jnp.float32)
        for c in range(chunks):
            ids = jnp.broadcast_to(table[c : c + 1, :], (LANES, LANES)).T
            rows = pl.ds(s * height + c * LANES, LANES)
            ids_ref[rows, :] = ids
            other_ref[rows, :] = jnp.where(ids < 0.0, DEAD, -4.0)

    for s in range(1 if first else 0, len(r_refs)):
        spread(s)
    for copy in fetch:
        copy.wait()
    if first:
        spread(0)
        for s, q_ref in enumerate(q_refs):
            behind = pl.ds(qblocks * LANES // parts, TABLE)
            table = q_ref[0][behind, pl.ds(0, LANES)].astype(jnp.float32)
            info_out[s : s + 1, :] = table[0:1, :].astype(jnp.int32)
        copy = pltpu.make_async_copy(info_out, info, info_sem)
        copy.start()
        copy.wait()

    q_count = jnp.int32(0)
    for source in range(4):
        blocks = info[source, qblocks]

        def one_block(block, carry, source=source, q_count=q_count):
            q_list[q_count + block, 0] = source * qblocks + block
            q_list[q_count + block, 1] = info[source, block]
            return carry

        lax.fori_loop(0, blocks, one_block, 0)
        each = qblocks // parts
        for p in range(parts if first else 0):

            def move(block, carry, source=source, q_count=q_count, p=p):
                place = rows_of(q_count + p * each + block)
                qv[place, :] = q_refs[source][p][rows_of(block), :]
                return carry

            lax.fori_loop(0, jnp.clip(blocks - p * each, 0, each), move, 0)
        q_count = q_count + blocks

    factor = LOG2E / math.sqrt(width)
    out_ref[...] = jnp.zeros_like(out_ref) if first else prev_ref[...]

    def query_blocks(group, carry):
        sides = []
        for side in range(wide):
            entry = jnp.minimum(wide * group + side, q_count - 1)
            slot, cluster = q_list[entry, 0], q_list[entry, 1]
            beta = beta_ref[cluster]
            sides.append(
                (slot, cluster.astype(jnp.float32), beta * factor, beta * beta * (0.5 * LOG2E))
            )
        accs = [jnp.zeros((8, LANES), jnp.float32) for _ in range(wide)]
        for s, r_ref in enumerate(r_refs):
            tile = r_ref[pl.ds(0, height), :]
            rows = pl.ds(s * height, height)
            for pair in range(wide // 2):
                score = lax.dot_general(
                    tile,
                    qv[rows_of(wide * group + 2 * pair, 2), :],
                    (((1,), (1,)), ((), ())),
                    preferred_element_type=jnp.float32,
                )
                for half in range(2):
                    side = 2 * pair + half
                    _, cluster, scale, offset = sides[side]
                    part = score[:, half * LANES : (half + 1) * LANES]
                    weight = jnp.where(ids_ref[rows, :] == cluster, 0.0, other_ref[rows, :])
                    value = jnp.exp2((part * scale - offset) + weight)
                    accs[side] += jnp.sum(value.reshape(height // 8, 8, LANES), axis=0)
        for side in range(wide):
            total = jnp.sum(accs[side], axis=0, keepdims=True)

            @pl.when(wide * group + side < q_count)
            def _(side=side, total=total):
                row = pl.ds(sides[side][0], 1)
                out_ref[row, :] = out_ref[row, :] + total

        return carry

    lax.fori_loop(0, (q_count + wide - 1) // wide, query_blocks, 0)


def score_call(chunks, qblocks, parts, wide, beta, given, payloads, first):
    width = payloads[0].shape[1]
    slots = 4 * qblocks
    height = chunks * LANES
    totals_shape = jax.ShapeDtypeStruct((slots, LANES), jnp.float32)
    packed_shape = jax.ShapeDtypeStruct((slots * LANES, width), jnp.bfloat16)
    info_shape = jax.ShapeDtypeStruct((8, LANES), jnp.int32)
    spread = pltpu.VMEM((len(payloads) * height, LANES), jnp.float32)
    scratch = [pltpu.SMEM((slots, 2), jnp.int32), spread, spread]
    specs = [VMEM] * (len(given) + len(payloads))
    if first:
        for i in (*range(parts), len(given)):
            specs[i] = ANY
        scratch += [
            pltpu.SMEM((8, LANES), jnp.int32),
            pltpu.SemaphoreType.DMA((parts + 1,)),
            pltpu.SemaphoreType.DMA,
            pltpu.VMEM(payloads[0].shape, jnp.bfloat16),
            *[pltpu.VMEM(q.shape, jnp.bfloat16) for q in given[:parts]],
        ]
    else:
        specs[0] = SMEM
    return pl.pallas_call(
        functools.partial(score_kernel, chunks, qblocks, parts, first, wide),
        out_shape=(totals_shape, packed_shape, info_shape) if first else totals_shape,
        in_specs=[SMEM] + specs,
        out_specs=(VMEM, VMEM, VMEM) if first else VMEM,
        scratch_shapes=scratch,
        compiler_params=PARAMS,
        cost_estimate=cost(1, 1),
    )(beta, *given, *payloads)


def per_device(
    queries,
    query_block_cluster,
    block_count,
    references,
    ref_cluster,
    ref_rows,
    cluster_beta,
    cluster_member_count,
):
    nblk, nhelper = lax.axis_size("blk"), lax.axis_size("helper")
    helper = lax.axis_index("helper").astype(jnp.int32)
    qblocks = query_block_cluster.shape[0]
    rows, width = references.shape
    tiles = rows // LANES
    chunks = tiles // nhelper
    sources = nblk // 2

    parts = 2
    q_height = queries.shape[0] // parts
    own, *q_own = pl.pallas_call(
        functools.partial(pack_kernel, nhelper),
        out_shape=[jax.ShapeDtypeStruct((chunks * LANES + TABLE, width), jnp.bfloat16)]
        + [
            jax.ShapeDtypeStruct((q_height + (TABLE if p == 0 else 0), width), jnp.bfloat16)
            for p in range(parts)
        ],
        in_specs=[SMEM] + [ANY] * 6,
        out_specs=[VMEM] * (1 + parts),
        scratch_shapes=[
            pltpu.VMEM((tiles, LANES), jnp.int32),
            pltpu.SMEM((qblocks,), jnp.int32),
            pltpu.SMEM((1,), jnp.int32),
            pltpu.SMEM((1,), jnp.int32),
            pltpu.SemaphoreType.DMA((4 + chunks + parts,)),
        ],
        compiler_params=WHOLE,
        cost_estimate=cost(1, 4 * rows * width),
    )(
        helper[None],
        references,
        queries,
        ref_cluster.reshape(tiles, LANES),
        query_block_cluster,
        ref_rows,
        block_count,
    )
    q_partner = [swap(q, "blk") for q in q_own]
    q_helper = [swap(q, "helper") for q in q_own]

    above, below = [own], [own]
    for step in range(1, sources // 2 + 1):
        above.append(turn(above[-1], 2))
        if step < (sources + 1) // 2:
            below.append(turn(below[-1], -2))
    early = [own] + above[1:-1] + below[1:]
    q_both = [swap(after(q, above[-2]), "helper") for q in q_partner[:-1]]
    q_both.append(swap(after(q_partner[-1], below[-1]), "helper"))
    all_queries = (*q_own, *q_helper, *q_partner, *q_both)

    totals, packed, info = score_call(
        chunks, qblocks, parts, 2, cluster_beta, all_queries, early, True
    )
    totals = score_call(
        chunks, qblocks, parts, 4, cluster_beta, (info, packed, totals), above[-1:], False
    )
    totals = totals.reshape(4, qblocks, LANES)
    total = totals[0] + swap(totals[1], "helper") + swap(totals[2], "blk") + swap_both(totals[3])
    columns = jnp.arange(cluster_member_count.shape[0], dtype=jnp.int32)
    onehot = query_block_cluster[:, None] == columns[None, :]
    sizes = jnp.sum(jnp.where(onehot, cluster_member_count[None, :], 0), axis=1)
    density = jnp.log1p(total / sizes.astype(jnp.float32)[:, None])
    return density.reshape(queries.shape[0])


def solution(mesh):
    in_specs = (
        P(("parts", "blk", "helper"), None),
        P(("parts", "blk", "helper")),
        P(("parts", "blk", "helper")),
        P(("parts", "blk"), None),
        P(("parts", "blk")),
        P(("parts", "blk")),
        P("parts"),
        P("parts"),
    )
    out_specs = P(("parts", "blk", "helper"))
    return jax.shard_map(
        per_device, mesh=mesh, in_specs=in_specs, out_specs=out_specs, check_vma=False
    )
```

```python
import functools
import math

import jax
import jax.numpy as jnp
from jax import lax
from jax.experimental import pallas as pl
from jax.experimental.pallas import tpu as pltpu
from jax.sharding import PartitionSpec as P

LANES = 128
TABLE = 16
LOG2E = 1.4426950408889634
DEAD = -1.0e30
SMEM = pl.BlockSpec(memory_space=pltpu.SMEM)
VMEM = pl.BlockSpec(memory_space=pltpu.VMEM)
ANY = pl.BlockSpec(memory_space=pl.ANY)
WHOLE = pltpu.CompilerParams(vmem_limit_bytes=60 * 1024 * 1024)
PARAMS = pltpu.CompilerParams(vmem_limit_bytes=24 * 1024 * 1024)


def turn(value, by):
    length = lax.axis_size("blk")
    return lax.ppermute(value, "blk", [(i, (i + by) % length) for i in range(length)])


def swap(value, axis):
    length = lax.axis_size(axis)
    return lax.ppermute(value, axis, [(i, i ^ 1) for i in range(length)])


def swap_both(value):
    nblk, nhelper = lax.axis_size("blk"), lax.axis_size("helper")
    pairs = [(i, (i ^ nhelper) ^ 1) for i in range(nblk * nhelper)]
    return lax.ppermute(value, ("blk", "helper"), pairs)


def after(value, *others):
    return lax.optimization_barrier((value, *others))[0]


def cost(flops, moved):
    return pl.CostEstimate(flops=flops, bytes_accessed=moved, transcendentals=0)


def rows_of(index, count=1):
    return pl.ds(pl.multiple_of(index * LANES, LANES), count * LANES)


def pack_kernel(
    nhelper, helper_ref, r_ref, q_ref, ids_ref, clusters_ref, live_ref, count_ref, r_out, *refs
):
    q_outs, (ids, clusters, live, count, r_table, q_table, sem) = refs[:-7], refs[-7:]
    chunks = ids_ref.shape[0] // nhelper
    qblocks = clusters_ref.shape[0]
    pairs = [(ids_ref, ids), (live_ref, live), (clusters_ref, clusters), (count_ref, count)]
    for c in range(chunks):
        rows = rows_of(helper_ref[0] + nhelper * c)
        pairs.append((r_ref.at[rows], r_out.at[rows_of(c)]))
    start = 0
    for out in q_outs:
        height = out.shape[0] // LANES * LANES
        pairs.append((q_ref.at[pl.ds(start, height)], out.at[pl.ds(0, height)]))
        start += height
    pairs.append((r_table, r_out.at[pl.ds(chunks * LANES, TABLE)]))
    pairs.append((q_table, q_outs[0].at[pl.ds(q_outs[0].shape[0] - TABLE, TABLE)]))
    copies = [pltpu.make_async_copy(*pair, sem.at[i]) for i, pair in enumerate(pairs)]
    for copy in copies[:-2]:
        copy.start()
    for copy in copies[:4]:
        copy.wait()
    lane = lax.broadcasted_iota(jnp.int32, (TABLE, LANES), 1)
    row = lax.broadcasted_iota(jnp.int32, (TABLE, LANES), 0)
    rows = jnp.full((TABLE, LANES), -1, jnp.int32)
    for c in range(chunks):
        tile = helper_ref[0] + nhelper * c
        here = jnp.where(tile * LANES + lane < live[0], ids[pl.ds(tile, 1), :], -1)
        rows = jnp.where(row == c, here, rows)
    r_table[...] = jnp.zeros_like(r_table)
    r_table[:, pl.ds(0, LANES)] = rows.astype(jnp.float32).astype(jnp.bfloat16)
    copies[-2].start()
    rows = jnp.where(lane == qblocks, count[0], 0)
    for k in range(qblocks):
        rows = jnp.where(lane == k, clusters[k], rows)
    q_table[...] = jnp.zeros_like(q_table)
    q_table[:, pl.ds(0, LANES)] = rows.astype(jnp.float32).astype(jnp.bfloat16)
    copies[-1].start()
    for copy in copies[4:]:
        copy.wait()


def stage_kernel(*refs):
    half = len(refs) // 2
    for source, out in zip(refs[:half], refs[half:]):
        out[...] = source[...]


def score_kernel(chunks, qblocks, parts, first, wide, beta_ref, *refs):
    if first:
        q_refs = [refs[i : i + parts] for i in range(0, 4 * parts, parts)]
        r_refs, refs = refs[4 * parts : -8], refs[-8:]
        out_ref, qv, info_out, q_list, ids_ref, other_ref, info, info_sem = refs
    else:
        info, qv, prev_ref, *r_refs, out_ref, q_list, ids_ref, other_ref = refs
    width = qv.shape[1]
    height = chunks * LANES

    for s in range(len(r_refs)):
        table = r_refs[s][pl.ds(height, TABLE), pl.ds(0, LANES)].astype(jnp.float32)
        for c in range(chunks):
            ids = jnp.broadcast_to(table[c : c + 1, :], (LANES, LANES)).T
            rows = pl.ds(s * height + c * LANES, LANES)
            ids_ref[rows, :] = ids
            other_ref[rows, :] = jnp.where(ids < 0.0, DEAD, -4.0)
    if first:
        for s, q_ref in enumerate(q_refs):
            behind = pl.ds(qblocks * LANES // parts, TABLE)
            table = q_ref[0][behind, pl.ds(0, LANES)].astype(jnp.float32)
            info_out[s : s + 1, :] = table[0:1, :].astype(jnp.int32)
        copy = pltpu.make_async_copy(info_out, info, info_sem)
        copy.start()
        copy.wait()

    q_count = jnp.int32(0)
    for source in range(4):
        blocks = info[source, qblocks]

        def one_block(block, carry, source=source, q_count=q_count):
            q_list[q_count + block, 0] = source * qblocks + block
            q_list[q_count + block, 1] = info[source, block]
            return carry

        lax.fori_loop(0, blocks, one_block, 0)
        each = qblocks // parts
        for p in range(parts if first else 0):

            def move(block, carry, source=source, q_count=q_count, p=p):
                place = rows_of(q_count + p * each + block)
                qv[place, :] = q_refs[source][p][rows_of(block), :]
                return carry

            lax.fori_loop(0, jnp.clip(blocks - p * each, 0, each), move, 0)
        q_count = q_count + blocks

    factor = LOG2E / math.sqrt(width)
    out_ref[...] = jnp.zeros_like(out_ref) if first else prev_ref[...]

    def query_blocks(group, carry):
        sides = []
        for side in range(wide):
            entry = jnp.minimum(wide * group + side, q_count - 1)
            slot, cluster = q_list[entry, 0], q_list[entry, 1]
            beta = beta_ref[0, cluster]
            sides.append(
                (slot, cluster.astype(jnp.float32), beta * factor, beta * beta * (0.5 * LOG2E))
            )
        accs = [jnp.zeros((8, LANES), jnp.float32) for _ in range(wide)]
        for s, r_ref in enumerate(r_refs):
            tile = r_ref[pl.ds(0, height), :]
            rows = pl.ds(s * height, height)
            for pair in range(wide // 2):
                score = lax.dot_general(
                    tile,
                    qv[rows_of(wide * group + 2 * pair, 2), :],
                    (((1,), (1,)), ((), ())),
                    preferred_element_type=jnp.float32,
                )
                for half in range(2):
                    side = 2 * pair + half
                    _, cluster, scale, offset = sides[side]
                    part = score[:, half * LANES : (half + 1) * LANES]
                    weight = jnp.where(ids_ref[rows, :] == cluster, 0.0, other_ref[rows, :])
                    value = jnp.exp2((part * scale - offset) + weight)
                    accs[side] += jnp.sum(value.reshape(height // 8, 8, LANES), axis=0)
        for side in range(wide):
            total = jnp.sum(accs[side], axis=0, keepdims=True)

            @pl.when(wide * group + side < q_count)
            def _(side=side, total=total):
                row = pl.ds(sides[side][0], 1)
                out_ref[row, :] = out_ref[row, :] + total

        return carry

    lax.fori_loop(0, (q_count + wide - 1) // wide, query_blocks, 0)


def score_call(chunks, qblocks, parts, wide, beta, given, payloads, first):
    width = payloads[0].shape[1]
    slots = 4 * qblocks
    height = chunks * LANES
    totals_shape = jax.ShapeDtypeStruct((slots, LANES), jnp.float32)
    packed_shape = jax.ShapeDtypeStruct((slots * LANES, width), jnp.bfloat16)
    info_shape = jax.ShapeDtypeStruct((8, LANES), jnp.int32)
    spread = pltpu.VMEM((len(payloads) * height, LANES), jnp.float32)
    scratch = [pltpu.SMEM((slots, 2), jnp.int32), spread, spread]
    specs = [VMEM] * (len(given) + len(payloads))
    if first:
        scratch += [pltpu.SMEM((8, LANES), jnp.int32), pltpu.SemaphoreType.DMA]
    else:
        specs[0] = SMEM
    return pl.pallas_call(
        functools.partial(score_kernel, chunks, qblocks, parts, first, wide),
        out_shape=(totals_shape, packed_shape, info_shape) if first else totals_shape,
        in_specs=[SMEM] + specs,
        out_specs=(VMEM, VMEM, VMEM) if first else VMEM,
        scratch_shapes=scratch,
        compiler_params=PARAMS,
        cost_estimate=cost(1, 1),
    )(beta, *given, *payloads)


def per_device(
    queries,
    query_block_cluster,
    block_count,
    references,
    ref_cluster,
    ref_rows,
    cluster_beta,
    cluster_member_count,
):
    nblk, nhelper = lax.axis_size("blk"), lax.axis_size("helper")
    helper = lax.axis_index("helper").astype(jnp.int32)
    qblocks = query_block_cluster.shape[0]
    rows, width = references.shape
    tiles = rows // LANES
    chunks = tiles // nhelper
    sources = nblk // 2

    split = (qblocks // 2, qblocks - qblocks // 2)
    parts = len(split)
    own, *q_own = pl.pallas_call(
        functools.partial(pack_kernel, nhelper),
        out_shape=[jax.ShapeDtypeStruct((chunks * LANES + TABLE, width), jnp.bfloat16)]
        + [
            jax.ShapeDtypeStruct((n * LANES + (TABLE if p == 0 else 0), width), jnp.bfloat16)
            for p, n in enumerate(split)
        ],
        in_specs=[SMEM] + [ANY] * 6,
        out_specs=[ANY] * (1 + parts),
        scratch_shapes=[
            pltpu.VMEM((tiles, LANES), jnp.int32),
            pltpu.SMEM((qblocks,), jnp.int32),
            pltpu.SMEM((1,), jnp.int32),
            pltpu.SMEM((1,), jnp.int32),
            pltpu.VMEM((TABLE, width), jnp.bfloat16),
            pltpu.VMEM((TABLE, width), jnp.bfloat16),
            pltpu.SemaphoreType.DMA((6 + chunks + parts,)),
        ],
        compiler_params=WHOLE,
        cost_estimate=cost(1, 1),
    )(
        helper[None],
        references,
        queries,
        ref_cluster.reshape(tiles, LANES),
        query_block_cluster,
        ref_rows,
        block_count,
    )
    beta = cluster_beta.reshape(1, -1)
    staged_own, *staged_q, beta = staged = pl.pallas_call(
        stage_kernel,
        out_shape=[jax.ShapeDtypeStruct(x.shape, x.dtype) for x in (own, *q_own, beta)],
        in_specs=[VMEM] * (2 + parts),
        out_specs=[VMEM] * (2 + parts),
        compiler_params=PARAMS,
        cost_estimate=cost(1, 1),
    )(own, *q_own, beta)
    q_partner = [swap(q, "blk") for q in q_own]
    q_helper = [swap(q, "helper") for q in q_own]

    above, below = [own], [own]
    for step in range(1, sources // 2 + 1):
        above.append(turn(after(above[-1], *staged) if step > 1 else own, 2))
        if step < (sources + 1) // 2:
            below.append(turn(below[-1], -2))
    early = [staged_own] + above[1:-1] + below[1:]
    q_both = [swap(after(q, above[-2]), "helper") for q in q_partner[:-1]]
    q_both.append(swap(after(q_partner[-1], below[-1]), "helper"))
    all_queries = (*staged_q, *q_helper, *q_partner, *q_both)

    totals, packed, info = score_call(
        chunks, qblocks, parts, 2, beta, all_queries, early, True
    )
    totals = score_call(
        chunks, qblocks, parts, 4, beta, (info, packed, totals), above[-1:], False
    )
    totals = totals.reshape(4, qblocks, LANES)
    total = totals[0] + swap(totals[1], "helper") + swap(totals[2], "blk") + swap_both(totals[3])
    columns = jnp.arange(cluster_member_count.shape[0], dtype=jnp.int32)
    onehot = query_block_cluster[:, None] == columns[None, :]
    sizes = jnp.sum(jnp.where(onehot, cluster_member_count[None, :], 0), axis=1)
    density = jnp.log1p(total / sizes.astype(jnp.float32)[:, None])
    return density.reshape(queries.shape[0])


def solution(mesh):
    in_specs = (
        P(("parts", "blk", "helper"), None),
        P(("parts", "blk", "helper")),
        P(("parts", "blk", "helper")),
        P(("parts", "blk"), None),
        P(("parts", "blk")),
        P(("parts", "blk")),
        P("parts"),
        P("parts"),
    )
    out_specs = P(("parts", "blk", "helper"))
    return jax.shard_map(
        per_device, mesh=mesh, in_specs=in_specs, out_specs=out_specs, check_vma=False
    )
```

```python
import functools
import math

import jax
import jax.numpy as jnp
from jax import lax
from jax.experimental import pallas as pl
from jax.experimental.pallas import tpu as pltpu
from jax.sharding import PartitionSpec as P

LANES = 128
TABLE = 16
LOG2E = 1.4426950408889634
DEAD = -1.0e30
SMEM = pl.BlockSpec(memory_space=pltpu.SMEM)
VMEM = pl.BlockSpec(memory_space=pltpu.VMEM)
ANY = pl.BlockSpec(memory_space=pl.ANY)
WHOLE = pltpu.CompilerParams(vmem_limit_bytes=60 * 1024 * 1024)
PARAMS = pltpu.CompilerParams(vmem_limit_bytes=24 * 1024 * 1024)


def turn(value, by):
    length = lax.axis_size("blk")
    return lax.ppermute(value, "blk", [(i, (i + by) % length) for i in range(length)])


def swap(value, axis):
    length = lax.axis_size(axis)
    return lax.ppermute(value, axis, [(i, i ^ 1) for i in range(length)])


def swap_both(value):
    nblk, nhelper = lax.axis_size("blk"), lax.axis_size("helper")
    pairs = [(i, (i ^ nhelper) ^ 1) for i in range(nblk * nhelper)]
    return lax.ppermute(value, ("blk", "helper"), pairs)


def after(value, *others):
    return lax.optimization_barrier((value, *others))[0]


def cost(flops, moved):
    return pl.CostEstimate(flops=flops, bytes_accessed=moved, transcendentals=0)


def rows_of(index, count=1):
    return pl.ds(pl.multiple_of(index * LANES, LANES), count * LANES)


def pack_kernel(
    nhelper, helper_ref, r_ref, q_ref, ids_ref, clusters_ref, live_ref, count_ref, r_out, *refs
):
    q_outs, (ids, clusters, live, count, sem) = refs[:-5], refs[-5:]
    chunks = ids_ref.shape[0] // nhelper
    qblocks = clusters_ref.shape[0]
    pairs = [(ids_ref, ids), (live_ref, live), (clusters_ref, clusters), (count_ref, count)]
    for c in range(chunks):
        rows = rows_of(helper_ref[0] + nhelper * c)
        pairs.append((r_ref.at[rows], r_out.at[rows_of(c)]))
    start = 0
    for out in q_outs:
        height = out.shape[0] // LANES * LANES
        pairs.append((q_ref.at[pl.ds(start, height)], out.at[pl.ds(0, height)]))
        start += height
    copies = [pltpu.make_async_copy(*pair, sem.at[i]) for i, pair in enumerate(pairs)]
    for copy in copies:
        copy.start()
    for copy in copies[:4]:
        copy.wait()
    lane = lax.broadcasted_iota(jnp.int32, (TABLE, LANES), 1)
    row = lax.broadcasted_iota(jnp.int32, (TABLE, LANES), 0)
    rows = jnp.full((TABLE, LANES), -1, jnp.int32)
    for c in range(chunks):
        tile = helper_ref[0] + nhelper * c
        here = jnp.where(tile * LANES + lane < live[0], ids[pl.ds(tile, 1), :], -1)
        rows = jnp.where(row == c, here, rows)
    r_out[pl.ds(chunks * LANES, TABLE), pl.ds(0, LANES)] = rows.astype(jnp.float32).astype(
        jnp.bfloat16
    )
    rows = jnp.where(lane == qblocks, count[0], 0)
    for k in range(qblocks):
        rows = jnp.where(lane == k, clusters[k], rows)
    q_outs[0][pl.ds(q_outs[0].shape[0] - TABLE, TABLE), pl.ds(0, LANES)] = rows.astype(
        jnp.float32
    ).astype(jnp.bfloat16)
    for copy in copies[4:]:
        copy.wait()


def stage_kernel(*refs):
    half = len(refs) // 2
    for source, out in zip(refs[:half], refs[half:]):
        out[...] = source[...]


def score_kernel(chunks, qblocks, parts, first, wide, beta_ref, *refs):
    if first:
        q_refs = [refs[i : i + parts] for i in range(0, 4 * parts, parts)]
        r_refs, refs = refs[4 * parts : -8], refs[-8:]
        out_ref, qv, info_out, q_list, ids_ref, other_ref, info, info_sem = refs
    else:
        info, qv, prev_ref, *r_refs, out_ref, q_list, ids_ref, other_ref = refs
    width = qv.shape[1]
    height = chunks * LANES

    for s in range(len(r_refs)):
        table = r_refs[s][pl.ds(height, TABLE), pl.ds(0, LANES)].astype(jnp.float32)
        for c in range(chunks):
            ids = jnp.broadcast_to(table[c : c + 1, :], (LANES, LANES)).T
            rows = pl.ds(s * height + c * LANES, LANES)
            ids_ref[rows, :] = ids
            other_ref[rows, :] = jnp.where(ids < 0.0, DEAD, -4.0)
    if first:
        for s, q_ref in enumerate(q_refs):
            behind = pl.ds(qblocks * LANES // parts, TABLE)
            table = q_ref[0][behind, pl.ds(0, LANES)].astype(jnp.float32)
            info_out[s : s + 1, :] = table[0:1, :].astype(jnp.int32)
        copy = pltpu.make_async_copy(info_out, info, info_sem)
        copy.start()
        copy.wait()

    q_count = jnp.int32(0)
    for source in range(4):
        blocks = info[source, qblocks]

        def one_block(block, carry, source=source, q_count=q_count):
            q_list[q_count + block, 0] = source * qblocks + block
            q_list[q_count + block, 1] = info[source, block]
            return carry

        lax.fori_loop(0, blocks, one_block, 0)
        each = qblocks // parts
        for p in range(parts if first else 0):

            def move(block, carry, source=source, q_count=q_count, p=p):
                place = rows_of(q_count + p * each + block)
                qv[place, :] = q_refs[source][p][rows_of(block), :]
                return carry

            lax.fori_loop(0, jnp.clip(blocks - p * each, 0, each), move, 0)
        q_count = q_count + blocks

    factor = LOG2E / math.sqrt(width)
    out_ref[...] = jnp.zeros_like(out_ref) if first else prev_ref[...]

    def query_blocks(group, carry):
        sides = []
        for side in range(wide):
            entry = jnp.minimum(wide * group + side, q_count - 1)
            slot, cluster = q_list[entry, 0], q_list[entry, 1]
            beta = beta_ref[cluster]
            sides.append(
                (slot, cluster.astype(jnp.float32), beta * factor, beta * beta * (0.5 * LOG2E))
            )
        accs = [jnp.zeros((8, LANES), jnp.float32) for _ in range(wide)]
        for s, r_ref in enumerate(r_refs):
            tile = r_ref[pl.ds(0, height), :]
            rows = pl.ds(s * height, height)
            for pair in range(wide // 2):
                score = lax.dot_general(
                    tile,
                    qv[rows_of(wide * group + 2 * pair, 2), :],
                    (((1,), (1,)), ((), ())),
                    preferred_element_type=jnp.float32,
                )
                for half in range(2):
                    side = 2 * pair + half
                    _, cluster, scale, offset = sides[side]
                    part = score[:, half * LANES : (half + 1) * LANES]
                    weight = jnp.where(ids_ref[rows, :] == cluster, 0.0, other_ref[rows, :])
                    value = jnp.exp2((part * scale - offset) + weight)
                    accs[side] += jnp.sum(value.reshape(height // 8, 8, LANES), axis=0)
        for side in range(wide):
            total = jnp.sum(accs[side], axis=0, keepdims=True)

            @pl.when(wide * group + side < q_count)
            def _(side=side, total=total):
                row = pl.ds(sides[side][0], 1)
                out_ref[row, :] = out_ref[row, :] + total

        return carry

    lax.fori_loop(0, (q_count + wide - 1) // wide, query_blocks, 0)


def score_call(chunks, qblocks, parts, wide, beta, given, payloads, first):
    width = payloads[0].shape[1]
    slots = 4 * qblocks
    height = chunks * LANES
    totals_shape = jax.ShapeDtypeStruct((slots, LANES), jnp.float32)
    packed_shape = jax.ShapeDtypeStruct((slots * LANES, width), jnp.bfloat16)
    info_shape = jax.ShapeDtypeStruct((8, LANES), jnp.int32)
    spread = pltpu.VMEM((len(payloads) * height, LANES), jnp.float32)
    scratch = [pltpu.SMEM((slots, 2), jnp.int32), spread, spread]
    specs = [VMEM] * (len(given) + len(payloads))
    if first:
        scratch += [pltpu.SMEM((8, LANES), jnp.int32), pltpu.SemaphoreType.DMA]
    else:
        specs[0] = SMEM
    return pl.pallas_call(
        functools.partial(score_kernel, chunks, qblocks, parts, first, wide),
        out_shape=(totals_shape, packed_shape, info_shape) if first else totals_shape,
        in_specs=[SMEM] + specs,
        out_specs=(VMEM, VMEM, VMEM) if first else VMEM,
        scratch_shapes=scratch,
        compiler_params=PARAMS,
        cost_estimate=cost(1, 1),
    )(beta, *given, *payloads)


def per_device(
    queries,
    query_block_cluster,
    block_count,
    references,
    ref_cluster,
    ref_rows,
    cluster_beta,
    cluster_member_count,
):
    nblk, nhelper = lax.axis_size("blk"), lax.axis_size("helper")
    helper = lax.axis_index("helper").astype(jnp.int32)
    qblocks = query_block_cluster.shape[0]
    rows, width = references.shape
    tiles = rows // LANES
    chunks = tiles // nhelper
    sources = nblk // 2

    split = (qblocks // 2, qblocks - qblocks // 2)
    parts = len(split)
    own, *q_own = pl.pallas_call(
        functools.partial(pack_kernel, nhelper),
        out_shape=[jax.ShapeDtypeStruct((chunks * LANES + TABLE, width), jnp.bfloat16)]
        + [
            jax.ShapeDtypeStruct((n * LANES + (TABLE if p == 0 else 0), width), jnp.bfloat16)
            for p, n in enumerate(split)
        ],
        in_specs=[SMEM] + [ANY] * 6,
        out_specs=[VMEM] * (1 + parts),
        scratch_shapes=[
            pltpu.VMEM((tiles, LANES), jnp.int32),
            pltpu.SMEM((qblocks,), jnp.int32),
            pltpu.SMEM((1,), jnp.int32),
            pltpu.SMEM((1,), jnp.int32),
            pltpu.SemaphoreType.DMA((4 + chunks + parts,)),
        ],
        compiler_params=WHOLE,
        cost_estimate=cost(1, 1),
    )(
        helper[None],
        references,
        queries,
        ref_cluster.reshape(tiles, LANES),
        query_block_cluster,
        ref_rows,
        block_count,
    )
    staged_own, *staged_q = staged = pl.pallas_call(
        stage_kernel,
        out_shape=[jax.ShapeDtypeStruct(x.shape, x.dtype) for x in (own, *q_own)],
        in_specs=[VMEM] * (1 + parts),
        out_specs=[VMEM] * (1 + parts),
        compiler_params=PARAMS,
        cost_estimate=cost(1, 1),
    )(own, *q_own)
    q_partner = [swap(q, "blk") for q in q_own]
    q_helper = [swap(q, "helper") for q in q_own]

    above, below = [own], [own]
    for step in range(1, sources // 2 + 1):
        above.append(turn(after(above[-1], *staged) if step > 1 else own, 2))
        if step < (sources + 1) // 2:
            below.append(turn(below[-1], -2))
    early = [staged_own] + above[1:-1] + below[1:]
    q_both = [swap(after(q, above[-2]), "helper") for q in q_partner[:-1]]
    q_both.append(swap(after(q_partner[-1], below[-1]), "helper"))
    all_queries = (*staged_q, *q_helper, *q_partner, *q_both)

    totals, packed, info = score_call(
        chunks, qblocks, parts, 2, cluster_beta, all_queries, early, True
    )
    totals = score_call(
        chunks, qblocks, parts, 4, cluster_beta, (info, packed, totals), above[-1:], False
    )
    totals = totals.reshape(4, qblocks, LANES)
    total = totals[0] + swap(totals[1], "helper") + swap(totals[2], "blk") + swap_both(totals[3])
    columns = jnp.arange(cluster_member_count.shape[0], dtype=jnp.int32)
    onehot = query_block_cluster[:, None] == columns[None, :]
    sizes = jnp.sum(jnp.where(onehot, cluster_member_count[None, :], 0), axis=1)
    density = jnp.log1p(total / sizes.astype(jnp.float32)[:, None])
    return density.reshape(queries.shape[0])


def solution(mesh):
    in_specs = (
        P(("parts", "blk", "helper"), None),
        P(("parts", "blk", "helper")),
        P(("parts", "blk", "helper")),
        P(("parts", "blk"), None),
        P(("parts", "blk")),
        P(("parts", "blk")),
        P("parts"),
        P("parts"),
    )
    out_specs = P(("parts", "blk", "helper"))
    return jax.shard_map(
        per_device, mesh=mesh, in_specs=in_specs, out_specs=out_specs, check_vma=False
    )
```

```python
import functools
import math

import jax
import jax.numpy as jnp
from jax import lax
from jax.experimental import pallas as pl
from jax.experimental.pallas import tpu as pltpu
from jax.sharding import PartitionSpec as P

LANES = 128
TABLE = 16
LOG2E = 1.4426950408889634
DEAD = -1.0e30
SMEM = pl.BlockSpec(memory_space=pltpu.SMEM)
VMEM = pl.BlockSpec(memory_space=pltpu.VMEM)
ANY = pl.BlockSpec(memory_space=pl.ANY)
WHOLE = pltpu.CompilerParams(vmem_limit_bytes=60 * 1024 * 1024)
PARAMS = pltpu.CompilerParams(vmem_limit_bytes=24 * 1024 * 1024)


def trade(value, mask):
    length = lax.axis_size("blk")
    return lax.ppermute(value, "blk", [(i, i ^ mask) for i in range(length)])


def swap(value, axis):
    length = lax.axis_size(axis)
    return lax.ppermute(value, axis, [(i, i ^ 1) for i in range(length)])


def swap_both(value):
    nblk, nhelper = lax.axis_size("blk"), lax.axis_size("helper")
    pairs = [(i, (i ^ nhelper) ^ 1) for i in range(nblk * nhelper)]
    return lax.ppermute(value, ("blk", "helper"), pairs)


def after(value, *others):
    return lax.optimization_barrier((value, *others))[0]


def cost(flops, moved):
    return pl.CostEstimate(flops=flops, bytes_accessed=moved, transcendentals=0)


def rows_of(index, count=1):
    return pl.ds(pl.multiple_of(index * LANES, LANES), count * LANES)


def pack_kernel(
    nhelper, helper_ref, r_ref, q_ref, ids_ref, clusters_ref, live_ref, count_ref, r_out, *refs
):
    q_outs, (ids, clusters, live, count, sem) = refs[:-5], refs[-5:]
    chunks = ids_ref.shape[0] // nhelper
    qblocks = clusters_ref.shape[0]
    pairs = [(ids_ref, ids), (live_ref, live), (clusters_ref, clusters), (count_ref, count)]
    for c in range(chunks):
        rows = rows_of(helper_ref[0] + nhelper * c)
        pairs.append((r_ref.at[rows], r_out.at[rows_of(c)]))
    start = 0
    for out in q_outs:
        height = out.shape[0] // LANES * LANES
        pairs.append((q_ref.at[pl.ds(start, height)], out.at[pl.ds(0, height)]))
        start += height
    copies = [pltpu.make_async_copy(*pair, sem.at[i]) for i, pair in enumerate(pairs)]
    for copy in copies:
        copy.start()
    for copy in copies[:4]:
        copy.wait()
    lane = lax.broadcasted_iota(jnp.int32, (TABLE, LANES), 1)
    row = lax.broadcasted_iota(jnp.int32, (TABLE, LANES), 0)
    rows = jnp.full((TABLE, LANES), -1, jnp.int32)
    for c in range(chunks):
        tile = helper_ref[0] + nhelper * c
        here = jnp.where(tile * LANES + lane < live[0], ids[pl.ds(tile, 1), :], -1)
        rows = jnp.where(row == c, here, rows)
    r_out[pl.ds(chunks * LANES, TABLE), pl.ds(0, LANES)] = rows.astype(jnp.float32).astype(
        jnp.bfloat16
    )
    rows = jnp.where(lane == qblocks, count[0], 0)
    for k in range(qblocks):
        rows = jnp.where(lane == k, clusters[k], rows)
    q_outs[0][pl.ds(q_outs[0].shape[0] - TABLE, TABLE), pl.ds(0, LANES)] = rows.astype(
        jnp.float32
    ).astype(jnp.bfloat16)
    for copy in copies[4:]:
        copy.wait()


def stage_kernel(*refs):
    half = len(refs) // 2
    for source, out in zip(refs[:half], refs[half:]):
        out[...] = source[...]


def score_kernel(chunks, qblocks, parts, first, wide, beta_ref, *refs):
    if first:
        q_refs = [refs[i : i + parts] for i in range(0, 4 * parts, parts)]
        r_refs, refs = refs[4 * parts : -8], refs[-8:]
        out_ref, qv, info_out, q_list, ids_ref, other_ref, info, info_sem = refs
    else:
        info, qv, prev_ref, *r_refs, out_ref, q_list, ids_ref, other_ref = refs
    width = qv.shape[1]
    height = chunks * LANES

    for s in range(len(r_refs)):
        table = r_refs[s][pl.ds(height, TABLE), pl.ds(0, LANES)].astype(jnp.float32)
        for c in range(chunks):
            ids = jnp.broadcast_to(table[c : c + 1, :], (LANES, LANES)).T
            rows = pl.ds(s * height + c * LANES, LANES)
            ids_ref[rows, :] = ids
            other_ref[rows, :] = jnp.where(ids < 0.0, DEAD, -4.0)
    if first:
        for s, q_ref in enumerate(q_refs):
            behind = pl.ds(qblocks * LANES // parts, TABLE)
            table = q_ref[0][behind, pl.ds(0, LANES)].astype(jnp.float32)
            info_out[s : s + 1, :] = table[0:1, :].astype(jnp.int32)
        copy = pltpu.make_async_copy(info_out, info, info_sem)
        copy.start()
        copy.wait()

    q_count = jnp.int32(0)
    for source in range(4):
        blocks = info[source, qblocks]

        def one_block(block, carry, source=source, q_count=q_count):
            q_list[q_count + block, 0] = source * qblocks + block
            q_list[q_count + block, 1] = info[source, block]
            return carry

        lax.fori_loop(0, blocks, one_block, 0)
        each = qblocks // parts
        for p in range(parts if first else 0):

            def move(block, carry, source=source, q_count=q_count, p=p):
                place = rows_of(q_count + p * each + block)
                qv[place, :] = q_refs[source][p][rows_of(block), :]
                return carry

            lax.fori_loop(0, jnp.clip(blocks - p * each, 0, each), move, 0)
        q_count = q_count + blocks

    factor = LOG2E / math.sqrt(width)
    out_ref[...] = jnp.zeros_like(out_ref) if first else prev_ref[...]

    def query_blocks(group, carry):
        sides = []
        for side in range(wide):
            entry = jnp.minimum(wide * group + side, q_count - 1)
            slot, cluster = q_list[entry, 0], q_list[entry, 1]
            beta = beta_ref[cluster]
            sides.append(
                (slot, cluster.astype(jnp.float32), beta * factor, beta * beta * (0.5 * LOG2E))
            )
        accs = [jnp.zeros((8, LANES), jnp.float32) for _ in range(wide)]
        for s, r_ref in enumerate(r_refs):
            tile = r_ref[pl.ds(0, height), :]
            rows = pl.ds(s * height, height)
            for pair in range(wide // 2):
                score = lax.dot_general(
                    tile,
                    qv[rows_of(wide * group + 2 * pair, 2), :],
                    (((1,), (1,)), ((), ())),
                    preferred_element_type=jnp.float32,
                )
                for half in range(2):
                    side = 2 * pair + half
                    _, cluster, scale, offset = sides[side]
                    part = score[:, half * LANES : (half + 1) * LANES]
                    weight = jnp.where(ids_ref[rows, :] == cluster, 0.0, other_ref[rows, :])
                    value = jnp.exp2((part * scale - offset) + weight)
                    accs[side] += jnp.sum(value.reshape(height // 8, 8, LANES), axis=0)
        for side in range(wide):
            total = jnp.sum(accs[side], axis=0, keepdims=True)

            @pl.when(wide * group + side < q_count)
            def _(side=side, total=total):
                row = pl.ds(sides[side][0], 1)
                out_ref[row, :] = out_ref[row, :] + total

        return carry

    lax.fori_loop(0, (q_count + wide - 1) // wide, query_blocks, 0)


def score_call(chunks, qblocks, parts, wide, beta, given, payloads, first):
    width = payloads[0].shape[1]
    slots = 4 * qblocks
    height = chunks * LANES
    totals_shape = jax.ShapeDtypeStruct((slots, LANES), jnp.float32)
    packed_shape = jax.ShapeDtypeStruct((slots * LANES, width), jnp.bfloat16)
    info_shape = jax.ShapeDtypeStruct((8, LANES), jnp.int32)
    spread = pltpu.VMEM((len(payloads) * height, LANES), jnp.float32)
    scratch = [pltpu.SMEM((slots, 2), jnp.int32), spread, spread]
    specs = [VMEM] * (len(given) + len(payloads))
    if first:
        scratch += [pltpu.SMEM((8, LANES), jnp.int32), pltpu.SemaphoreType.DMA]
    else:
        specs[0] = SMEM
    return pl.pallas_call(
        functools.partial(score_kernel, chunks, qblocks, parts, first, wide),
        out_shape=(totals_shape, packed_shape, info_shape) if first else totals_shape,
        in_specs=[SMEM] + specs,
        out_specs=(VMEM, VMEM, VMEM) if first else VMEM,
        scratch_shapes=scratch,
        compiler_params=PARAMS,
        cost_estimate=cost(1, 1),
    )(beta, *given, *payloads)


def per_device(
    queries,
    query_block_cluster,
    block_count,
    references,
    ref_cluster,
    ref_rows,
    cluster_beta,
    cluster_member_count,
):
    nblk, nhelper = lax.axis_size("blk"), lax.axis_size("helper")
    helper = lax.axis_index("helper").astype(jnp.int32)
    qblocks = query_block_cluster.shape[0]
    rows, width = references.shape
    tiles = rows // LANES
    chunks = tiles // nhelper
    sources = nblk // 2

    split = (qblocks // 2, qblocks - qblocks // 2)
    parts = len(split)
    own, *q_own = pl.pallas_call(
        functools.partial(pack_kernel, nhelper),
        out_shape=[jax.ShapeDtypeStruct((chunks * LANES + TABLE, width), jnp.bfloat16)]
        + [
            jax.ShapeDtypeStruct((n * LANES + (TABLE if p == 0 else 0), width), jnp.bfloat16)
            for p, n in enumerate(split)
        ],
        in_specs=[SMEM] + [ANY] * 6,
        out_specs=[VMEM] * (1 + parts),
        scratch_shapes=[
            pltpu.VMEM((tiles, LANES), jnp.int32),
            pltpu.SMEM((qblocks,), jnp.int32),
            pltpu.SMEM((1,), jnp.int32),
            pltpu.SMEM((1,), jnp.int32),
            pltpu.SemaphoreType.DMA((4 + chunks + parts,)),
        ],
        compiler_params=WHOLE,
        cost_estimate=cost(1, 1),
    )(
        helper[None],
        references,
        queries,
        ref_cluster.reshape(tiles, LANES),
        query_block_cluster,
        ref_rows,
        block_count,
    )
    staged_own, *staged_q = staged = pl.pallas_call(
        stage_kernel,
        out_shape=[jax.ShapeDtypeStruct(x.shape, x.dtype) for x in (own, *q_own)],
        in_specs=[VMEM] * (1 + parts),
        out_specs=[VMEM] * (1 + parts),
        compiler_params=PARAMS,
        cost_estimate=cost(1, 1),
    )(own, *q_own)
    q_partner = [swap(q, "blk") for q in q_own]
    q_helper = [swap(q, "helper") for q in q_own]

    held, mask = [own], sources - 1
    while mask:
        fresh = [trade(after(x, *staged) if x is not own else x, 2 * mask) for x in held]
        held, mask = held + fresh, mask // 2
    early = [staged_own] + held[1:-1]
    q_both = [swap(after(q, held[-3]), "helper") for q in q_partner[:-1]]
    q_both.append(swap(after(q_partner[-1], held[-2]), "helper"))
    all_queries = (*staged_q, *q_helper, *q_partner, *q_both)

    totals, packed, info = score_call(
        chunks, qblocks, parts, 2, cluster_beta, all_queries, early, True
    )
    totals = score_call(
        chunks, qblocks, parts, 4, cluster_beta, (info, packed, totals), held[-1:], False
    )
    totals = totals.reshape(4, qblocks, LANES)
    total = totals[0] + swap(totals[1], "helper") + swap(totals[2], "blk") + swap_both(totals[3])
    columns = jnp.arange(cluster_member_count.shape[0], dtype=jnp.int32)
    onehot = query_block_cluster[:, None] == columns[None, :]
    sizes = jnp.sum(jnp.where(onehot, cluster_member_count[None, :], 0), axis=1)
    density = jnp.log1p(total / sizes.astype(jnp.float32)[:, None])
    return density.reshape(queries.shape[0])


def solution(mesh):
    in_specs = (
        P(("parts", "blk", "helper"), None),
        P(("parts", "blk", "helper")),
        P(("parts", "blk", "helper")),
        P(("parts", "blk"), None),
        P(("parts", "blk")),
        P(("parts", "blk")),
        P("parts"),
        P("parts"),
    )
    out_specs = P(("parts", "blk", "helper"))
    return jax.shard_map(
        per_device, mesh=mesh, in_specs=in_specs, out_specs=out_specs, check_vma=False
    )
```

```python
import functools
import math

import jax
import jax.numpy as jnp
from jax import lax
from jax.experimental import pallas as pl
from jax.experimental.pallas import tpu as pltpu
from jax.sharding import PartitionSpec as P

LANES = 128
LOG2E = 1.4426950408889634
DEAD = -1.0e30
SMEM = pl.BlockSpec(memory_space=pltpu.SMEM)
VMEM = pl.BlockSpec(memory_space=pltpu.VMEM)
PARAMS = pltpu.CompilerParams(vmem_limit_bytes=24 * 1024 * 1024)


def trade(value, mask):
    length = lax.axis_size("blk")
    return lax.ppermute(value, "blk", [(i, i ^ mask) for i in range(length)])


def swap(value, axis):
    length = lax.axis_size(axis)
    return lax.ppermute(value, axis, [(i, i ^ 1) for i in range(length)])


def swap_both(value):
    nblk, nhelper = lax.axis_size("blk"), lax.axis_size("helper")
    pairs = [(i, (i ^ nhelper) ^ 1) for i in range(nblk * nhelper)]
    return lax.ppermute(value, ("blk", "helper"), pairs)


def after(value, *others):
    return lax.optimization_barrier((value, *others))[0]


def cost(flops, moved):
    return pl.CostEstimate(flops=flops, bytes_accessed=moved, transcendentals=0)


def rows_of(index, count=1):
    return pl.ds(pl.multiple_of(index * LANES, LANES), count * LANES)


def table_kernel(
    nhelper, helper_ref, clusters_ref, count_ref, live_ref, ids_ref, out_ref
):
    lane = lax.broadcasted_iota(jnp.int32, (1, LANES), 1)
    chunks = ids_ref.shape[0] // nhelper
    out_ref[...] = jnp.zeros_like(out_ref)
    for c in range(chunks):
        tile = helper_ref[0] + nhelper * c
        ids = ids_ref[pl.ds(tile, 1), :]
        out_ref[c : c + 1, :] = jnp.where(tile * LANES + lane < live_ref[0], ids, -1)
    qblocks = clusters_ref.shape[0]
    row = jnp.where(lane == qblocks, count_ref[0], 0)
    for k in range(qblocks):
        row = jnp.where(lane == k, clusters_ref[k], row)
    out_ref[chunks : chunks + 1, :] = row


def stage_kernel(*refs):
    half = len(refs) // 2
    for source, out in zip(refs[:half], refs[half:]):
        out[...] = source[...]


def score_kernel(chunks, qblocks, first, wide, beta_ref, *refs):
    if first:
        (*given, out_ref, qv, info_out, q_list, ids_ref, other_ref, info, info_sem) = refs
        q_refs, t_refs, given = given[:4], given[4:8], given[8:]
    else:
        (info, qv, prev_ref, *given, out_ref, q_list, ids_ref, other_ref) = refs
    r_refs, i_refs = given[: len(given) // 2], given[len(given) // 2 :]
    width = qv.shape[1]
    height = chunks * LANES
    if first:
        for s, t_ref in enumerate(t_refs):
            info_out[s : s + 1, :] = t_ref[chunks : chunks + 1, :]
        copy = pltpu.make_async_copy(info_out, info, info_sem)
        copy.start()

    for s, i_ref in enumerate(i_refs):
        for c in range(chunks):
            ids = i_ref[c : c + 1, :].astype(jnp.float32)
            ids = jnp.broadcast_to(ids, (LANES, LANES)).T
            rows = pl.ds(s * height + c * LANES, LANES)
            ids_ref[rows, :] = ids
            other_ref[rows, :] = jnp.where(ids < 0.0, DEAD, -4.0)
    if first:
        copy.wait()

    q_count = jnp.int32(0)
    for source in range(4):
        blocks = info[source, qblocks]

        def one_block(block, carry, source=source, q_count=q_count):
            if first:
                qv[rows_of(q_count + block), :] = q_refs[source][rows_of(block), :]
            q_list[q_count + block, 0] = source * qblocks + block
            q_list[q_count + block, 1] = info[source, block]
            return carry

        lax.fori_loop(0, blocks, one_block, 0)
        q_count = q_count + blocks

    factor = LOG2E / math.sqrt(width)
    out_ref[...] = jnp.zeros_like(out_ref) if first else prev_ref[...]

    def query_blocks(group, carry):
        sides = []
        for side in range(wide):
            entry = jnp.minimum(wide * group + side, q_count - 1)
            slot, cluster = q_list[entry, 0], q_list[entry, 1]
            beta = beta_ref[cluster]
            sides.append(
                (slot, cluster.astype(jnp.float32), beta * factor, beta * beta * (0.5 * LOG2E))
            )
        accs = [jnp.zeros((8, LANES), jnp.float32) for _ in range(wide)]
        for s, r_ref in enumerate(r_refs):
            tile = r_ref[pl.ds(0, height), :]
            rows = pl.ds(s * height, height)
            for pair in range(wide // 2):
                score = lax.dot_general(
                    tile,
                    qv[rows_of(wide * group + 2 * pair, 2), :],
                    (((1,), (1,)), ((), ())),
                    preferred_element_type=jnp.float32,
                )
                for half in range(2):
                    side = 2 * pair + half
                    _, cluster, scale, offset = sides[side]
                    part = score[:, half * LANES : (half + 1) * LANES]
                    weight = jnp.where(ids_ref[rows, :] == cluster, 0.0, other_ref[rows, :])
                    value = jnp.exp2((part * scale - offset) + weight)
                    accs[side] += jnp.sum(value.reshape(height // 8, 8, LANES), axis=0)
        for side in range(wide):
            total = jnp.sum(accs[side], axis=0, keepdims=True)

            @pl.when(wide * group + side < q_count)
            def _(side=side, total=total):
                row = pl.ds(sides[side][0], 1)
                out_ref[row, :] = out_ref[row, :] + total

        return carry

    lax.fori_loop(0, (q_count + wide - 1) // wide, query_blocks, 0)


def score_call(chunks, qblocks, wide, beta, given, payloads, tables, first):
    width = payloads[0].shape[1]
    slots = 4 * qblocks
    height = chunks * LANES
    totals_shape = jax.ShapeDtypeStruct((slots, LANES), jnp.float32)
    packed_shape = jax.ShapeDtypeStruct((slots * LANES, width), jnp.bfloat16)
    info_shape = jax.ShapeDtypeStruct((8, LANES), jnp.int32)
    spread = pltpu.VMEM((len(payloads) * height, LANES), jnp.float32)
    scratch = [pltpu.SMEM((slots, 2), jnp.int32), spread, spread]
    specs = [VMEM] * (len(given) + len(payloads) + len(tables))
    if first:
        scratch += [pltpu.SMEM((8, LANES), jnp.int32), pltpu.SemaphoreType.DMA]
    else:
        specs[0] = SMEM
    return pl.pallas_call(
        functools.partial(score_kernel, chunks, qblocks, first, wide),
        out_shape=(totals_shape, packed_shape, info_shape) if first else totals_shape,
        in_specs=[SMEM] + specs,
        out_specs=(VMEM, VMEM, VMEM) if first else VMEM,
        scratch_shapes=scratch,
        compiler_params=PARAMS,
        cost_estimate=cost(1, 1),
    )(beta, *given, *payloads, *tables)


def per_device(
    queries,
    query_block_cluster,
    block_count,
    references,
    ref_cluster,
    ref_rows,
    cluster_beta,
    cluster_member_count,
):
    nblk, nhelper = lax.axis_size("blk"), lax.axis_size("helper")
    helper = lax.axis_index("helper").astype(jnp.int32)
    qblocks = query_block_cluster.shape[0]
    rows, width = references.shape
    tiles = rows // LANES
    chunks = tiles // nhelper
    sources = nblk // 2

    q_partner = swap(queries, "blk")
    by_chunk = references.reshape(chunks, nhelper, LANES, width)
    own = lax.dynamic_index_in_dim(by_chunk, helper, 1, keepdims=False)
    own = own.reshape(chunks * LANES, width)

    held, masks, mask = [own], [0], sources - 1
    while mask:
        held = held + [trade(x, 2 * mask) for x in held]
        masks, mask = masks + [m ^ mask for m in masks], mask // 2
    q_helper = swap(queries, "helper")

    table = pl.pallas_call(
        functools.partial(table_kernel, nhelper),
        out_shape=jax.ShapeDtypeStruct((8 * ((chunks + 8) // 8), LANES), jnp.int32),
        in_specs=[SMEM] * 4 + [VMEM],
        out_specs=VMEM,
        compiler_params=PARAMS,
        cost_estimate=cost(1, 1),
    )(
        helper[None],
        after(query_block_cluster, own),
        block_count,
        ref_rows,
        ref_cluster.reshape(tiles, LANES),
    )
    r_tables = [table] + [trade(table, 2 * m) for m in masks[1:]]
    q_tables = [table, swap(table, "helper"), swap(table, "blk"), swap_both(table)]
    staged = pl.pallas_call(
        stage_kernel,
        out_shape=jax.ShapeDtypeStruct(queries.shape, queries.dtype),
        in_specs=[VMEM],
        out_specs=VMEM,
        compiler_params=PARAMS,
        cost_estimate=cost(1, 1),
    )(queries)
    q_both = swap(after(q_partner, staged, *held[1:-1], *r_tables, *q_tables), "helper")

    totals, packed, info = score_call(
        chunks,
        qblocks,
        2,
        cluster_beta,
        (staged, q_helper, q_partner, q_both, *q_tables),
        held[:-1],
        r_tables[:-1],
        True,
    )
    totals = score_call(
        chunks,
        qblocks,
        4,
        cluster_beta,
        (info, packed, totals),
        held[-1:],
        r_tables[-1:],
        False,
    )
    totals = totals.reshape(4, qblocks, LANES)
    total = totals[0] + swap(totals[1], "helper") + swap(totals[2], "blk") + swap_both(totals[3])
    columns = jnp.arange(cluster_member_count.shape[0], dtype=jnp.int32)
    onehot = query_block_cluster[:, None] == columns[None, :]
    sizes = jnp.sum(jnp.where(onehot, cluster_member_count[None, :], 0), axis=1)
    density = jnp.log1p(total / sizes.astype(jnp.float32)[:, None])
    return density.reshape(queries.shape[0])


def solution(mesh):
    in_specs = (
        P(("parts", "blk", "helper"), None),
        P(("parts", "blk", "helper")),
        P(("parts", "blk", "helper")),
        P(("parts", "blk"), None),
        P(("parts", "blk")),
        P(("parts", "blk")),
        P("parts"),
        P("parts"),
    )
    out_specs = P(("parts", "blk", "helper"))
    return jax.shard_map(
        per_device, mesh=mesh, in_specs=in_specs, out_specs=out_specs, check_vma=False
    )
```

```python
import functools
import math

import jax
import jax.numpy as jnp
from jax import lax
from jax.experimental import pallas as pl
from jax.experimental.pallas import tpu as pltpu
from jax.sharding import PartitionSpec as P

LANES = 128
TABLE = 16
LOG2E = 1.4426950408889634
DEAD = -1.0e30
SMEM = pl.BlockSpec(memory_space=pltpu.SMEM)
VMEM = pl.BlockSpec(memory_space=pltpu.VMEM)
PARAMS = pltpu.CompilerParams(vmem_limit_bytes=24 * 1024 * 1024)


def trade(value, mask):
    length = lax.axis_size("blk")
    return lax.ppermute(value, "blk", [(i, i ^ mask) for i in range(length)])


def swap(value, axis):
    length = lax.axis_size(axis)
    return lax.ppermute(value, axis, [(i, i ^ 1) for i in range(length)])


def swap_both(value):
    nblk, nhelper = lax.axis_size("blk"), lax.axis_size("helper")
    pairs = [(i, (i ^ nhelper) ^ 1) for i in range(nblk * nhelper)]
    return lax.ppermute(value, ("blk", "helper"), pairs)


def after(value, *others):
    return lax.optimization_barrier((value, *others))[0]


def cost(flops, moved):
    return pl.CostEstimate(flops=flops, bytes_accessed=moved, transcendentals=0)


def rows_of(index, count=1):
    return pl.ds(pl.multiple_of(index * LANES, LANES), count * LANES)


def pack_kernel(nhelper, helper_ref, live_ref, ids_ref, r_ref, out_ref):
    lane = lax.broadcasted_iota(jnp.int32, (TABLE, LANES), 1)
    row = lax.broadcasted_iota(jnp.int32, (TABLE, LANES), 0)
    table = jnp.full((TABLE, LANES), -1, jnp.int32)
    height = r_ref.shape[0]
    for c in range(height // LANES):
        tile = helper_ref[0] + nhelper * c
        ids = ids_ref[pl.ds(tile, 1), :]
        table = jnp.where(row == c, jnp.where(tile * LANES + lane < live_ref[0], ids, -1), table)
    out_ref[pl.ds(0, height), :] = r_ref[...]
    out_ref[pl.ds(height, TABLE), pl.ds(0, LANES)] = table.astype(jnp.float32).astype(jnp.bfloat16)


def table_kernel(clusters_ref, count_ref, out_ref):
    lane = lax.broadcasted_iota(jnp.int32, out_ref.shape, 1)
    qblocks = clusters_ref.shape[0]
    row = jnp.where(lane == qblocks, count_ref[0], 0)
    for k in range(qblocks):
        row = jnp.where(lane == k, clusters_ref[k], row)
    out_ref[...] = row


def stage_kernel(*refs):
    half = len(refs) // 2
    for source, out in zip(refs[:half], refs[half:]):
        out[...] = source[...]


def score_kernel(chunks, qblocks, first, wide, beta_ref, *refs):
    if first:
        (*given, out_ref, qv, info_out, q_list, ids_ref, other_ref, info, info_sem) = refs
        q_refs, t_refs, r_refs = given[:4], given[4:8], given[8:]
    else:
        (info, qv, prev_ref, *r_refs, out_ref, q_list, ids_ref, other_ref) = refs
    width = qv.shape[1]
    height = chunks * LANES
    if first:
        for s, t_ref in enumerate(t_refs):
            info_out[s : s + 1, :] = t_ref[0:1, :]
        copy = pltpu.make_async_copy(info_out, info, info_sem)
        copy.start()

    for s, r_ref in enumerate(r_refs):
        table = r_ref[pl.ds(height, TABLE), pl.ds(0, LANES)].astype(jnp.float32)
        for c in range(chunks):
            ids = jnp.broadcast_to(table[c : c + 1, :], (LANES, LANES)).T
            rows = pl.ds(s * height + c * LANES, LANES)
            ids_ref[rows, :] = ids
            other_ref[rows, :] = jnp.where(ids < 0.0, DEAD, -4.0)
    if first:
        copy.wait()

    q_count = jnp.int32(0)
    for source in range(4):
        blocks = info[source, qblocks]

        def one_block(block, carry, source=source, q_count=q_count):
            if first:
                qv[rows_of(q_count + block), :] = q_refs[source][rows_of(block), :]
            q_list[q_count + block, 0] = source * qblocks + block
            q_list[q_count + block, 1] = info[source, block]
            return carry

        lax.fori_loop(0, blocks, one_block, 0)
        q_count = q_count + blocks

    factor = LOG2E / math.sqrt(width)
    out_ref[...] = jnp.zeros_like(out_ref) if first else prev_ref[...]

    def query_blocks(group, carry):
        sides = []
        for side in range(wide):
            entry = jnp.minimum(wide * group + side, q_count - 1)
            slot, cluster = q_list[entry, 0], q_list[entry, 1]
            beta = beta_ref[cluster]
            sides.append(
                (slot, cluster.astype(jnp.float32), beta * factor, beta * beta * (0.5 * LOG2E))
            )
        accs = [jnp.zeros((8, LANES), jnp.float32) for _ in range(wide)]
        for s, r_ref in enumerate(r_refs):
            tile = r_ref[pl.ds(0, height), :]
            rows = pl.ds(s * height, height)
            for pair in range(wide // 2):
                score = lax.dot_general(
                    tile,
                    qv[rows_of(wide * group + 2 * pair, 2), :],
                    (((1,), (1,)), ((), ())),
                    preferred_element_type=jnp.float32,
                )
                for half in range(2):
                    side = 2 * pair + half
                    _, cluster, scale, offset = sides[side]
                    part = score[:, half * LANES : (half + 1) * LANES]
                    weight = jnp.where(ids_ref[rows, :] == cluster, 0.0, other_ref[rows, :])
                    value = jnp.exp2((part * scale - offset) + weight)
                    accs[side] += jnp.sum(value.reshape(height // 8, 8, LANES), axis=0)
        for side in range(wide):
            total = jnp.sum(accs[side], axis=0, keepdims=True)

            @pl.when(wide * group + side < q_count)
            def _(side=side, total=total):
                row = pl.ds(sides[side][0], 1)
                out_ref[row, :] = out_ref[row, :] + total

        return carry

    lax.fori_loop(0, (q_count + wide - 1) // wide, query_blocks, 0)


def score_call(chunks, qblocks, wide, beta, given, payloads, first):
    width = payloads[0].shape[1]
    slots = 4 * qblocks
    height = chunks * LANES
    totals_shape = jax.ShapeDtypeStruct((slots, LANES), jnp.float32)
    packed_shape = jax.ShapeDtypeStruct((slots * LANES, width), jnp.bfloat16)
    info_shape = jax.ShapeDtypeStruct((8, LANES), jnp.int32)
    spread = pltpu.VMEM((len(payloads) * height, LANES), jnp.float32)
    scratch = [pltpu.SMEM((slots, 2), jnp.int32), spread, spread]
    specs = [VMEM] * (len(given) + len(payloads))
    if first:
        scratch += [pltpu.SMEM((8, LANES), jnp.int32), pltpu.SemaphoreType.DMA]
    else:
        specs[0] = SMEM
    return pl.pallas_call(
        functools.partial(score_kernel, chunks, qblocks, first, wide),
        out_shape=(totals_shape, packed_shape, info_shape) if first else totals_shape,
        in_specs=[SMEM] + specs,
        out_specs=(VMEM, VMEM, VMEM) if first else VMEM,
        scratch_shapes=scratch,
        compiler_params=PARAMS,
        cost_estimate=cost(1, 1),
    )(beta, *given, *payloads)


def per_device(
    queries,
    query_block_cluster,
    block_count,
    references,
    ref_cluster,
    ref_rows,
    cluster_beta,
    cluster_member_count,
):
    nblk, nhelper = lax.axis_size("blk"), lax.axis_size("helper")
    helper = lax.axis_index("helper").astype(jnp.int32)
    qblocks = query_block_cluster.shape[0]
    rows, width = references.shape
    tiles = rows // LANES
    chunks = tiles // nhelper
    sources = nblk // 2

    q_partner = swap(queries, "blk")
    by_chunk = references.reshape(chunks, nhelper, LANES, width)
    own = lax.dynamic_index_in_dim(by_chunk, helper, 1, keepdims=False)
    own = pl.pallas_call(
        functools.partial(pack_kernel, nhelper),
        out_shape=jax.ShapeDtypeStruct((chunks * LANES + TABLE, width), jnp.bfloat16),
        in_specs=[SMEM] * 2 + [VMEM] * 2,
        out_specs=VMEM,
        compiler_params=PARAMS,
        cost_estimate=cost(1, 1),
    )(
        helper[None],
        ref_rows,
        ref_cluster.reshape(tiles, LANES),
        own.reshape(chunks * LANES, width),
    )

    held, mask = [own], sources - 1
    while mask:
        held = held + [trade(x, 2 * mask) for x in held]
        mask //= 2
    q_helper = swap(queries, "helper")

    table = pl.pallas_call(
        table_kernel,
        out_shape=jax.ShapeDtypeStruct((8, LANES), jnp.int32),
        in_specs=[SMEM] * 2,
        out_specs=VMEM,
        compiler_params=PARAMS,
        cost_estimate=cost(1, 1),
    )(after(query_block_cluster, own), block_count)
    q_tables = (table, swap(table, "helper"), swap(table, "blk"), swap_both(table))
    staged = pl.pallas_call(
        stage_kernel,
        out_shape=jax.ShapeDtypeStruct(queries.shape, queries.dtype),
        in_specs=[VMEM],
        out_specs=VMEM,
        compiler_params=PARAMS,
        cost_estimate=cost(1, 1),
    )(queries)
    q_both = swap(after(q_partner, staged, *held[1:-1], *q_tables), "helper")

    totals, packed, info = score_call(
        chunks,
        qblocks,
        2,
        cluster_beta,
        (staged, q_helper, q_partner, q_both, *q_tables),
        held[:-1],
        True,
    )
    totals = score_call(
        chunks,
        qblocks,
        4,
        cluster_beta,
        (info, packed, totals),
        held[-1:],
        False,
    )
    totals = totals.reshape(4, qblocks, LANES)
    total = totals[0] + swap(totals[1], "helper") + swap(totals[2], "blk") + swap_both(totals[3])
    columns = jnp.arange(cluster_member_count.shape[0], dtype=jnp.int32)
    onehot = query_block_cluster[:, None] == columns[None, :]
    sizes = jnp.sum(jnp.where(onehot, cluster_member_count[None, :], 0), axis=1)
    density = jnp.log1p(total / sizes.astype(jnp.float32)[:, None])
    return density.reshape(queries.shape[0])


def solution(mesh):
    in_specs = (
        P(("parts", "blk", "helper"), None),
        P(("parts", "blk", "helper")),
        P(("parts", "blk", "helper")),
        P(("parts", "blk"), None),
        P(("parts", "blk")),
        P(("parts", "blk")),
        P("parts"),
        P("parts"),
    )
    out_specs = P(("parts", "blk", "helper"))
    return jax.shard_map(
        per_device, mesh=mesh, in_specs=in_specs, out_specs=out_specs, check_vma=False
    )
```

```python
import functools
import math

import jax
import jax.numpy as jnp
from jax import lax
from jax.experimental import pallas as pl
from jax.experimental.pallas import tpu as pltpu
from jax.sharding import PartitionSpec as P

LANES = 128
TABLE = 8
LOG2E = 1.4426950408889634
DEAD = -1.0e30
SMEM = pl.BlockSpec(memory_space=pltpu.SMEM)
VMEM = pl.BlockSpec(memory_space=pltpu.VMEM)
PARAMS = pltpu.CompilerParams(vmem_limit_bytes=24 * 1024 * 1024)


def trade(value, mask):
    length = lax.axis_size("blk")
    return lax.ppermute(value, "blk", [(i, i ^ mask) for i in range(length)])


def swap(value, axis):
    length = lax.axis_size(axis)
    return lax.ppermute(value, axis, [(i, i ^ 1) for i in range(length)])


def swap_both(value):
    nblk, nhelper = lax.axis_size("blk"), lax.axis_size("helper")
    pairs = [(i, (i ^ nhelper) ^ 1) for i in range(nblk * nhelper)]
    return lax.ppermute(value, ("blk", "helper"), pairs)


def after(value, *others):
    return lax.optimization_barrier((value, *others))[0]


def cost(flops, moved):
    return pl.CostEstimate(flops=flops, bytes_accessed=moved, transcendentals=0)


def rows_of(index, count=1):
    return pl.ds(pl.multiple_of(index * LANES, LANES), count * LANES)


def pack_kernel(nhelper, helper_ref, live_ref, ids_ref, r_ref, out_ref):
    lane = lax.broadcasted_iota(jnp.int32, (TABLE, LANES), 1)
    row = lax.broadcasted_iota(jnp.int32, (TABLE, LANES), 0)
    table = jnp.full((TABLE, LANES), -1, jnp.int32)
    height = r_ref.shape[0]
    for c in range(height // LANES):
        tile = helper_ref[0] + nhelper * c
        ids = ids_ref[pl.ds(tile, 1), :]
        table = jnp.where(row == c, jnp.where(tile * LANES + lane < live_ref[0], ids, -1), table)
    out_ref[pl.ds(0, height), :] = r_ref[...]
    out_ref[pl.ds(height, TABLE), pl.ds(0, LANES)] = table.astype(jnp.float32).astype(jnp.bfloat16)


def table_kernel(clusters_ref, count_ref, out_ref):
    lane = lax.broadcasted_iota(jnp.int32, out_ref.shape, 1)
    qblocks = clusters_ref.shape[0]
    row = jnp.where(lane == qblocks, count_ref[0], 0)
    for k in range(qblocks):
        row = jnp.where(lane == k, clusters_ref[k], row)
    out_ref[...] = row


def stage_kernel(*refs):
    half = len(refs) // 2
    for source, out in zip(refs[:half], refs[half:]):
        out[...] = source[...]


def score_kernel(chunks, qblocks, pieces, first, wide, beta_ref, *refs):
    if first:
        (*given, out_ref, qv, info_out, q_list, ids_ref, other_ref, info, info_sem) = refs
        q_refs = []
        for n in pieces:
            q_refs.append(given[:n])
            given = given[n:]
        t_refs, r_refs = given[:4], given[4:]
    else:
        (info, qv, prev_ref, *r_refs, out_ref, q_list, ids_ref, other_ref) = refs
    width = qv.shape[0]
    height = chunks * LANES
    if first:
        for s, t_ref in enumerate(t_refs):
            info_out[s : s + 1, :] = t_ref[0:1, :]
        copy = pltpu.make_async_copy(info_out, info, info_sem)
        copy.start()

    for s, r_ref in enumerate(r_refs):
        table = r_ref[pl.ds(height, TABLE), pl.ds(0, LANES)].astype(jnp.float32)
        for c in range(chunks):
            ids = jnp.broadcast_to(table[c : c + 1, :], (LANES, LANES)).T
            rows = pl.ds(s * height + c * LANES, LANES)
            ids_ref[rows, :] = ids
            other_ref[rows, :] = jnp.where(ids < 0.0, DEAD, -4.0)
    if first:
        copy.wait()

    q_count = jnp.int32(0)
    for source in range(4):
        blocks = info[source, qblocks]

        def one_block(block, carry, source=source, q_count=q_count):
            q_list[q_count + block, 0] = source * qblocks + block
            q_list[q_count + block, 1] = info[source, block]
            return carry

        lax.fori_loop(0, blocks, one_block, 0)
        start = 0
        for piece in q_refs[source] if first else ():
            each = piece.shape[0] // LANES

            def move(block, carry, place=q_count + start, piece=piece):
                qv[:, rows_of(place + block)] = piece[rows_of(block), :].T
                return carry

            lax.fori_loop(0, jnp.clip(blocks - start, 0, each), move, 0)
            start += each
        q_count = q_count + blocks

    factor = LOG2E / math.sqrt(width)
    out_ref[...] = jnp.zeros_like(out_ref) if first else prev_ref[...]

    def query_blocks(group, carry):
        sides = []
        for side in range(wide):
            entry = jnp.minimum(wide * group + side, q_count - 1)
            slot, cluster = q_list[entry, 0], q_list[entry, 1]
            beta = beta_ref[cluster]
            sides.append(
                (slot, cluster.astype(jnp.float32), beta * factor, beta * beta * (0.5 * LOG2E))
            )
        accs = [jnp.zeros((8, LANES), jnp.float32) for _ in range(wide)]
        for s, r_ref in enumerate(r_refs):
            tile = r_ref[pl.ds(0, height), :]
            rows = pl.ds(s * height, height)
            for pair in range(wide // 2):
                score = lax.dot_general(
                    tile,
                    qv[:, rows_of(wide * group + 2 * pair, 2)],
                    (((1,), (0,)), ((), ())),
                    preferred_element_type=jnp.float32,
                )
                for half in range(2):
                    side = 2 * pair + half
                    _, cluster, scale, offset = sides[side]
                    part = score[:, half * LANES : (half + 1) * LANES]
                    weight = jnp.where(ids_ref[rows, :] == cluster, 0.0, other_ref[rows, :])
                    value = jnp.exp2((part * scale - offset) + weight)
                    accs[side] += jnp.sum(value.reshape(height // 8, 8, LANES), axis=0)
        for side in range(wide):
            total = jnp.sum(accs[side], axis=0, keepdims=True)

            @pl.when(wide * group + side < q_count)
            def _(side=side, total=total):
                row = pl.ds(sides[side][0], 1)
                out_ref[row, :] = out_ref[row, :] + total

        return carry

    lax.fori_loop(0, (q_count + wide - 1) // wide, query_blocks, 0)


def score_call(chunks, qblocks, pieces, wide, beta, given, payloads, first):
    width = payloads[0].shape[1]
    slots = 4 * qblocks
    height = chunks * LANES
    totals_shape = jax.ShapeDtypeStruct((slots, LANES), jnp.float32)
    packed_shape = jax.ShapeDtypeStruct((width, slots * LANES), jnp.bfloat16)
    info_shape = jax.ShapeDtypeStruct((8, LANES), jnp.int32)
    spread = pltpu.VMEM((len(payloads) * height, LANES), jnp.float32)
    scratch = [pltpu.SMEM((slots, 2), jnp.int32), spread, spread]
    specs = [VMEM] * (len(given) + len(payloads))
    if first:
        scratch += [pltpu.SMEM((8, LANES), jnp.int32), pltpu.SemaphoreType.DMA]
    else:
        specs[0] = SMEM
    return pl.pallas_call(
        functools.partial(score_kernel, chunks, qblocks, pieces, first, wide),
        out_shape=(totals_shape, packed_shape, info_shape) if first else totals_shape,
        in_specs=[SMEM] + specs,
        out_specs=(VMEM, VMEM, VMEM) if first else VMEM,
        scratch_shapes=scratch,
        compiler_params=PARAMS,
        cost_estimate=cost(1, 1),
    )(beta, *given, *payloads)


def per_device(
    queries,
    query_block_cluster,
    block_count,
    references,
    ref_cluster,
    ref_rows,
    cluster_beta,
    cluster_member_count,
):
    nblk, nhelper = lax.axis_size("blk"), lax.axis_size("helper")
    helper = lax.axis_index("helper").astype(jnp.int32)
    qblocks = query_block_cluster.shape[0]
    rows, width = references.shape
    tiles = rows // LANES
    chunks = tiles // nhelper
    sources = nblk // 2

    q_partner = swap(queries, "blk")
    by_chunk = references.reshape(chunks, nhelper, LANES, width)
    own = lax.dynamic_index_in_dim(by_chunk, helper, 1, keepdims=False)
    own = pl.pallas_call(
        functools.partial(pack_kernel, nhelper),
        out_shape=jax.ShapeDtypeStruct((chunks * LANES + TABLE, width), jnp.bfloat16),
        in_specs=[SMEM] * 2 + [VMEM] * 2,
        out_specs=VMEM,
        compiler_params=PARAMS,
        cost_estimate=cost(1, 1),
    )(
        helper[None],
        ref_rows,
        ref_cluster.reshape(tiles, LANES),
        own.reshape(chunks * LANES, width),
    )

    held, mask = [own], sources - 1
    while mask:
        held = held + [trade(x, 2 * mask) for x in held]
        mask //= 2
    q_helper = swap(queries, "helper")

    table = pl.pallas_call(
        table_kernel,
        out_shape=jax.ShapeDtypeStruct((8, LANES), jnp.int32),
        in_specs=[SMEM] * 2,
        out_specs=VMEM,
        compiler_params=PARAMS,
        cost_estimate=cost(1, 1),
    )(after(query_block_cluster, own), block_count)
    q_tables = (table, swap(table, "helper"), swap(table, "blk"), swap_both(table))
    staged = pl.pallas_call(
        stage_kernel,
        out_shape=jax.ShapeDtypeStruct(queries.shape, queries.dtype),
        in_specs=[VMEM],
        out_specs=VMEM,
        compiler_params=PARAMS,
        cost_estimate=cost(1, 1),
    )(queries)
    q_partner = after(q_partner, staged, *held[1:-1], *q_tables)
    half = qblocks // 2 * LANES
    q_both = [swap(q_partner[:half], "helper"), swap(q_partner[half:], "helper")]
    queries = (staged, q_helper, q_partner, *q_both)
    pieces = (1, 1, 1, 2)

    totals, packed, info = score_call(
        chunks,
        qblocks,
        pieces,
        2,
        cluster_beta,
        (*queries, *q_tables),
        held[:-1],
        True,
    )
    totals = score_call(
        chunks,
        qblocks,
        pieces,
        4,
        cluster_beta,
        (info, packed, totals),
        held[-1:],
        False,
    )
    totals = totals.reshape(4, qblocks, LANES)
    total = totals[0] + swap(totals[1], "helper") + swap(totals[2], "blk") + swap_both(totals[3])
    columns = jnp.arange(cluster_member_count.shape[0], dtype=jnp.int32)
    onehot = query_block_cluster[:, None] == columns[None, :]
    sizes = jnp.sum(jnp.where(onehot, cluster_member_count[None, :], 0), axis=1)
    density = jnp.log1p(total / sizes.astype(jnp.float32)[:, None])
    return density.reshape(qblocks * LANES)


def solution(mesh):
    in_specs = (
        P(("parts", "blk", "helper"), None),
        P(("parts", "blk", "helper")),
        P(("parts", "blk", "helper")),
        P(("parts", "blk"), None),
        P(("parts", "blk")),
        P(("parts", "blk")),
        P("parts"),
        P("parts"),
    )
    out_specs = P(("parts", "blk", "helper"))
    return jax.shard_map(
        per_device, mesh=mesh, in_specs=in_specs, out_specs=out_specs, check_vma=False
    )
```

```python
import functools
import math

import jax
import jax.numpy as jnp
from jax import lax
from jax.experimental import pallas as pl
from jax.experimental.pallas import tpu as pltpu
from jax.sharding import PartitionSpec as P

LANES = 128
TABLE = 8
LOG2E = 1.4426950408889634
DEAD = -1.0e30
SMEM = pl.BlockSpec(memory_space=pltpu.SMEM)
VMEM = pl.BlockSpec(memory_space=pltpu.VMEM)
PARAMS = pltpu.CompilerParams(vmem_limit_bytes=24 * 1024 * 1024)


def trade(value, mask):
    length = lax.axis_size("blk")
    return lax.ppermute(value, "blk", [(i, i ^ mask) for i in range(length)])


def swap(value, axis):
    length = lax.axis_size(axis)
    return lax.ppermute(value, axis, [(i, i ^ 1) for i in range(length)])


def swap_both(value):
    nblk, nhelper = lax.axis_size("blk"), lax.axis_size("helper")
    pairs = [(i, (i ^ nhelper) ^ 1) for i in range(nblk * nhelper)]
    return lax.ppermute(value, ("blk", "helper"), pairs)


def after(value, *others):
    return lax.optimization_barrier((value, *others))[0]


def cost(flops, moved):
    return pl.CostEstimate(flops=flops, bytes_accessed=moved, transcendentals=0)


def rows_of(index, count=1):
    return pl.ds(pl.multiple_of(index * LANES, LANES), count * LANES)


def pack_kernel(nhelper, helper_ref, live_ref, ids_ref, r_ref, out_ref):
    lane = lax.broadcasted_iota(jnp.int32, (TABLE, LANES), 1)
    row = lax.broadcasted_iota(jnp.int32, (TABLE, LANES), 0)
    table = jnp.full((TABLE, LANES), -1, jnp.int32)
    height = r_ref.shape[0]
    for c in range(height // LANES):
        tile = helper_ref[0] + nhelper * c
        ids = ids_ref[pl.ds(tile, 1), :]
        table = jnp.where(row == c, jnp.where(tile * LANES + lane < live_ref[0], ids, -1), table)
    out_ref[pl.ds(0, height), :] = r_ref[...]
    out_ref[pl.ds(height, TABLE), pl.ds(0, LANES)] = table.astype(jnp.float32).astype(jnp.bfloat16)


def table_kernel(clusters_ref, count_ref, out_ref):
    lane = lax.broadcasted_iota(jnp.int32, out_ref.shape, 1)
    qblocks = clusters_ref.shape[0]
    row = jnp.where(lane == qblocks, count_ref[0], 0)
    for k in range(qblocks):
        row = jnp.where(lane == k, clusters_ref[k], row)
    out_ref[...] = row


def stage_kernel(*refs):
    half = len(refs) // 2
    for source, out in zip(refs[:half], refs[half:]):
        out[...] = source[...]


def score_kernel(chunks, qblocks, pieces, first, wide, beta_ref, *refs):
    if first:
        (*given, out_ref, qv, info_out, q_list, ids_ref, other_ref, info, info_sem) = refs
        q_refs = []
        for n in pieces:
            q_refs.append(given[:n])
            given = given[n:]
        t_refs, r_refs = given[:4], given[4:]
    else:
        (info, qv, prev_ref, *r_refs, out_ref, q_list, ids_ref, other_ref) = refs
    width = qv.shape[1]
    height = chunks * LANES
    if first:
        for s, t_ref in enumerate(t_refs):
            info_out[s : s + 1, :] = t_ref[0:1, :]
        copy = pltpu.make_async_copy(info_out, info, info_sem)
        copy.start()

    for s, r_ref in enumerate(r_refs):
        table = r_ref[pl.ds(height, TABLE), pl.ds(0, LANES)].astype(jnp.float32)
        for c in range(chunks):
            ids = jnp.broadcast_to(table[c : c + 1, :], (LANES, LANES)).T
            rows = pl.ds(s * height + c * LANES, LANES)
            ids_ref[rows, :] = ids
            other_ref[rows, :] = jnp.where(ids < 0.0, DEAD, -4.0)
    if first:
        copy.wait()

    q_count = jnp.int32(0)
    for source in range(4):
        blocks = info[source, qblocks]

        def one_block(block, carry, source=source, q_count=q_count):
            q_list[q_count + block, 0] = source * qblocks + block
            q_list[q_count + block, 1] = info[source, block]
            return carry

        lax.fori_loop(0, blocks, one_block, 0)
        start = 0
        for piece in q_refs[source] if first else ():
            each = piece.shape[0] // LANES

            def move(block, carry, place=q_count + start, piece=piece):
                qv[rows_of(place + block), :] = piece[rows_of(block), :]
                return carry

            lax.fori_loop(0, jnp.clip(blocks - start, 0, each), move, 0)
            start += each
        q_count = q_count + blocks

    factor = LOG2E / math.sqrt(width)
    out_ref[...] = jnp.zeros_like(out_ref) if first else prev_ref[...]

    def query_blocks(group, carry):
        sides = []
        for side in range(wide):
            entry = jnp.minimum(wide * group + side, q_count - 1)
            slot, cluster = q_list[entry, 0], q_list[entry, 1]
            beta = beta_ref[cluster]
            sides.append(
                (slot, cluster.astype(jnp.float32), beta * factor, beta * beta * (0.5 * LOG2E))
            )
        accs = [jnp.zeros((8, LANES), jnp.float32) for _ in range(wide)]
        for s, r_ref in enumerate(r_refs):
            tile = r_ref[pl.ds(0, height), :]
            rows = pl.ds(s * height, height)
            for pair in range(wide // 2):
                score = lax.dot_general(
                    tile,
                    qv[rows_of(wide * group + 2 * pair, 2), :],
                    (((1,), (1,)), ((), ())),
                    preferred_element_type=jnp.float32,
                )
                for half in range(2):
                    side = 2 * pair + half
                    _, cluster, scale, offset = sides[side]
                    part = score[:, half * LANES : (half + 1) * LANES]
                    weight = jnp.where(ids_ref[rows, :] == cluster, 0.0, other_ref[rows, :])
                    value = jnp.exp2((part * scale - offset) + weight)
                    accs[side] += jnp.sum(value.reshape(height // 8, 8, LANES), axis=0)
        for side in range(wide):
            total = jnp.sum(accs[side], axis=0, keepdims=True)

            @pl.when(wide * group + side < q_count)
            def _(side=side, total=total):
                row = pl.ds(sides[side][0], 1)
                out_ref[row, :] = out_ref[row, :] + total

        return carry

    lax.fori_loop(0, (q_count + wide - 1) // wide, query_blocks, 0)


def score_call(chunks, qblocks, pieces, wide, beta, given, payloads, first):
    width = payloads[0].shape[1]
    slots = 4 * qblocks
    height = chunks * LANES
    totals_shape = jax.ShapeDtypeStruct((slots, LANES), jnp.float32)
    packed_shape = jax.ShapeDtypeStruct((slots * LANES, width), jnp.bfloat16)
    info_shape = jax.ShapeDtypeStruct((8, LANES), jnp.int32)
    spread = pltpu.VMEM((len(payloads) * height, LANES), jnp.float32)
    scratch = [pltpu.SMEM((slots, 2), jnp.int32), spread, spread]
    specs = [VMEM] * (len(given) + len(payloads))
    if first:
        scratch += [pltpu.SMEM((8, LANES), jnp.int32), pltpu.SemaphoreType.DMA]
    else:
        specs[0] = SMEM
    return pl.pallas_call(
        functools.partial(score_kernel, chunks, qblocks, pieces, first, wide),
        out_shape=(totals_shape, packed_shape, info_shape) if first else totals_shape,
        in_specs=[SMEM] + specs,
        out_specs=(VMEM, VMEM, VMEM) if first else VMEM,
        scratch_shapes=scratch,
        compiler_params=PARAMS,
        cost_estimate=cost(1, 1),
    )(beta, *given, *payloads)


def per_device(
    queries,
    query_block_cluster,
    block_count,
    references,
    ref_cluster,
    ref_rows,
    cluster_beta,
    cluster_member_count,
):
    nblk, nhelper = lax.axis_size("blk"), lax.axis_size("helper")
    helper = lax.axis_index("helper").astype(jnp.int32)
    qblocks = query_block_cluster.shape[0]
    rows, width = references.shape
    tiles = rows // LANES
    chunks = tiles // nhelper
    sources = nblk // 2

    q_partner = swap(queries, "blk")
    by_chunk = references.reshape(chunks, nhelper, LANES, width)
    own = lax.dynamic_index_in_dim(by_chunk, helper, 1, keepdims=False)
    own = pl.pallas_call(
        functools.partial(pack_kernel, nhelper),
        out_shape=jax.ShapeDtypeStruct((chunks * LANES + TABLE, width), jnp.bfloat16),
        in_specs=[SMEM] * 2 + [VMEM] * 2,
        out_specs=VMEM,
        compiler_params=PARAMS,
        cost_estimate=cost(1, 1),
    )(
        helper[None],
        ref_rows,
        ref_cluster.reshape(tiles, LANES),
        own.reshape(chunks * LANES, width),
    )

    held, mask = [own], sources - 1
    while mask:
        held = held + [trade(x, 2 * mask) for x in held]
        mask //= 2
    q_helper = swap(queries, "helper")

    table = pl.pallas_call(
        table_kernel,
        out_shape=jax.ShapeDtypeStruct((8, LANES), jnp.int32),
        in_specs=[SMEM] * 2,
        out_specs=VMEM,
        compiler_params=PARAMS,
        cost_estimate=cost(1, 1),
    )(after(query_block_cluster, own), block_count)
    q_tables = (table, swap(table, "helper"), swap(table, "blk"), swap_both(table))
    staged = pl.pallas_call(
        stage_kernel,
        out_shape=jax.ShapeDtypeStruct(queries.shape, queries.dtype),
        in_specs=[VMEM],
        out_specs=VMEM,
        compiler_params=PARAMS,
        cost_estimate=cost(1, 1),
    )(queries)
    q_partner = after(q_partner, staged, *held[1:-1], *q_tables)
    half = qblocks // 2 * LANES
    q_both = [swap(q_partner[:half], "helper"), swap(q_partner[half:], "helper")]
    queries = (staged, q_helper, q_partner, *q_both)
    pieces = (1, 1, 1, 2)

    totals, packed, info = score_call(
        chunks,
        qblocks,
        pieces,
        2,
        cluster_beta,
        (*queries, *q_tables),
        held[:-1],
        True,
    )
    totals = score_call(
        chunks,
        qblocks,
        pieces,
        8,
        cluster_beta,
        (info, packed, totals),
        held[-1:],
        False,
    )
    totals = totals.reshape(4, qblocks, LANES)
    total = totals[0] + swap(totals[1], "helper") + swap(totals[2], "blk") + swap_both(totals[3])
    columns = jnp.arange(cluster_member_count.shape[0], dtype=jnp.int32)
    onehot = query_block_cluster[:, None] == columns[None, :]
    sizes = jnp.sum(jnp.where(onehot, cluster_member_count[None, :], 0), axis=1)
    density = jnp.log1p(total / sizes.astype(jnp.float32)[:, None])
    return density.reshape(qblocks * LANES)


def solution(mesh):
    in_specs = (
        P(("parts", "blk", "helper"), None),
        P(("parts", "blk", "helper")),
        P(("parts", "blk", "helper")),
        P(("parts", "blk"), None),
        P(("parts", "blk")),
        P(("parts", "blk")),
        P("parts"),
        P("parts"),
    )
    out_specs = P(("parts", "blk", "helper"))
    return jax.shard_map(
        per_device, mesh=mesh, in_specs=in_specs, out_specs=out_specs, check_vma=False
    )
```

```python
import functools
import math

import jax
import jax.numpy as jnp
from jax import lax
from jax.experimental import pallas as pl
from jax.experimental.pallas import tpu as pltpu
from jax.sharding import PartitionSpec as P

LANES = 128
TABLE = 8
LATE = 64
LOG2E = 1.4426950408889634
DEAD = -1.0e30
SMEM = pl.BlockSpec(memory_space=pltpu.SMEM)
VMEM = pl.BlockSpec(memory_space=pltpu.VMEM)
PARAMS = pltpu.CompilerParams(vmem_limit_bytes=24 * 1024 * 1024)


def trade(value, mask):
    length = lax.axis_size("blk")
    return lax.ppermute(value, "blk", [(i, i ^ mask) for i in range(length)])


def swap(value, axis):
    length = lax.axis_size(axis)
    return lax.ppermute(value, axis, [(i, i ^ 1) for i in range(length)])


def swap_both(value):
    nblk, nhelper = lax.axis_size("blk"), lax.axis_size("helper")
    pairs = [(i, (i ^ nhelper) ^ 1) for i in range(nblk * nhelper)]
    return lax.ppermute(value, ("blk", "helper"), pairs)


def after(value, *others):
    return lax.optimization_barrier((value, *others))[0]


def cost(flops, moved):
    return pl.CostEstimate(flops=flops, bytes_accessed=moved, transcendentals=0)


def rows_of(index, count=1):
    return pl.ds(pl.multiple_of(index * LANES, LANES), count * LANES)


def pack_kernel(nhelper, helper_ref, live_ref, ids_ref, r_ref, whole_ref, most_ref, late_ref):
    lane = lax.broadcasted_iota(jnp.int32, (TABLE, LANES), 1)
    row = lax.broadcasted_iota(jnp.int32, (TABLE, LANES), 0)
    table = jnp.full((TABLE, LANES), -1, jnp.int32)
    height = r_ref.shape[0]
    for c in range(height // LANES):
        tile = helper_ref[0] + nhelper * c
        ids = ids_ref[pl.ds(tile, 1), :]
        table = jnp.where(row == c, jnp.where(tile * LANES + lane < live_ref[0], ids, -1), table)
    table = table.astype(jnp.float32).astype(jnp.bfloat16)
    for out_ref, count in ((whole_ref, height), (most_ref, height - LATE)):
        out_ref[pl.ds(0, count), :] = r_ref[pl.ds(0, count), :]
        out_ref[pl.ds(count, TABLE), pl.ds(0, LANES)] = table
    late_ref[...] = r_ref[pl.ds(height - LATE, LATE), :]


def table_kernel(clusters_ref, count_ref, out_ref):
    lane = lax.broadcasted_iota(jnp.int32, out_ref.shape, 1)
    qblocks = clusters_ref.shape[0]
    row = jnp.where(lane == qblocks, count_ref[0], 0)
    for k in range(qblocks):
        row = jnp.where(lane == k, clusters_ref[k], row)
    out_ref[...] = row


def stage_kernel(*refs):
    half = len(refs) // 2
    for source, out in zip(refs[:half], refs[half:]):
        out[...] = source[...]


def score_kernel(spans, qblocks, pieces, first, wide, beta_ref, *refs):
    if first:
        (*given, out_ref, qv, info_out, q_list, ids_ref, other_ref, info, info_sem) = refs
        q_refs = []
        for n in pieces:
            q_refs.append(given[:n])
            given = given[n:]
        t_refs, r_refs = given[:4], given[4:]
    else:
        (info, qv, prev_ref, *r_refs, out_ref, q_list, ids_ref, other_ref) = refs
    width = qv.shape[1]
    if first:
        for s, t_ref in enumerate(t_refs):
            info_out[s : s + 1, :] = t_ref[0:1, :]
        copy = pltpu.make_async_copy(info_out, info, info_sem)
        copy.start()

    start = 0
    for (begin, end, behind), r_ref in zip(spans, r_refs):
        if behind is None:
            r_ref, behind = r_refs[-1], r_refs[-1].shape[0] - TABLE
        table = r_ref[pl.ds(behind, TABLE), pl.ds(0, LANES)].astype(jnp.float32)
        for c in range(begin // LANES, -(-end // LANES)):
            low, high = max(begin, c * LANES), min(end, (c + 1) * LANES)
            ids = jnp.broadcast_to(table[c : c + 1, :], (LANES, LANES)).T
            ids = ids[low - c * LANES : high - c * LANES, :]
            rows = pl.ds(start, high - low)
            ids_ref[rows, :] = ids
            other_ref[rows, :] = jnp.where(ids < 0.0, DEAD, -4.0)
            start += high - low
    if first:
        copy.wait()

    q_count = jnp.int32(0)
    for source in range(4):
        blocks = info[source, qblocks]

        def one_block(block, carry, source=source, q_count=q_count):
            q_list[q_count + block, 0] = source * qblocks + block
            q_list[q_count + block, 1] = info[source, block]
            return carry

        lax.fori_loop(0, blocks, one_block, 0)
        start = 0
        for piece in q_refs[source] if first else ():
            each = piece.shape[0] // LANES

            def move(block, carry, place=q_count + start, piece=piece):
                qv[rows_of(place + block), :] = piece[rows_of(block), :]
                return carry

            lax.fori_loop(0, jnp.clip(blocks - start, 0, each), move, 0)
            start += each
        q_count = q_count + blocks

    factor = LOG2E / math.sqrt(width)
    out_ref[...] = jnp.zeros_like(out_ref) if first else prev_ref[...]

    def query_blocks(group, carry):
        sides = []
        for side in range(wide):
            entry = jnp.minimum(wide * group + side, q_count - 1)
            slot, cluster = q_list[entry, 0], q_list[entry, 1]
            beta = beta_ref[0, cluster]
            sides.append(
                (slot, cluster.astype(jnp.float32), beta * factor, beta * beta * (0.5 * LOG2E))
            )
        accs = [jnp.zeros((8, LANES), jnp.float32) for _ in range(wide)]
        start = 0
        for (begin, end, _), r_ref in zip(spans, r_refs):
            height = end - begin
            tile = r_ref[pl.ds(0, height), :]
            rows = pl.ds(start, height)
            start += height
            for pair in range(wide // 2):
                score = lax.dot_general(
                    tile,
                    qv[rows_of(wide * group + 2 * pair, 2), :],
                    (((1,), (1,)), ((), ())),
                    preferred_element_type=jnp.float32,
                )
                for half in range(2):
                    side = 2 * pair + half
                    _, cluster, scale, offset = sides[side]
                    part = score[:, half * LANES : (half + 1) * LANES]
                    weight = jnp.where(ids_ref[rows, :] == cluster, 0.0, other_ref[rows, :])
                    value = jnp.exp2((part * scale - offset) + weight)
                    accs[side] += jnp.sum(value.reshape(height // 8, 8, LANES), axis=0)
        for side in range(wide):
            total = jnp.sum(accs[side], axis=0, keepdims=True)

            @pl.when(wide * group + side < q_count)
            def _(side=side, total=total):
                row = pl.ds(sides[side][0], 1)
                out_ref[row, :] = out_ref[row, :] + total

        return carry

    lax.fori_loop(0, (q_count + wide - 1) // wide, query_blocks, 0)


def score_call(spans, qblocks, pieces, wide, beta, given, payloads, first):
    width = payloads[0].shape[1]
    slots = 4 * qblocks
    height = sum(end - begin for begin, end, _ in spans)
    totals_shape = jax.ShapeDtypeStruct((slots, LANES), jnp.float32)
    packed_shape = jax.ShapeDtypeStruct((slots * LANES, width), jnp.bfloat16)
    info_shape = jax.ShapeDtypeStruct((8, LANES), jnp.int32)
    spread = pltpu.VMEM((height, LANES), jnp.float32)
    scratch = [pltpu.SMEM((slots, 2), jnp.int32), spread, spread]
    specs = [VMEM] * (len(given) + len(payloads))
    if first:
        scratch += [pltpu.SMEM((8, LANES), jnp.int32), pltpu.SemaphoreType.DMA]
    else:
        specs[0] = SMEM
    return pl.pallas_call(
        functools.partial(score_kernel, spans, qblocks, pieces, first, wide),
        out_shape=(totals_shape, packed_shape, info_shape) if first else totals_shape,
        in_specs=[SMEM] + specs,
        out_specs=(VMEM, VMEM, VMEM) if first else VMEM,
        scratch_shapes=scratch,
        compiler_params=PARAMS,
        cost_estimate=cost(1, 1),
    )(beta, *given, *payloads)


def per_device(
    queries,
    query_block_cluster,
    block_count,
    references,
    ref_cluster,
    ref_rows,
    cluster_beta,
    cluster_member_count,
):
    nblk, nhelper = lax.axis_size("blk"), lax.axis_size("helper")
    helper = lax.axis_index("helper").astype(jnp.int32)
    qblocks = query_block_cluster.shape[0]
    rows, width = references.shape
    tiles = rows // LANES
    chunks = tiles // nhelper
    sources = nblk // 2

    q_partner = swap(queries, "blk")
    by_chunk = references.reshape(chunks, nhelper, LANES, width)
    own = lax.dynamic_index_in_dim(by_chunk, helper, 1, keepdims=False)
    height = chunks * LANES
    own, most, late = pl.pallas_call(
        functools.partial(pack_kernel, nhelper),
        out_shape=[
            jax.ShapeDtypeStruct((n, width), jnp.bfloat16)
            for n in (height + TABLE, height - LATE + TABLE, LATE)
        ],
        in_specs=[SMEM] * 2 + [VMEM] * 2,
        out_specs=[VMEM] * 3,
        compiler_params=PARAMS,
        cost_estimate=cost(1, 1),
    )(
        helper[None],
        ref_rows,
        ref_cluster.reshape(tiles, LANES),
        own.reshape(chunks * LANES, width),
    )

    held, mask = [own], sources - 1
    while mask > 1:
        held, mask = held + [trade(x, 2 * mask) for x in held], mask // 2
    held += [trade(most, 2)] + [trade(x, 2) for x in held[1:]]
    late = trade(late, 2)
    spans = [(0, height, height)] * len(held)
    spans[len(held) // 2] = (0, height - LATE, height - LATE)
    tabled = held[len(held) // 2]
    q_helper = swap(queries, "helper")

    table = pl.pallas_call(
        table_kernel,
        out_shape=jax.ShapeDtypeStruct((8, LANES), jnp.int32),
        in_specs=[SMEM] * 2,
        out_specs=VMEM,
        compiler_params=PARAMS,
        cost_estimate=cost(1, 1),
    )(after(query_block_cluster, own), block_count)
    q_tables = (table, swap(table, "helper"), swap(table, "blk"), swap_both(table))
    beta = cluster_beta.reshape(1, -1)
    staged, beta = pl.pallas_call(
        stage_kernel,
        out_shape=[jax.ShapeDtypeStruct(x.shape, x.dtype) for x in (queries, beta)],
        in_specs=[VMEM] * 2,
        out_specs=[VMEM] * 2,
        compiler_params=PARAMS,
        cost_estimate=cost(1, 1),
    )(queries, beta)
    q_partner = after(q_partner, staged, *held[1:-1], *q_tables)
    half = qblocks // 2 * LANES
    q_both = [swap(q_partner[:half], "helper"), swap(q_partner[half:], "helper")]
    queries = (staged, q_helper, q_partner, *q_both)
    pieces = (1, 1, 1, 2)

    totals, packed, info = score_call(
        tuple(spans[:-1]),
        qblocks,
        pieces,
        4,
        beta,
        (*queries, *q_tables),
        held[:-1],
        True,
    )
    for payloads, span in (
        (held[-1:], spans[-1]),
        ([late, tabled], (height - LATE, height, None)),
    ):
        given = (info, packed, totals)
        totals = score_call((span,), qblocks, pieces, 8, beta, given, payloads, False)
    totals = totals.reshape(4, qblocks, LANES)
    total = totals[0] + swap(totals[1], "helper") + swap(totals[2], "blk") + swap_both(totals[3])
    columns = jnp.arange(cluster_member_count.shape[0], dtype=jnp.int32)
    onehot = query_block_cluster[:, None] == columns[None, :]
    sizes = jnp.sum(jnp.where(onehot, cluster_member_count[None, :], 0), axis=1)
    density = jnp.log1p(total / sizes.astype(jnp.float32)[:, None])
    return density.reshape(qblocks * LANES)


def solution(mesh):
    in_specs = (
        P(("parts", "blk", "helper"), None),
        P(("parts", "blk", "helper")),
        P(("parts", "blk", "helper")),
        P(("parts", "blk"), None),
        P(("parts", "blk")),
        P(("parts", "blk")),
        P("parts"),
        P("parts"),
    )
    out_specs = P(("parts", "blk", "helper"))
    return jax.shard_map(
        per_device, mesh=mesh, in_specs=in_specs, out_specs=out_specs, check_vma=False
    )
```

```python
import functools
import math

import jax
import jax.numpy as jnp
from jax import lax
from jax.experimental import pallas as pl
from jax.experimental.pallas import tpu as pltpu
from jax.sharding import PartitionSpec as P

LANES = 128
TABLE = 8
LOG2E = 1.4426950408889634
DEAD = -1.0e30
SMEM = pl.BlockSpec(memory_space=pltpu.SMEM)
VMEM = pl.BlockSpec(memory_space=pltpu.VMEM)
PARAMS = pltpu.CompilerParams(vmem_limit_bytes=24 * 1024 * 1024)


def trade(value, mask):
    length = lax.axis_size("blk")
    return lax.ppermute(value, "blk", [(i, i ^ mask) for i in range(length)])


def swap(value, axis):
    length = lax.axis_size(axis)
    return lax.ppermute(value, axis, [(i, i ^ 1) for i in range(length)])


def swap_both(value):
    nblk, nhelper = lax.axis_size("blk"), lax.axis_size("helper")
    pairs = [(i, (i ^ nhelper) ^ 1) for i in range(nblk * nhelper)]
    return lax.ppermute(value, ("blk", "helper"), pairs)


def after(value, *others):
    return lax.optimization_barrier((value, *others))[0]


def cost(flops, moved):
    return pl.CostEstimate(flops=flops, bytes_accessed=moved, transcendentals=0)


def rows_of(index, count=1):
    return pl.ds(pl.multiple_of(index * LANES, LANES), count * LANES)


def pack_kernel(nhelper, helper_ref, live_ref, ids_ref, r_ref, out_ref):
    lane = lax.broadcasted_iota(jnp.int32, (TABLE, LANES), 1)
    row = lax.broadcasted_iota(jnp.int32, (TABLE, LANES), 0)
    table = jnp.full((TABLE, LANES), -1, jnp.int32)
    height = r_ref.shape[0]
    for c in range(height // LANES):
        tile = helper_ref[0] + nhelper * c
        ids = ids_ref[pl.ds(tile, 1), :]
        table = jnp.where(row == c, jnp.where(tile * LANES + lane < live_ref[0], ids, -1), table)
    out_ref[pl.ds(0, height), :] = r_ref[...]
    out_ref[pl.ds(height, TABLE), pl.ds(0, LANES)] = table.astype(jnp.float32).astype(jnp.bfloat16)


def table_kernel(clusters_ref, count_ref, out_ref):
    lane = lax.broadcasted_iota(jnp.int32, out_ref.shape, 1)
    qblocks = clusters_ref.shape[0]
    row = jnp.where(lane == qblocks, count_ref[0], 0)
    for k in range(qblocks):
        row = jnp.where(lane == k, clusters_ref[k], row)
    out_ref[...] = row


def stage_kernel(*refs):
    half = len(refs) // 2
    for source, out in zip(refs[:half], refs[half:]):
        out[...] = source[...]


def score_kernel(chunks, qblocks, pieces, first, wide, *refs):
    if first:
        (beta_ref, *given, out_ref, qv, slot_ref, number_ref, info_v, info, ids_ref, other_ref, info_sem) = refs
        q_refs = []
        for n in pieces:
            q_refs.append(given[:n])
            given = given[n:]
        t_refs, r_refs = given[:4], given[4:]
    else:
        (slot_ref, number_ref, qv, prev_ref, *r_refs, out_ref, ids_ref, other_ref) = refs
    width = qv.shape[1]
    height = chunks * LANES
    slots = 4 * qblocks
    if first:
        for s, t_ref in enumerate(t_refs):
            info_v[s : s + 1, :] = t_ref[0:1, :]
        copy = pltpu.make_async_copy(info_v, info, info_sem)
        copy.start()

    for s, r_ref in enumerate(r_refs):
        table = r_ref[pl.ds(height, TABLE), pl.ds(0, LANES)].astype(jnp.float32)
        for c in range(chunks):
            ids = jnp.broadcast_to(table[c : c + 1, :], (LANES, LANES)).T
            rows = pl.ds(s * height + c * LANES, LANES)
            ids_ref[rows, :] = ids
            other_ref[rows, :] = jnp.where(ids < 0.0, DEAD, -4.0)

    if first:
        copy.wait()
        factor = LOG2E / math.sqrt(width)
        q_count = jnp.int32(0)
        for source in range(4):
            blocks = info[source, qblocks]

            def enter(block, carry, source=source, q_count=q_count):
                entry = q_count + block
                cluster = info[source, block]
                beta = beta_ref[0, cluster]
                slot_ref[entry] = source * qblocks + block
                number_ref[3 * entry] = cluster.astype(jnp.float32)
                number_ref[3 * entry + 1] = beta * factor
                number_ref[3 * entry + 2] = beta * beta * (0.5 * LOG2E)
                return carry

            lax.fori_loop(0, blocks, enter, 0)
            start = 0
            for piece in q_refs[source]:
                each = piece.shape[0] // LANES

                def move(block, carry, place=q_count + start, piece=piece):
                    qv[rows_of(place + block), :] = piece[rows_of(block), :]
                    return carry

                lax.fori_loop(0, jnp.clip(blocks - start, 0, each), move, 0)
                start += each
            q_count = q_count + blocks

        def spare(entry, carry):
            slot_ref[entry] = slots
            for i in range(3):
                number_ref[3 * entry + i] = 0.0
            return carry

        lax.fori_loop(q_count, slots, spare, 0)
        slot_ref[slots] = q_count
        out_ref[...] = jnp.zeros_like(out_ref)
    else:
        q_count = slot_ref[slots]
        out_ref[...] = prev_ref[...]

    def query_blocks(group, carry):
        sides = [wide * group + side for side in range(wide)]
        numbers = [[number_ref[3 * entry + i] for i in range(3)] for entry in sides]
        accs = [jnp.zeros((8, LANES), jnp.float32) for _ in range(wide)]
        for s, r_ref in enumerate(r_refs):
            tile = r_ref[pl.ds(0, height), :]
            rows = pl.ds(s * height, height)
            for pair in range(wide // 2):
                score = lax.dot_general(
                    tile,
                    qv[rows_of(wide * group + 2 * pair, 2), :],
                    (((1,), (1,)), ((), ())),
                    preferred_element_type=jnp.float32,
                )
                for half in range(2):
                    side = 2 * pair + half
                    cluster, scale, offset = numbers[side]
                    part = score[:, half * LANES : (half + 1) * LANES]
                    weight = jnp.where(ids_ref[rows, :] == cluster, 0.0, other_ref[rows, :])
                    value = jnp.exp2((part * scale - offset) + weight)
                    accs[side] += jnp.sum(value.reshape(height // 8, 8, LANES), axis=0)
        for entry, acc in zip(sides, accs):
            row = pl.ds(slot_ref[entry], 1)
            out_ref[row, :] = out_ref[row, :] + jnp.sum(acc, axis=0, keepdims=True)
        return carry

    lax.fori_loop(0, (q_count + wide - 1) // wide, query_blocks, 0)


def score_call(chunks, qblocks, pieces, wide, given, payloads, first):
    width = payloads[0].shape[1]
    slots = 4 * qblocks
    rows = len(payloads) * chunks * LANES
    totals_shape = jax.ShapeDtypeStruct((slots + 8, LANES), jnp.float32)
    packed_shape = jax.ShapeDtypeStruct((slots * LANES, width), jnp.bfloat16)
    slot_shape = jax.ShapeDtypeStruct((slots + 8,), jnp.int32)
    number_shape = jax.ShapeDtypeStruct((3 * slots,), jnp.float32)
    scratch = [pltpu.VMEM((rows, LANES), jnp.float32)] * 2
    if first:
        scratch = [pltpu.VMEM((8, LANES), jnp.int32), pltpu.SMEM((8, LANES), jnp.int32)] + scratch
        scratch.append(pltpu.SemaphoreType.DMA)
        specs = [SMEM] + [VMEM] * (len(given) - 1 + len(payloads))
    else:
        specs = [SMEM] * 2 + [VMEM] * (len(given) - 2 + len(payloads))
    return pl.pallas_call(
        functools.partial(score_kernel, chunks, qblocks, pieces, first, wide),
        out_shape=(totals_shape, packed_shape, slot_shape, number_shape) if first else totals_shape,
        in_specs=specs,
        out_specs=(VMEM, VMEM, SMEM, SMEM) if first else VMEM,
        scratch_shapes=scratch,
        compiler_params=PARAMS,
        cost_estimate=cost(1, 1),
    )(*given, *payloads)


def per_device(
    queries,
    query_block_cluster,
    block_count,
    references,
    ref_cluster,
    ref_rows,
    cluster_beta,
    cluster_member_count,
):
    nblk, nhelper = lax.axis_size("blk"), lax.axis_size("helper")
    helper = lax.axis_index("helper").astype(jnp.int32)
    qblocks = query_block_cluster.shape[0]
    rows, width = references.shape
    tiles = rows // LANES
    chunks = tiles // nhelper
    sources = nblk // 2

    q_partner = swap(queries, "blk")
    by_chunk = references.reshape(chunks, nhelper, LANES, width)
    own = lax.dynamic_index_in_dim(by_chunk, helper, 1, keepdims=False)
    own = pl.pallas_call(
        functools.partial(pack_kernel, nhelper),
        out_shape=jax.ShapeDtypeStruct((chunks * LANES + TABLE, width), jnp.bfloat16),
        in_specs=[SMEM] * 2 + [VMEM] * 2,
        out_specs=VMEM,
        compiler_params=PARAMS,
        cost_estimate=cost(1, 1),
    )(
        helper[None],
        ref_rows,
        ref_cluster.reshape(tiles, LANES),
        own.reshape(chunks * LANES, width),
    )

    held, mask = [own], sources - 1
    while mask:
        held = held + [trade(x, 2 * mask) for x in held]
        mask //= 2
    q_helper = swap(queries, "helper")

    table = pl.pallas_call(
        table_kernel,
        out_shape=jax.ShapeDtypeStruct((8, LANES), jnp.int32),
        in_specs=[SMEM] * 2,
        out_specs=VMEM,
        compiler_params=PARAMS,
        cost_estimate=cost(1, 1),
    )(after(query_block_cluster, own), block_count)
    q_tables = (table, swap(table, "helper"), swap(table, "blk"), swap_both(table))
    beta = cluster_beta.reshape(1, -1)
    staged, beta = pl.pallas_call(
        stage_kernel,
        out_shape=[jax.ShapeDtypeStruct(x.shape, x.dtype) for x in (queries, beta)],
        in_specs=[VMEM] * 2,
        out_specs=[VMEM] * 2,
        compiler_params=PARAMS,
        cost_estimate=cost(1, 1),
    )(queries, beta)
    q_partner = after(q_partner, staged, *held[1:-1], *q_tables)
    half = qblocks // 2 * LANES
    q_both = [swap(q_partner[:half], "helper"), swap(q_partner[half:], "helper")]
    queries = (staged, q_helper, q_partner, *q_both)
    pieces = (1, 1, 1, 2)

    given = (beta, *queries, *q_tables)
    totals, packed, *plan = score_call(chunks, qblocks, pieces, 4, given, held[:-1], True)
    given = (*plan, packed, totals)
    totals = score_call(chunks, qblocks, pieces, 8, given, held[-1:], False)
    totals = totals[: 4 * qblocks]
    totals = totals.reshape(4, qblocks, LANES)
    total = totals[0] + swap(totals[1], "helper") + swap(totals[2], "blk") + swap_both(totals[3])
    columns = jnp.arange(cluster_member_count.shape[0], dtype=jnp.int32)
    onehot = query_block_cluster[:, None] == columns[None, :]
    sizes = jnp.sum(jnp.where(onehot, cluster_member_count[None, :], 0), axis=1)
    density = jnp.log1p(total / sizes.astype(jnp.float32)[:, None])
    return density.reshape(qblocks * LANES)


def solution(mesh):
    in_specs = (
        P(("parts", "blk", "helper"), None),
        P(("parts", "blk", "helper")),
        P(("parts", "blk", "helper")),
        P(("parts", "blk"), None),
        P(("parts", "blk")),
        P(("parts", "blk")),
        P("parts"),
        P("parts"),
    )
    out_specs = P(("parts", "blk", "helper"))
    return jax.shard_map(
        per_device, mesh=mesh, in_specs=in_specs, out_specs=out_specs, check_vma=False
    )
```

```python
import functools
import math

import jax
import jax.numpy as jnp
from jax import lax
from jax.experimental import pallas as pl
from jax.experimental.pallas import tpu as pltpu
from jax.sharding import PartitionSpec as P

LANES = 128
TABLE = 8
LOG2E = 1.4426950408889634
DEAD = -1.0e30
SMEM = pl.BlockSpec(memory_space=pltpu.SMEM)
VMEM = pl.BlockSpec(memory_space=pltpu.VMEM)
PARAMS = pltpu.CompilerParams(vmem_limit_bytes=24 * 1024 * 1024)


def trade(value, mask):
    length = lax.axis_size("blk")
    return lax.ppermute(value, "blk", [(i, i ^ mask) for i in range(length)])


def swap(value, axis):
    length = lax.axis_size(axis)
    return lax.ppermute(value, axis, [(i, i ^ 1) for i in range(length)])


def swap_both(value):
    nblk, nhelper = lax.axis_size("blk"), lax.axis_size("helper")
    pairs = [(i, (i ^ nhelper) ^ 1) for i in range(nblk * nhelper)]
    return lax.ppermute(value, ("blk", "helper"), pairs)


def after(value, *others):
    return lax.optimization_barrier((value, *others))[0]


def cost(flops, moved):
    return pl.CostEstimate(flops=flops, bytes_accessed=moved, transcendentals=0)


def rows_of(index, count=1):
    return pl.ds(pl.multiple_of(index * LANES, LANES), count * LANES)


def pack_kernel(nhelper, helper_ref, live_ref, ids_ref, r_ref, out_ref):
    lane = lax.broadcasted_iota(jnp.int32, (TABLE, LANES), 1)
    row = lax.broadcasted_iota(jnp.int32, (TABLE, LANES), 0)
    table = jnp.full((TABLE, LANES), -1, jnp.int32)
    height = r_ref.shape[0]
    for c in range(height // LANES):
        tile = helper_ref[0] + nhelper * c
        ids = ids_ref[pl.ds(tile, 1), :]
        table = jnp.where(row == c, jnp.where(tile * LANES + lane < live_ref[0], ids, -1), table)
    out_ref[pl.ds(0, height), :] = r_ref[...]
    out_ref[pl.ds(height, TABLE), pl.ds(0, LANES)] = table.astype(jnp.float32).astype(jnp.bfloat16)


def table_kernel(clusters_ref, count_ref, out_ref):
    lane = lax.broadcasted_iota(jnp.int32, out_ref.shape, 1)
    qblocks = clusters_ref.shape[0]
    row = jnp.where(lane == qblocks, count_ref[0], 0)
    for k in range(qblocks):
        row = jnp.where(lane == k, clusters_ref[k], row)
    out_ref[...] = row


def stage_kernel(*refs):
    half = len(refs) // 2
    for source, out in zip(refs[:half], refs[half:]):
        out[...] = source[...]


def score_kernel(chunks, qblocks, pieces, first, wide, *refs):
    if first:
        (beta_ref, *given, out_ref, qv, slot_ref, number_ref, info_v, info, ids_ref, other_ref, info_sem) = refs
        q_refs = []
        for n in pieces:
            q_refs.append(given[:n])
            given = given[n:]
        t_refs, r_refs = given[:4], given[4:]
    else:
        (slot_ref, number_ref, qv, prev_ref, *r_refs, out_ref, ids_ref, other_ref) = refs
    width = qv.shape[1]
    height = chunks * LANES
    slots = 4 * qblocks
    if first:
        for s, t_ref in enumerate(t_refs):
            info_v[s : s + 1, :] = t_ref[0:1, :]
        copy = pltpu.make_async_copy(info_v, info, info_sem)
        copy.start()

    for s, r_ref in enumerate(r_refs):
        table = r_ref[pl.ds(height, TABLE), pl.ds(0, LANES)].astype(jnp.float32)
        for c in range(chunks):
            ids = jnp.broadcast_to(table[c : c + 1, :], (LANES, LANES)).T
            rows = pl.ds(s * height + c * LANES, LANES)
            ids_ref[rows, :] = ids
            other_ref[rows, :] = jnp.where(ids < 0.0, DEAD, -4.0)

    if first:
        copy.wait()
        factor = LOG2E / math.sqrt(width)
        q_count = jnp.int32(0)
        for source in range(4):
            blocks = info[source, qblocks]

            def enter(block, carry, source=source, q_count=q_count):
                entry = q_count + block
                cluster = info[source, block]
                beta = beta_ref[0, cluster]
                slot_ref[entry] = source * qblocks + block
                number_ref[3 * entry] = cluster.astype(jnp.float32)
                number_ref[3 * entry + 1] = beta * factor
                number_ref[3 * entry + 2] = beta * beta * (0.5 * LOG2E)
                return carry

            lax.fori_loop(0, blocks, enter, 0)
            start = 0
            for piece in q_refs[source]:
                each = piece.shape[0] // LANES

                def move(block, carry, place=q_count + start, piece=piece):
                    qv[rows_of(place + block), :] = piece[rows_of(block), :]
                    return carry

                lax.fori_loop(0, jnp.clip(blocks - start, 0, each), move, 0)
                start += each
            q_count = q_count + blocks

        def spare(entry, carry):
            slot_ref[entry] = slots
            for i in range(3):
                number_ref[3 * entry + i] = 0.0
            return carry

        lax.fori_loop(q_count, slots, spare, 0)
        slot_ref[slots] = q_count
        out_ref[...] = jnp.zeros_like(out_ref)
    else:
        q_count = slot_ref[slots]
        out_ref[...] = prev_ref[...]

    def query_blocks(group, carry):
        sides = [wide * group + side for side in range(wide)]
        numbers = [[number_ref[3 * entry + i] for i in range(3)] for entry in sides]
        accs = [jnp.zeros((8, LANES), jnp.float32) for _ in range(wide)]
        for s, r_ref in enumerate(r_refs):
            tile = r_ref[pl.ds(0, height), :]
            rows = pl.ds(s * height, height)
            for pair in range(wide // 2):
                score = lax.dot_general(
                    tile,
                    qv[rows_of(wide * group + 2 * pair, 2), :],
                    (((1,), (1,)), ((), ())),
                    preferred_element_type=jnp.float32,
                )
                for half in range(2):
                    side = 2 * pair + half
                    cluster, scale, offset = numbers[side]
                    part = score[:, half * LANES : (half + 1) * LANES]
                    weight = jnp.where(ids_ref[rows, :] == cluster, 0.0, other_ref[rows, :])
                    value = jnp.exp2((part * scale - offset) + weight)
                    accs[side] += jnp.sum(value.reshape(height // 8, 8, LANES), axis=0)
        for entry, acc in zip(sides, accs):
            row = pl.ds(slot_ref[entry], 1)
            out_ref[row, :] = out_ref[row, :] + jnp.sum(acc, axis=0, keepdims=True)
        return carry

    lax.fori_loop(0, (q_count + wide - 1) // wide, query_blocks, 0)


def last_kernel(chunks, wide, slot_ref, number_ref, qv, prev_ref, r_ref, out_ref):
    height = chunks * LANES
    table = r_ref[pl.ds(height, TABLE), pl.ds(0, LANES)].astype(jnp.float32)
    ids = [table[c : c + 1, :] for c in range(chunks)]
    other = [jnp.where(row < 0.0, DEAD, -4.0) for row in ids]
    out_ref[...] = prev_ref[...]

    def query_blocks(group, carry):
        score = lax.dot_general(
            qv[rows_of(wide * group, wide), :],
            r_ref[pl.ds(0, height), :],
            (((1,), (1,)), ((), ())),
            preferred_element_type=jnp.float32,
        )
        for side in range(wide):
            entry = wide * group + side
            cluster, scale, offset = (number_ref[3 * entry + i] for i in range(3))
            acc = jnp.zeros((LANES, LANES), jnp.float32)
            for c in range(chunks):
                part = score[side * LANES : (side + 1) * LANES, c * LANES : (c + 1) * LANES]
                bias = jnp.where(ids[c] == cluster, 0.0, other[c]) - offset
                acc = acc + jnp.exp2(part * scale + bias)
            row = pl.ds(slot_ref[entry], 1)
            out_ref[row, :] = out_ref[row, :] + jnp.sum(acc.T, axis=0, keepdims=True)
        return carry

    q_count = slot_ref[slot_ref.shape[0] - 8]
    lax.fori_loop(0, (q_count + wide - 1) // wide, query_blocks, 0)


def score_call(chunks, qblocks, pieces, wide, given, payloads, first):
    width = payloads[0].shape[1]
    slots = 4 * qblocks
    rows = len(payloads) * chunks * LANES
    totals_shape = jax.ShapeDtypeStruct((slots + 8, LANES), jnp.float32)
    packed_shape = jax.ShapeDtypeStruct((slots * LANES, width), jnp.bfloat16)
    slot_shape = jax.ShapeDtypeStruct((slots + 8,), jnp.int32)
    number_shape = jax.ShapeDtypeStruct((3 * slots,), jnp.float32)
    scratch = [pltpu.VMEM((rows, LANES), jnp.float32)] * 2
    if first:
        scratch = [pltpu.VMEM((8, LANES), jnp.int32), pltpu.SMEM((8, LANES), jnp.int32)] + scratch
        scratch.append(pltpu.SemaphoreType.DMA)
        specs = [SMEM] + [VMEM] * (len(given) - 1 + len(payloads))
    else:
        specs = [SMEM] * 2 + [VMEM] * (len(given) - 2 + len(payloads))
    kernel = functools.partial(score_kernel, chunks, qblocks, pieces, first, wide)
    if not first:
        kernel, scratch = functools.partial(last_kernel, chunks, wide), []
    return pl.pallas_call(
        kernel,
        out_shape=(totals_shape, packed_shape, slot_shape, number_shape) if first else totals_shape,
        in_specs=specs,
        out_specs=(VMEM, VMEM, SMEM, SMEM) if first else VMEM,
        scratch_shapes=scratch,
        compiler_params=PARAMS,
        cost_estimate=cost(1, 1),
    )(*given, *payloads)


def per_device(
    queries,
    query_block_cluster,
    block_count,
    references,
    ref_cluster,
    ref_rows,
    cluster_beta,
    cluster_member_count,
):
    nblk, nhelper = lax.axis_size("blk"), lax.axis_size("helper")
    helper = lax.axis_index("helper").astype(jnp.int32)
    qblocks = query_block_cluster.shape[0]
    rows, width = references.shape
    tiles = rows // LANES
    chunks = tiles // nhelper
    sources = nblk // 2

    q_partner = swap(queries, "blk")
    by_chunk = references.reshape(chunks, nhelper, LANES, width)
    own = lax.dynamic_index_in_dim(by_chunk, helper, 1, keepdims=False)
    own = pl.pallas_call(
        functools.partial(pack_kernel, nhelper),
        out_shape=jax.ShapeDtypeStruct((chunks * LANES + TABLE, width), jnp.bfloat16),
        in_specs=[SMEM] * 2 + [VMEM] * 2,
        out_specs=VMEM,
        compiler_params=PARAMS,
        cost_estimate=cost(1, 1),
    )(
        helper[None],
        ref_rows,
        ref_cluster.reshape(tiles, LANES),
        own.reshape(chunks * LANES, width),
    )

    held, mask = [own], sources - 1
    while mask:
        held = held + [trade(x, 2 * mask) for x in held]
        mask //= 2
    q_helper = swap(queries, "helper")

    beta = cluster_beta.reshape(1, -1)
    staged, beta = pl.pallas_call(
        stage_kernel,
        out_shape=[jax.ShapeDtypeStruct(x.shape, x.dtype) for x in (queries, beta)],
        in_specs=[VMEM] * 2,
        out_specs=[VMEM] * 2,
        compiler_params=PARAMS,
        cost_estimate=cost(1, 1),
    )(queries, beta)
    table = pl.pallas_call(
        table_kernel,
        out_shape=jax.ShapeDtypeStruct((8, LANES), jnp.int32),
        in_specs=[SMEM] * 2,
        out_specs=VMEM,
        compiler_params=PARAMS,
        cost_estimate=cost(1, 1),
    )(after(query_block_cluster, own, staged), block_count)
    q_tables = (table, swap(table, "helper"), swap(table, "blk"), swap_both(table))
    q_partner = after(q_partner, staged, *held[1:-1], *q_tables)
    half = qblocks // 2 * LANES
    q_both = [swap(q_partner[:half], "helper"), swap(q_partner[half:], "helper")]
    queries = (staged, q_helper, q_partner, *q_both)
    pieces = (1, 1, 1, 2)

    given = (beta, *queries, *q_tables)
    totals, packed, *plan = score_call(chunks, qblocks, pieces, 4, given, held[:-1], True)
    given = (*plan, packed, totals)
    totals = score_call(chunks, qblocks, pieces, 8, given, held[-1:], False)
    totals = totals[: 4 * qblocks]
    totals = totals.reshape(4, qblocks, LANES)
    total = totals[0] + swap(totals[1], "helper") + swap(totals[2], "blk") + swap_both(totals[3])
    columns = jnp.arange(cluster_member_count.shape[0], dtype=jnp.int32)
    onehot = query_block_cluster[:, None] == columns[None, :]
    sizes = jnp.sum(jnp.where(onehot, cluster_member_count[None, :], 0), axis=1)
    density = jnp.log1p(total / sizes.astype(jnp.float32)[:, None])
    return density.reshape(qblocks * LANES)


def solution(mesh):
    in_specs = (
        P(("parts", "blk", "helper"), None),
        P(("parts", "blk", "helper")),
        P(("parts", "blk", "helper")),
        P(("parts", "blk"), None),
        P(("parts", "blk")),
        P(("parts", "blk")),
        P("parts"),
        P("parts"),
    )
    out_specs = P(("parts", "blk", "helper"))
    return jax.shard_map(
        per_device, mesh=mesh, in_specs=in_specs, out_specs=out_specs, check_vma=False
    )
```

```python
import functools
import math

import jax
import jax.numpy as jnp
from jax import lax
from jax.experimental import pallas as pl
from jax.experimental.pallas import tpu as pltpu
from jax.sharding import PartitionSpec as P

LANES = 128
TABLE = 8
LOG2E = 1.4426950408889634
DEAD = -1.0e30
SMEM = pl.BlockSpec(memory_space=pltpu.SMEM)
VMEM = pl.BlockSpec(memory_space=pltpu.VMEM)
PARAMS = pltpu.CompilerParams(vmem_limit_bytes=24 * 1024 * 1024)


def trade(value, mask):
    length = lax.axis_size("blk")
    return lax.ppermute(value, "blk", [(i, i ^ mask) for i in range(length)])


def swap(value, axis):
    length = lax.axis_size(axis)
    return lax.ppermute(value, axis, [(i, i ^ 1) for i in range(length)])


def swap_both(value):
    nblk, nhelper = lax.axis_size("blk"), lax.axis_size("helper")
    pairs = [(i, (i ^ nhelper) ^ 1) for i in range(nblk * nhelper)]
    return lax.ppermute(value, ("blk", "helper"), pairs)


def after(value, *others):
    return lax.optimization_barrier((value, *others))[0]


def cost(flops, moved):
    return pl.CostEstimate(flops=flops, bytes_accessed=moved, transcendentals=0)


def rows_of(index, count=1):
    return pl.ds(pl.multiple_of(index * LANES, LANES), count * LANES)


def pack_kernel(nhelper, helper_ref, live_ref, ids_ref, r_ref, out_ref):
    lane = lax.broadcasted_iota(jnp.int32, (TABLE, LANES), 1)
    row = lax.broadcasted_iota(jnp.int32, (TABLE, LANES), 0)
    table = jnp.full((TABLE, LANES), -1, jnp.int32)
    height = r_ref.shape[0]
    for c in range(height // LANES):
        tile = helper_ref[0] + nhelper * c
        ids = ids_ref[pl.ds(tile, 1), :]
        table = jnp.where(row == c, jnp.where(tile * LANES + lane < live_ref[0], ids, -1), table)
    out_ref[pl.ds(0, height), :] = r_ref[...]
    out_ref[pl.ds(height, TABLE), pl.ds(0, LANES)] = table.astype(jnp.float32).astype(jnp.bfloat16)


def table_kernel(clusters_ref, count_ref, out_ref):
    lane = lax.broadcasted_iota(jnp.int32, out_ref.shape, 1)
    qblocks = clusters_ref.shape[0]
    row = jnp.where(lane == qblocks, count_ref[0], 0)
    for k in range(qblocks):
        row = jnp.where(lane == k, clusters_ref[k], row)
    out_ref[...] = row


def stage_kernel(*refs):
    half = len(refs) // 2
    for source, out in zip(refs[:half], refs[half:]):
        out[...] = source[...]


def first_kernel(chunks, qblocks, pieces, wide, beta_ref, *refs):
    *given, out_ref, qv, slot_ref, number_ref, info_v, info, ids_ref, other_ref, info_sem = refs
    q_refs = []
    for n in pieces:
        q_refs.append(given[:n])
        given = given[n:]
    t_refs, r_refs = given[:4], given[4:]
    width = qv.shape[1]
    height = chunks * LANES
    slots = 4 * qblocks
    for s, t_ref in enumerate(t_refs):
        info_v[s : s + 1, :] = t_ref[0:1, :]
    copy = pltpu.make_async_copy(info_v, info, info_sem)
    copy.start()

    for s, r_ref in enumerate(r_refs):
        table = r_ref[pl.ds(height, TABLE), pl.ds(0, LANES)].astype(jnp.float32)
        for c in range(chunks):
            ids = jnp.broadcast_to(table[c : c + 1, :], (LANES, LANES)).T
            rows = pl.ds(s * height + c * LANES, LANES)
            ids_ref[rows, :] = ids
            other_ref[rows, :] = jnp.where(ids < 0.0, DEAD, -4.0)

    copy.wait()
    factor = LOG2E / math.sqrt(width)
    q_count = jnp.int32(0)
    for source in range(4):
        blocks = info[source, qblocks]

        def enter(block, carry, source=source, q_count=q_count):
            entry = q_count + block
            cluster = info[source, block]
            beta = beta_ref[0, cluster]
            slot_ref[entry] = source * qblocks + block
            number_ref[3 * entry] = cluster.astype(jnp.float32)
            number_ref[3 * entry + 1] = beta * factor
            number_ref[3 * entry + 2] = beta * beta * (0.5 * LOG2E)
            return carry

        lax.fori_loop(0, blocks, enter, 0)
        start = 0
        for piece in q_refs[source]:
            each = piece.shape[0] // LANES

            def move(block, carry, place=q_count + start, piece=piece):
                qv[rows_of(place + block), :] = piece[rows_of(block), :]
                return carry

            lax.fori_loop(0, jnp.clip(blocks - start, 0, each), move, 0)
            start += each
        q_count = q_count + blocks

    def spare(entry, carry):
        slot_ref[entry] = slots
        for i in range(3):
            number_ref[3 * entry + i] = 0.0
        return carry

    lax.fori_loop(q_count, slots, spare, 0)
    slot_ref[slots] = q_count
    out_ref[...] = jnp.zeros_like(out_ref)

    def query_blocks(group, carry):
        sides = [wide * group + side for side in range(wide)]
        numbers = [[number_ref[3 * entry + i] for i in range(3)] for entry in sides]
        accs = [jnp.zeros((8, LANES), jnp.float32) for _ in range(wide)]
        for s, r_ref in enumerate(r_refs):
            tile = r_ref[pl.ds(0, height), :]
            rows = pl.ds(s * height, height)
            for pair in range(wide // 2):
                score = lax.dot_general(
                    tile,
                    qv[rows_of(wide * group + 2 * pair, 2), :],
                    (((1,), (1,)), ((), ())),
                    preferred_element_type=jnp.float32,
                )
                for half in range(2):
                    side = 2 * pair + half
                    cluster, scale, offset = numbers[side]
                    part = score[:, half * LANES : (half + 1) * LANES]
                    weight = jnp.where(ids_ref[rows, :] == cluster, 0.0, other_ref[rows, :])
                    value = jnp.exp2((part * scale - offset) + weight)
                    accs[side] += jnp.sum(value.reshape(height // 8, 8, LANES), axis=0)
        for entry, acc in zip(sides, accs):
            row = pl.ds(slot_ref[entry], 1)
            out_ref[row, :] = out_ref[row, :] + jnp.sum(acc, axis=0, keepdims=True)
        return carry

    lax.fori_loop(0, (q_count + wide - 1) // wide, query_blocks, 0)


def last_kernel(chunks, wide, slot_ref, number_ref, qv, prev_ref, r_ref, out_ref):
    height = chunks * LANES
    table = r_ref[pl.ds(height, TABLE), pl.ds(0, LANES)].astype(jnp.float32)
    ids = [table[c : c + 1, :] for c in range(chunks)]
    other = [jnp.where(row < 0.0, DEAD, -4.0) for row in ids]
    out_ref[...] = prev_ref[...]

    def query_blocks(group, carry):
        score = lax.dot_general(
            qv[rows_of(wide * group, wide), :],
            r_ref[pl.ds(0, height), :],
            (((1,), (1,)), ((), ())),
            preferred_element_type=jnp.float32,
        )
        for side in range(wide):
            entry = wide * group + side
            cluster, scale, offset = (number_ref[3 * entry + i] for i in range(3))
            acc = jnp.zeros((LANES, LANES), jnp.float32)
            for c in range(chunks):
                part = score[side * LANES : (side + 1) * LANES, c * LANES : (c + 1) * LANES]
                bias = jnp.where(ids[c] == cluster, 0.0, other[c]) - offset
                acc = acc + jnp.exp2(part * scale + bias)
            row = pl.ds(slot_ref[entry], 1)
            out_ref[row, :] = out_ref[row, :] + jnp.sum(acc.T, axis=0, keepdims=True)
        return carry

    q_count = slot_ref[slot_ref.shape[0] - 8]
    lax.fori_loop(0, (q_count + wide - 1) // wide, query_blocks, 0)


def first_call(chunks, qblocks, pieces, wide, given, payloads):
    width = payloads[0].shape[1]
    slots = 4 * qblocks
    rows = len(payloads) * chunks * LANES
    return pl.pallas_call(
        functools.partial(first_kernel, chunks, qblocks, pieces, wide),
        out_shape=(
            jax.ShapeDtypeStruct((slots + 8, LANES), jnp.float32),
            jax.ShapeDtypeStruct((slots * LANES, width), jnp.bfloat16),
            jax.ShapeDtypeStruct((slots + 8,), jnp.int32),
            jax.ShapeDtypeStruct((3 * slots,), jnp.float32),
        ),
        in_specs=[SMEM] + [VMEM] * (len(given) - 1 + len(payloads)),
        out_specs=(VMEM, VMEM, SMEM, SMEM),
        scratch_shapes=[
            pltpu.VMEM((8, LANES), jnp.int32),
            pltpu.SMEM((8, LANES), jnp.int32),
            pltpu.VMEM((rows, LANES), jnp.float32),
            pltpu.VMEM((rows, LANES), jnp.float32),
            pltpu.SemaphoreType.DMA,
        ],
        compiler_params=PARAMS,
        cost_estimate=cost(1, 1),
    )(*given, *payloads)


def last_call(chunks, wide, slots, numbers, packed, totals, payload):
    return pl.pallas_call(
        functools.partial(last_kernel, chunks, wide),
        out_shape=jax.ShapeDtypeStruct(totals.shape, jnp.float32),
        in_specs=[SMEM] * 2 + [VMEM] * 3,
        out_specs=VMEM,
        compiler_params=PARAMS,
        cost_estimate=cost(1, 1),
    )(slots, numbers, packed, totals, payload)


def per_device(
    queries,
    query_block_cluster,
    block_count,
    references,
    ref_cluster,
    ref_rows,
    cluster_beta,
    cluster_member_count,
):
    nblk, nhelper = lax.axis_size("blk"), lax.axis_size("helper")
    helper = lax.axis_index("helper").astype(jnp.int32)
    qblocks = query_block_cluster.shape[0]
    rows, width = references.shape
    tiles = rows // LANES
    chunks = tiles // nhelper
    sources = nblk // 2

    q_partner = swap(queries, "blk")
    by_chunk = references.reshape(chunks, nhelper, LANES, width)
    own = lax.dynamic_index_in_dim(by_chunk, helper, 1, keepdims=False)
    own = pl.pallas_call(
        functools.partial(pack_kernel, nhelper),
        out_shape=jax.ShapeDtypeStruct((chunks * LANES + TABLE, width), jnp.bfloat16),
        in_specs=[SMEM] * 2 + [VMEM] * 2,
        out_specs=VMEM,
        compiler_params=PARAMS,
        cost_estimate=cost(1, 1),
    )(
        helper[None],
        ref_rows,
        ref_cluster.reshape(tiles, LANES),
        own.reshape(chunks * LANES, width),
    )

    held, mask = [own], sources - 1
    while mask:
        held = held + [trade(x, 2 * mask) for x in held]
        mask //= 2
    q_helper = swap(queries, "helper")

    beta = cluster_beta.reshape(1, -1)
    staged, beta = pl.pallas_call(
        stage_kernel,
        out_shape=[jax.ShapeDtypeStruct(x.shape, x.dtype) for x in (queries, beta)],
        in_specs=[VMEM] * 2,
        out_specs=[VMEM] * 2,
        compiler_params=PARAMS,
        cost_estimate=cost(1, 1),
    )(queries, beta)
    table = pl.pallas_call(
        table_kernel,
        out_shape=jax.ShapeDtypeStruct((8, LANES), jnp.int32),
        in_specs=[SMEM] * 2,
        out_specs=VMEM,
        compiler_params=PARAMS,
        cost_estimate=cost(1, 1),
    )(after(query_block_cluster, own, staged), block_count)
    q_tables = (table, swap(table, "helper"), swap(table, "blk"), swap_both(table))
    q_partner = after(q_partner, staged, *held[1:-1], *q_tables)
    half = qblocks // 2 * LANES
    q_both = [swap(q_partner[:half], "helper"), swap(q_partner[half:], "helper")]
    queries = (staged, q_helper, q_partner, *q_both)
    pieces = (1, 1, 1, 2)

    given = (beta, *queries, *q_tables)
    totals, packed, *plan = first_call(chunks, qblocks, pieces, 4, given, held[:-1])
    totals = last_call(chunks, 4, *plan, packed, totals, held[-1])
    totals = totals[: 4 * qblocks]
    totals = totals.reshape(4, qblocks, LANES)
    total = totals[0] + swap(totals[1], "helper") + swap(totals[2], "blk") + swap_both(totals[3])
    columns = jnp.arange(cluster_member_count.shape[0], dtype=jnp.int32)
    onehot = query_block_cluster[:, None] == columns[None, :]
    sizes = jnp.sum(jnp.where(onehot, cluster_member_count[None, :], 0), axis=1)
    density = jnp.log1p(total / sizes.astype(jnp.float32)[:, None])
    return density.reshape(qblocks * LANES)


def solution(mesh):
    in_specs = (
        P(("parts", "blk", "helper"), None),
        P(("parts", "blk", "helper")),
        P(("parts", "blk", "helper")),
        P(("parts", "blk"), None),
        P(("parts", "blk")),
        P(("parts", "blk")),
        P("parts"),
        P("parts"),
    )
    out_specs = P(("parts", "blk", "helper"))
    return jax.shard_map(
        per_device, mesh=mesh, in_specs=in_specs, out_specs=out_specs, check_vma=False
    )
```

```python
import functools
import math

import jax
import jax.numpy as jnp
from jax import lax
from jax.experimental import pallas as pl
from jax.experimental.pallas import tpu as pltpu
from jax.sharding import PartitionSpec as P

LANES = 128
TABLE = 8
LOG2E = 1.4426950408889634
DEAD = -1.0e30
SMEM = pl.BlockSpec(memory_space=pltpu.SMEM)
VMEM = pl.BlockSpec(memory_space=pltpu.VMEM)
PARAMS = pltpu.CompilerParams(vmem_limit_bytes=24 * 1024 * 1024)


def trade(value, mask):
    length = lax.axis_size("blk")
    return lax.ppermute(value, "blk", [(i, i ^ mask) for i in range(length)])


def swap(value, axis):
    length = lax.axis_size(axis)
    return lax.ppermute(value, axis, [(i, i ^ 1) for i in range(length)])


def swap_both(value):
    nblk, nhelper = lax.axis_size("blk"), lax.axis_size("helper")
    pairs = [(i, (i ^ nhelper) ^ 1) for i in range(nblk * nhelper)]
    return lax.ppermute(value, ("blk", "helper"), pairs)


def after(value, *others):
    return lax.optimization_barrier((value, *others))[0]


def cost(flops, moved):
    return pl.CostEstimate(flops=flops, bytes_accessed=moved, transcendentals=0)


def rows_of(index, count=1):
    return pl.ds(pl.multiple_of(index * LANES, LANES), count * LANES)


def pack_kernel(nhelper, helper_ref, live_ref, ids_ref, r_ref, out_ref):
    lane = lax.broadcasted_iota(jnp.int32, (TABLE, LANES), 1)
    row = lax.broadcasted_iota(jnp.int32, (TABLE, LANES), 0)
    table = jnp.full((TABLE, LANES), -1, jnp.int32)
    height = r_ref.shape[0]
    for c in range(height // LANES):
        tile = helper_ref[0] + nhelper * c
        ids = ids_ref[pl.ds(tile, 1), :]
        table = jnp.where(row == c, jnp.where(tile * LANES + lane < live_ref[0], ids, -1), table)
    out_ref[pl.ds(0, height), :] = r_ref[...]
    out_ref[pl.ds(height, TABLE), pl.ds(0, LANES)] = table.astype(jnp.float32).astype(jnp.bfloat16)


def table_kernel(clusters_ref, count_ref, out_ref):
    lane = lax.broadcasted_iota(jnp.int32, out_ref.shape, 1)
    qblocks = clusters_ref.shape[0]
    row = jnp.where(lane == qblocks, count_ref[0], 0)
    for k in range(qblocks):
        row = jnp.where(lane == k, clusters_ref[k], row)
    out_ref[...] = row


def stage_kernel(*refs):
    half = len(refs) // 2
    for source, out in zip(refs[:half], refs[half:]):
        out[...] = source[...]


def first_kernel(chunks, qblocks, pieces, wide, beta_ref, *refs):
    *given, out_ref, qv, slot_ref, number_ref, info_v, info, ids_ref, other_ref, info_sem = refs
    q_refs = []
    for n in pieces:
        q_refs.append(given[:n])
        given = given[n:]
    t_refs, r_refs = given[:4], given[4:]
    width = qv.shape[1]
    height = chunks * LANES
    slots = 4 * qblocks
    for s, t_ref in enumerate(t_refs):
        info_v[s : s + 1, :] = t_ref[0:1, :]
    copy = pltpu.make_async_copy(info_v, info, info_sem)
    copy.start()

    for s, r_ref in enumerate(r_refs):
        table = r_ref[pl.ds(height, TABLE), pl.ds(0, LANES)].astype(jnp.float32)
        for c in range(chunks):
            ids = jnp.broadcast_to(table[c : c + 1, :], (LANES, LANES)).T
            rows = pl.ds(s * height + c * LANES, LANES)
            ids_ref[rows, :] = ids
            other_ref[rows, :] = jnp.where(ids < 0.0, DEAD, -4.0)

    copy.wait()
    factor = LOG2E / math.sqrt(width)
    q_count = jnp.int32(0)
    for source in range(4):
        blocks = info[source, qblocks]

        def enter(block, carry, source=source, q_count=q_count):
            entry = q_count + block
            cluster = info[source, block]
            beta = beta_ref[0, cluster]
            slot_ref[entry] = source * qblocks + block
            number_ref[3 * entry] = cluster.astype(jnp.float32)
            number_ref[3 * entry + 1] = beta * factor
            number_ref[3 * entry + 2] = beta * beta * (0.5 * LOG2E)
            return carry

        lax.fori_loop(0, blocks, enter, 0)
        start = 0
        for piece in q_refs[source]:
            each = piece.shape[0] // LANES

            def move(block, carry, place=q_count + start, piece=piece):
                qv[rows_of(place + block), :] = piece[rows_of(block), :]
                return carry

            lax.fori_loop(0, jnp.clip(blocks - start, 0, each), move, 0)
            start += each
        q_count = q_count + blocks

    def spare(entry, carry):
        slot_ref[entry] = slots
        for i in range(3):
            number_ref[3 * entry + i] = 0.0
        return carry

    lax.fori_loop(q_count, slots, spare, 0)
    slot_ref[slots] = q_count
    out_ref[...] = jnp.zeros_like(out_ref)

    def query_blocks(group, carry):
        sides = [wide * group + side for side in range(wide)]
        numbers = [[number_ref[3 * entry + i] for i in range(3)] for entry in sides]
        accs = [jnp.zeros((8, LANES), jnp.float32) for _ in range(wide)]
        for s, r_ref in enumerate(r_refs):
            tile = r_ref[pl.ds(0, height), :]
            rows = pl.ds(s * height, height)
            for pair in range(wide // 2):
                score = lax.dot_general(
                    tile,
                    qv[rows_of(wide * group + 2 * pair, 2), :],
                    (((1,), (1,)), ((), ())),
                    preferred_element_type=jnp.float32,
                )
                for half in range(2):
                    side = 2 * pair + half
                    cluster, scale, offset = numbers[side]
                    part = score[:, half * LANES : (half + 1) * LANES]
                    weight = jnp.where(ids_ref[rows, :] == cluster, 0.0, other_ref[rows, :])
                    value = jnp.exp2((part * scale - offset) + weight)
                    accs[side] += jnp.sum(value.reshape(height // 8, 8, LANES), axis=0)
        for entry, acc in zip(sides, accs):
            row = pl.ds(slot_ref[entry], 1)
            out_ref[row, :] = out_ref[row, :] + jnp.sum(acc, axis=0, keepdims=True)
        return carry

    lax.fori_loop(0, (q_count + wide - 1) // wide, query_blocks, 0)


def last_kernel(chunks, wide, slot_ref, number_ref, qv, prev_ref, r_ref, out_ref):
    height = chunks * LANES
    table = r_ref[pl.ds(height, TABLE), pl.ds(0, LANES)].astype(jnp.float32)
    ids = [table[c : c + 1, :] for c in range(chunks)]
    other = [jnp.where(row < 0.0, DEAD, -4.0) for row in ids]
    out_ref[...] = prev_ref[...]

    for group in range(number_ref.shape[0] // (3 * wide)):
        score = lax.dot_general(
            qv[wide * group * LANES : wide * (group + 1) * LANES, :],
            r_ref[pl.ds(0, height), :],
            (((1,), (1,)), ((), ())),
            preferred_element_type=jnp.float32,
        )
        for side in range(wide):
            entry = wide * group + side
            cluster, scale, offset = (number_ref[3 * entry + i] for i in range(3))
            acc = jnp.zeros((LANES, LANES), jnp.float32)
            for c in range(chunks):
                part = score[side * LANES : (side + 1) * LANES, c * LANES : (c + 1) * LANES]
                bias = jnp.where(ids[c] == cluster, 0.0, other[c]) - offset
                acc = acc + jnp.exp2(part * scale + bias)
            row = pl.ds(slot_ref[entry], 1)
            out_ref[row, :] = out_ref[row, :] + jnp.sum(acc.T, axis=0, keepdims=True)


def first_call(chunks, qblocks, pieces, wide, given, payloads):
    width = payloads[0].shape[1]
    slots = 4 * qblocks
    rows = len(payloads) * chunks * LANES
    return pl.pallas_call(
        functools.partial(first_kernel, chunks, qblocks, pieces, wide),
        out_shape=(
            jax.ShapeDtypeStruct((slots + 8, LANES), jnp.float32),
            jax.ShapeDtypeStruct((slots * LANES, width), jnp.bfloat16),
            jax.ShapeDtypeStruct((slots + 8,), jnp.int32),
            jax.ShapeDtypeStruct((3 * slots,), jnp.float32),
        ),
        in_specs=[SMEM] + [VMEM] * (len(given) - 1 + len(payloads)),
        out_specs=(VMEM, VMEM, SMEM, SMEM),
        scratch_shapes=[
            pltpu.VMEM((8, LANES), jnp.int32),
            pltpu.SMEM((8, LANES), jnp.int32),
            pltpu.VMEM((rows, LANES), jnp.float32),
            pltpu.VMEM((rows, LANES), jnp.float32),
            pltpu.SemaphoreType.DMA,
        ],
        compiler_params=PARAMS,
        cost_estimate=cost(1, 1),
    )(*given, *payloads)


def last_call(chunks, wide, slots, numbers, packed, totals, payload):
    return pl.pallas_call(
        functools.partial(last_kernel, chunks, wide),
        out_shape=jax.ShapeDtypeStruct(totals.shape, jnp.float32),
        in_specs=[SMEM] * 2 + [VMEM] * 3,
        out_specs=VMEM,
        compiler_params=PARAMS,
        cost_estimate=cost(1, 1),
    )(slots, numbers, packed, totals, payload)


def per_device(
    queries,
    query_block_cluster,
    block_count,
    references,
    ref_cluster,
    ref_rows,
    cluster_beta,
    cluster_member_count,
):
    nblk, nhelper = lax.axis_size("blk"), lax.axis_size("helper")
    helper = lax.axis_index("helper").astype(jnp.int32)
    qblocks = query_block_cluster.shape[0]
    rows, width = references.shape
    tiles = rows // LANES
    chunks = tiles // nhelper
    sources = nblk // 2

    q_partner = swap(queries, "blk")
    by_chunk = references.reshape(chunks, nhelper, LANES, width)
    own = lax.dynamic_index_in_dim(by_chunk, helper, 1, keepdims=False)
    own = pl.pallas_call(
        functools.partial(pack_kernel, nhelper),
        out_shape=jax.ShapeDtypeStruct((chunks * LANES + TABLE, width), jnp.bfloat16),
        in_specs=[SMEM] * 2 + [VMEM] * 2,
        out_specs=VMEM,
        compiler_params=PARAMS,
        cost_estimate=cost(1, 1),
    )(
        helper[None],
        ref_rows,
        ref_cluster.reshape(tiles, LANES),
        own.reshape(chunks * LANES, width),
    )

    held, mask = [own], sources - 1
    while mask:
        held = held + [trade(x, 2 * mask) for x in held]
        mask //= 2
    q_helper = swap(queries, "helper")

    beta = cluster_beta.reshape(1, -1)
    staged, beta = pl.pallas_call(
        stage_kernel,
        out_shape=[jax.ShapeDtypeStruct(x.shape, x.dtype) for x in (queries, beta)],
        in_specs=[VMEM] * 2,
        out_specs=[VMEM] * 2,
        compiler_params=PARAMS,
        cost_estimate=cost(1, 1),
    )(queries, beta)
    table = pl.pallas_call(
        table_kernel,
        out_shape=jax.ShapeDtypeStruct((8, LANES), jnp.int32),
        in_specs=[SMEM] * 2,
        out_specs=VMEM,
        compiler_params=PARAMS,
        cost_estimate=cost(1, 1),
    )(after(query_block_cluster, own, staged), block_count)
    q_tables = (table, swap(table, "helper"), swap(table, "blk"), swap_both(table))
    q_partner = after(q_partner, staged, *held[1:-1], *q_tables)
    half = qblocks // 2 * LANES
    q_both = [swap(q_partner[:half], "helper"), swap(q_partner[half:], "helper")]
    queries = (staged, q_helper, q_partner, *q_both)
    pieces = (1, 1, 1, 2)

    given = (beta, *queries, *q_tables)
    totals, packed, *plan = first_call(chunks, qblocks, pieces, 4, given, held[:-1])
    totals = last_call(chunks, 4, *plan, packed, totals, held[-1])
    totals = totals[: 4 * qblocks]
    totals = totals.reshape(4, qblocks, LANES)
    total = totals[0] + swap(totals[1], "helper") + swap(totals[2], "blk") + swap_both(totals[3])
    columns = jnp.arange(cluster_member_count.shape[0], dtype=jnp.int32)
    onehot = query_block_cluster[:, None] == columns[None, :]
    sizes = jnp.sum(jnp.where(onehot, cluster_member_count[None, :], 0), axis=1)
    density = jnp.log1p(total / sizes.astype(jnp.float32)[:, None])
    return density.reshape(qblocks * LANES)


def solution(mesh):
    in_specs = (
        P(("parts", "blk", "helper"), None),
        P(("parts", "blk", "helper")),
        P(("parts", "blk", "helper")),
        P(("parts", "blk"), None),
        P(("parts", "blk")),
        P(("parts", "blk")),
        P("parts"),
        P("parts"),
    )
    out_specs = P(("parts", "blk", "helper"))
    return jax.shard_map(
        per_device, mesh=mesh, in_specs=in_specs, out_specs=out_specs, check_vma=False
    )
```

```python
import functools
import math

import jax
import jax.numpy as jnp
from jax import lax
from jax.experimental import pallas as pl
from jax.experimental.pallas import tpu as pltpu
from jax.sharding import PartitionSpec as P

LANES = 128
TABLE = 8
LOG2E = 1.4426950408889634
DEAD = -1.0e30
SMEM = pl.BlockSpec(memory_space=pltpu.SMEM)
VMEM = pl.BlockSpec(memory_space=pltpu.VMEM)
PARAMS = pltpu.CompilerParams(vmem_limit_bytes=24 * 1024 * 1024)


def trade(value, mask):
    length = lax.axis_size("blk")
    return lax.ppermute(value, "blk", [(i, i ^ mask) for i in range(length)])


def swap(value, axis):
    length = lax.axis_size(axis)
    return lax.ppermute(value, axis, [(i, i ^ 1) for i in range(length)])


def swap_both(value):
    nblk, nhelper = lax.axis_size("blk"), lax.axis_size("helper")
    pairs = [(i, (i ^ nhelper) ^ 1) for i in range(nblk * nhelper)]
    return lax.ppermute(value, ("blk", "helper"), pairs)


def after(value, *others):
    return lax.optimization_barrier((value, *others))[0]


def cost(flops, moved):
    return pl.CostEstimate(flops=flops, bytes_accessed=moved, transcendentals=0)


def rows_of(index, count=1):
    return pl.ds(pl.multiple_of(index * LANES, LANES), count * LANES)


def pack_kernel(nhelper, helper_ref, live_ref, ids_ref, r_ref, out_ref):
    lane = lax.broadcasted_iota(jnp.int32, (TABLE, LANES), 1)
    row = lax.broadcasted_iota(jnp.int32, (TABLE, LANES), 0)
    table = jnp.full((TABLE, LANES), -1, jnp.int32)
    height = r_ref.shape[0]
    for c in range(height // LANES):
        tile = helper_ref[0] + nhelper * c
        ids = ids_ref[pl.ds(tile, 1), :]
        table = jnp.where(row == c, jnp.where(tile * LANES + lane < live_ref[0], ids, -1), table)
    out_ref[pl.ds(0, height), :] = r_ref[...]
    out_ref[pl.ds(height, TABLE), pl.ds(0, LANES)] = table.astype(jnp.float32).astype(jnp.bfloat16)


def table_kernel(clusters_ref, count_ref, out_ref):
    lane = lax.broadcasted_iota(jnp.int32, out_ref.shape, 1)
    qblocks = clusters_ref.shape[0]
    row = jnp.where(lane == qblocks, count_ref[0], 0)
    for k in range(qblocks):
        row = jnp.where(lane == k, clusters_ref[k], row)
    out_ref[...] = row


def stage_kernel(*refs):
    half = len(refs) // 2
    for source, out in zip(refs[:half], refs[half:]):
        out[...] = source[...]


def first_kernel(chunks, qblocks, pieces, wide, beta_ref, *refs):
    *given, out_ref, qv, slot_ref, number_ref, info_v, info, ids_ref, other_ref, info_sem = refs
    q_refs = []
    for n in pieces:
        q_refs.append(given[:n])
        given = given[n:]
    t_refs, r_refs = given[:4], given[4:]
    width = qv.shape[1]
    height = chunks * LANES
    slots = 4 * qblocks
    for s, t_ref in enumerate(t_refs):
        info_v[s : s + 1, :] = t_ref[0:1, :]
    copy = pltpu.make_async_copy(info_v, info, info_sem)
    copy.start()

    for s, r_ref in enumerate(r_refs):
        table = r_ref[pl.ds(height, TABLE), pl.ds(0, LANES)].astype(jnp.float32)
        for c in range(chunks):
            ids = jnp.broadcast_to(table[c : c + 1, :], (LANES, LANES)).T
            rows = pl.ds(s * height + c * LANES, LANES)
            ids_ref[rows, :] = ids
            other_ref[rows, :] = jnp.where(ids < 0.0, DEAD, -4.0)

    copy.wait()
    factor = LOG2E / math.sqrt(width)
    q_count = jnp.int32(0)
    for source in range(4):
        blocks = info[source, qblocks]

        def enter(block, carry, source=source, q_count=q_count):
            entry = q_count + block
            cluster = info[source, block]
            beta = beta_ref[0, cluster]
            slot_ref[entry] = source * qblocks + block
            number_ref[3 * entry] = cluster.astype(jnp.float32)
            number_ref[3 * entry + 1] = beta * factor
            number_ref[3 * entry + 2] = beta * beta * (0.5 * LOG2E)
            return carry

        lax.fori_loop(0, blocks, enter, 0)
        start = 0
        for piece in q_refs[source]:
            each = piece.shape[0] // LANES

            def move(block, carry, place=q_count + start, piece=piece):
                qv[rows_of(place + block), :] = piece[rows_of(block), :]
                return carry

            lax.fori_loop(0, jnp.clip(blocks - start, 0, each), move, 0)
            start += each
        q_count = q_count + blocks

    def spare(entry, carry):
        slot_ref[entry] = slots
        for i in range(3):
            number_ref[3 * entry + i] = 0.0
        return carry

    lax.fori_loop(q_count, slots, spare, 0)
    slot_ref[slots] = q_count
    out_ref[...] = jnp.zeros_like(out_ref)

    def query_blocks(group, carry):
        sides = [wide * group + side for side in range(wide)]
        numbers = [[number_ref[3 * entry + i] for i in range(3)] for entry in sides]
        accs = [jnp.zeros((8, LANES), jnp.float32) for _ in range(wide)]
        for s, r_ref in enumerate(r_refs):
            tile = r_ref[pl.ds(0, height), :]
            rows = pl.ds(s * height, height)
            for pair in range(wide // 2):
                score = lax.dot_general(
                    tile,
                    qv[rows_of(wide * group + 2 * pair, 2), :],
                    (((1,), (1,)), ((), ())),
                    preferred_element_type=jnp.float32,
                )
                for half in range(2):
                    side = 2 * pair + half
                    cluster, scale, offset = numbers[side]
                    part = score[:, half * LANES : (half + 1) * LANES]
                    weight = jnp.where(ids_ref[rows, :] == cluster, 0.0, other_ref[rows, :])
                    value = jnp.exp2((part * scale - offset) + weight)
                    accs[side] += jnp.sum(value.reshape(height // 8, 8, LANES), axis=0)
        for entry, acc in zip(sides, accs):
            row = pl.ds(slot_ref[entry], 1)
            out_ref[row, :] = out_ref[row, :] + jnp.sum(acc, axis=0, keepdims=True)
        return carry

    lax.fori_loop(0, (q_count + wide - 1) // wide, query_blocks, 0)


def last_kernel(chunks, wide, slot_ref, number_ref, qv, prev_ref, r_ref, out_ref):
    height = chunks * LANES
    table = r_ref[pl.ds(height, TABLE), pl.ds(0, LANES)].astype(jnp.float32)
    ids = [table[c : c + 1, :] for c in range(chunks)]
    other = [jnp.where(row < 0.0, DEAD, -4.0) for row in ids]
    out_ref[...] = prev_ref[...]

    for group in range(number_ref.shape[0] // (3 * wide)):
        score = lax.dot_general(
            qv[wide * group * LANES : wide * (group + 1) * LANES, :],
            r_ref[pl.ds(0, height), :],
            (((1,), (1,)), ((), ())),
            preferred_element_type=jnp.float32,
        )
        for side in range(wide):
            entry = wide * group + side
            cluster, scale, offset = (number_ref[3 * entry + i] for i in range(3))
            acc = jnp.zeros((LANES, LANES), jnp.float32)
            for c in range(chunks):
                part = score[side * LANES : (side + 1) * LANES, c * LANES : (c + 1) * LANES]
                bias = jnp.where(ids[c] == cluster, 0.0, other[c]) - offset
                acc = acc + jnp.exp2(part * scale + bias)
            row = pl.ds(slot_ref[entry], 1)
            out_ref[row, :] = out_ref[row, :] + jnp.sum(acc.T, axis=0, keepdims=True)


def first_call(chunks, qblocks, pieces, wide, given, payloads):
    width = payloads[0].shape[1]
    slots = 4 * qblocks
    rows = len(payloads) * chunks * LANES
    return pl.pallas_call(
        functools.partial(first_kernel, chunks, qblocks, pieces, wide),
        out_shape=(
            jax.ShapeDtypeStruct((slots + 8, LANES), jnp.float32),
            jax.ShapeDtypeStruct((slots * LANES, width), jnp.bfloat16),
            jax.ShapeDtypeStruct((slots + 8,), jnp.int32),
            jax.ShapeDtypeStruct((3 * slots,), jnp.float32),
        ),
        in_specs=[SMEM] + [VMEM] * (len(given) - 1 + len(payloads)),
        out_specs=(VMEM, VMEM, SMEM, SMEM),
        scratch_shapes=[
            pltpu.VMEM((8, LANES), jnp.int32),
            pltpu.SMEM((8, LANES), jnp.int32),
            pltpu.VMEM((rows, LANES), jnp.float32),
            pltpu.VMEM((rows, LANES), jnp.float32),
            pltpu.SemaphoreType.DMA,
        ],
        compiler_params=PARAMS,
        cost_estimate=cost(1, 1),
    )(*given, *payloads)


def last_call(chunks, wide, slots, numbers, packed, totals, payload):
    return pl.pallas_call(
        functools.partial(last_kernel, chunks, wide),
        out_shape=jax.ShapeDtypeStruct(totals.shape, jnp.float32),
        in_specs=[SMEM] * 2 + [VMEM] * 3,
        out_specs=VMEM,
        compiler_params=PARAMS,
        cost_estimate=cost(1, 1),
    )(slots, numbers, packed, totals, payload)


def per_device(
    queries,
    query_block_cluster,
    block_count,
    references,
    ref_cluster,
    ref_rows,
    cluster_beta,
    cluster_member_count,
):
    nblk, nhelper = lax.axis_size("blk"), lax.axis_size("helper")
    helper = lax.axis_index("helper").astype(jnp.int32)
    qblocks = query_block_cluster.shape[0]
    rows, width = references.shape
    tiles = rows // LANES
    chunks = tiles // nhelper
    sources = nblk // 2

    q_partner = swap(queries, "blk")
    by_chunk = references.reshape(chunks, nhelper, LANES, width)
    own = lax.dynamic_index_in_dim(by_chunk, helper, 1, keepdims=False)
    own = pl.pallas_call(
        functools.partial(pack_kernel, nhelper),
        out_shape=jax.ShapeDtypeStruct((chunks * LANES + TABLE, width), jnp.bfloat16),
        in_specs=[SMEM] * 2 + [VMEM] * 2,
        out_specs=VMEM,
        compiler_params=PARAMS,
        cost_estimate=cost(1, 1),
    )(
        helper[None],
        ref_rows,
        ref_cluster.reshape(tiles, LANES),
        own.reshape(chunks * LANES, width),
    )

    held, mask = [own], sources // 2
    while mask:
        held = held + [trade(x, 2 * mask) for x in held]
        mask //= 2
    q_helper = swap(queries, "helper")

    beta = cluster_beta.reshape(1, -1)
    staged, beta = pl.pallas_call(
        stage_kernel,
        out_shape=[jax.ShapeDtypeStruct(x.shape, x.dtype) for x in (queries, beta)],
        in_specs=[VMEM] * 2,
        out_specs=[VMEM] * 2,
        compiler_params=PARAMS,
        cost_estimate=cost(1, 1),
    )(queries, beta)
    table = pl.pallas_call(
        table_kernel,
        out_shape=jax.ShapeDtypeStruct((8, LANES), jnp.int32),
        in_specs=[SMEM] * 2,
        out_specs=VMEM,
        compiler_params=PARAMS,
        cost_estimate=cost(1, 1),
    )(after(query_block_cluster, own, staged), block_count)
    q_tables = (table, swap(table, "helper"), swap(table, "blk"), swap_both(table))
    q_partner = after(q_partner, staged, *held[1:-1], *q_tables)
    half = qblocks // 2 * LANES
    q_both = [swap(q_partner[:half], "helper"), swap(q_partner[half:], "helper")]
    queries = (staged, q_helper, q_partner, *q_both)
    pieces = (1, 1, 1, 2)

    given = (beta, *queries, *q_tables)
    totals, packed, *plan = first_call(chunks, qblocks, pieces, 4, given, held[:-1])
    totals = last_call(chunks, 4, *plan, packed, totals, held[-1])
    totals = totals[: 4 * qblocks]
    totals = totals.reshape(4, qblocks, LANES)
    total = totals[0] + swap(totals[1], "helper") + swap(totals[2], "blk") + swap_both(totals[3])
    columns = jnp.arange(cluster_member_count.shape[0], dtype=jnp.int32)
    onehot = query_block_cluster[:, None] == columns[None, :]
    sizes = jnp.sum(jnp.where(onehot, cluster_member_count[None, :], 0), axis=1)
    density = jnp.log1p(total / sizes.astype(jnp.float32)[:, None])
    return density.reshape(qblocks * LANES)


def solution(mesh):
    in_specs = (
        P(("parts", "blk", "helper"), None),
        P(("parts", "blk", "helper")),
        P(("parts", "blk", "helper")),
        P(("parts", "blk"), None),
        P(("parts", "blk")),
        P(("parts", "blk")),
        P("parts"),
        P("parts"),
    )
    out_specs = P(("parts", "blk", "helper"))
    return jax.shard_map(
        per_device, mesh=mesh, in_specs=in_specs, out_specs=out_specs, check_vma=False
    )
```

```python
import functools
import math

import jax
import jax.numpy as jnp
from jax import lax
from jax.experimental import pallas as pl
from jax.experimental.pallas import tpu as pltpu
from jax.sharding import PartitionSpec as P

LANES = 128
TABLE = 8
LOG2E = 1.4426950408889634
DEAD = -1.0e30
SMEM = pl.BlockSpec(memory_space=pltpu.SMEM)
VMEM = pl.BlockSpec(memory_space=pltpu.VMEM)
PARAMS = pltpu.CompilerParams(vmem_limit_bytes=24 * 1024 * 1024)


def trade(value, mask):
    length = lax.axis_size("blk")
    return lax.ppermute(value, "blk", [(i, i ^ mask) for i in range(length)])


def swap(value, axis):
    length = lax.axis_size(axis)
    return lax.ppermute(value, axis, [(i, i ^ 1) for i in range(length)])


def swap_both(value):
    nblk, nhelper = lax.axis_size("blk"), lax.axis_size("helper")
    pairs = [(i, (i ^ nhelper) ^ 1) for i in range(nblk * nhelper)]
    return lax.ppermute(value, ("blk", "helper"), pairs)


def after(value, *others):
    return lax.optimization_barrier((value, *others))[0]


def cost(flops, moved):
    return pl.CostEstimate(flops=flops, bytes_accessed=moved, transcendentals=0)


def rows_of(index, count=1):
    return pl.ds(pl.multiple_of(index * LANES, LANES), count * LANES)


def pack_kernel(nhelper, helper_ref, live_ref, ids_ref, r_ref, out_ref):
    lane = lax.broadcasted_iota(jnp.int32, (TABLE, LANES), 1)
    row = lax.broadcasted_iota(jnp.int32, (TABLE, LANES), 0)
    table = jnp.full((TABLE, LANES), -1, jnp.int32)
    height = r_ref.shape[0]
    for c in range(height // LANES):
        tile = helper_ref[0] + nhelper * c
        ids = ids_ref[pl.ds(tile, 1), :]
        table = jnp.where(row == c, jnp.where(tile * LANES + lane < live_ref[0], ids, -1), table)
    out_ref[pl.ds(0, height), :] = r_ref[...]
    out_ref[pl.ds(height, TABLE), pl.ds(0, LANES)] = table.astype(jnp.float32).astype(jnp.bfloat16)


def table_kernel(clusters_ref, count_ref, out_ref):
    lane = lax.broadcasted_iota(jnp.int32, out_ref.shape, 1)
    qblocks = clusters_ref.shape[0]
    row = jnp.where(lane == qblocks, count_ref[0], 0)
    for k in range(qblocks):
        row = jnp.where(lane == k, clusters_ref[k], row)
    out_ref[...] = row


def stage_kernel(*refs):
    half = len(refs) // 2
    for source, out in zip(refs[:half], refs[half:]):
        out[...] = source[...]


def first_kernel(chunks, qblocks, pieces, wide, beta_ref, *refs):
    *given, out_ref, qv, slot_ref, number_ref, info_v, info, ids_ref, other_ref, info_sem = refs
    q_refs = []
    for n in pieces:
        q_refs.append(given[:n])
        given = given[n:]
    t_refs, r_refs = given[:4], given[4:]
    width = qv.shape[1]
    height = chunks * LANES
    slots = 4 * qblocks
    for s, t_ref in enumerate(t_refs):
        info_v[s : s + 1, :] = t_ref[0:1, :]
    copy = pltpu.make_async_copy(info_v, info, info_sem)
    copy.start()

    for s, r_ref in enumerate(r_refs):
        table = r_ref[pl.ds(height, TABLE), pl.ds(0, LANES)].astype(jnp.float32)
        for c in range(chunks):
            ids = jnp.broadcast_to(table[c : c + 1, :], (LANES, LANES)).T
            rows = pl.ds(s * height + c * LANES, LANES)
            ids_ref[rows, :] = ids
            other_ref[rows, :] = jnp.where(ids < 0.0, DEAD, -4.0)

    copy.wait()
    factor = LOG2E / math.sqrt(width)
    q_count = jnp.int32(0)
    for source in range(4):
        blocks = info[source, qblocks]

        def enter(block, carry, source=source, q_count=q_count):
            entry = q_count + block
            cluster = info[source, block]
            beta = beta_ref[0, cluster]
            slot_ref[entry] = (0, 2, 1, 3)[source] * qblocks + block
            number_ref[3 * entry] = cluster.astype(jnp.float32)
            number_ref[3 * entry + 1] = beta * factor
            number_ref[3 * entry + 2] = beta * beta * (0.5 * LOG2E)
            return carry

        lax.fori_loop(0, blocks, enter, 0)
        start = 0
        for piece in q_refs[source]:
            each = piece.shape[0] // LANES

            def move(block, carry, place=q_count + start, piece=piece):
                qv[rows_of(place + block), :] = piece[rows_of(block), :]
                return carry

            lax.fori_loop(0, jnp.clip(blocks - start, 0, each), move, 0)
            start += each
        q_count = q_count + blocks

    def spare(entry, carry):
        slot_ref[entry] = slots
        for i in range(3):
            number_ref[3 * entry + i] = 0.0
        return carry

    lax.fori_loop(q_count, slots, spare, 0)
    slot_ref[slots] = q_count
    out_ref[...] = jnp.zeros_like(out_ref)

    def query_blocks(group, carry):
        sides = [wide * group + side for side in range(wide)]
        numbers = [[number_ref[3 * entry + i] for i in range(3)] for entry in sides]
        accs = [jnp.zeros((8, LANES), jnp.float32) for _ in range(wide)]
        for s, r_ref in enumerate(r_refs):
            tile = r_ref[pl.ds(0, height), :]
            rows = pl.ds(s * height, height)
            for pair in range(wide // 2):
                score = lax.dot_general(
                    tile,
                    qv[rows_of(wide * group + 2 * pair, 2), :],
                    (((1,), (1,)), ((), ())),
                    preferred_element_type=jnp.float32,
                )
                for half in range(2):
                    side = 2 * pair + half
                    cluster, scale, offset = numbers[side]
                    part = score[:, half * LANES : (half + 1) * LANES]
                    weight = jnp.where(ids_ref[rows, :] == cluster, 0.0, other_ref[rows, :])
                    value = jnp.exp2((part * scale - offset) + weight)
                    accs[side] += jnp.sum(value.reshape(height // 8, 8, LANES), axis=0)
        for entry, acc in zip(sides, accs):
            row = pl.ds(slot_ref[entry], 1)
            out_ref[row, :] = out_ref[row, :] + jnp.sum(acc, axis=0, keepdims=True)
        return carry

    lax.fori_loop(0, (q_count + wide - 1) // wide, query_blocks, 0)


def last_kernel(chunks, wide, slot_ref, number_ref, qv, prev_ref, r_ref, keep_ref, give_ref, out_ref):
    height = chunks * LANES
    table = r_ref[pl.ds(height, TABLE), pl.ds(0, LANES)].astype(jnp.float32)
    ids = [table[c : c + 1, :] for c in range(chunks)]
    other = [jnp.where(row < 0.0, DEAD, -4.0) for row in ids]
    out_ref[...] = prev_ref[...]

    for group in range(number_ref.shape[0] // (3 * wide)):
        score = lax.dot_general(
            qv[wide * group * LANES : wide * (group + 1) * LANES, :],
            r_ref[pl.ds(0, height), :],
            (((1,), (1,)), ((), ())),
            preferred_element_type=jnp.float32,
        )
        for side in range(wide):
            entry = wide * group + side
            cluster, scale, offset = (number_ref[3 * entry + i] for i in range(3))
            acc = jnp.zeros((LANES, LANES), jnp.float32)
            for c in range(chunks):
                part = score[side * LANES : (side + 1) * LANES, c * LANES : (c + 1) * LANES]
                bias = jnp.where(ids[c] == cluster, 0.0, other[c]) - offset
                acc = acc + jnp.exp2(part * scale + bias)
            row = pl.ds(slot_ref[entry], 1)
            out_ref[row, :] = out_ref[row, :] + jnp.sum(acc.T, axis=0, keepdims=True)
    half = keep_ref.shape[0]
    keep_ref[...] = out_ref[pl.ds(0, half), :]
    give_ref[...] = out_ref[pl.ds(half, half), :]


def first_call(chunks, qblocks, pieces, wide, given, payloads):
    width = payloads[0].shape[1]
    slots = 4 * qblocks
    rows = len(payloads) * chunks * LANES
    return pl.pallas_call(
        functools.partial(first_kernel, chunks, qblocks, pieces, wide),
        out_shape=(
            jax.ShapeDtypeStruct((slots + 8, LANES), jnp.float32),
            jax.ShapeDtypeStruct((slots * LANES, width), jnp.bfloat16),
            jax.ShapeDtypeStruct((slots + 8,), jnp.int32),
            jax.ShapeDtypeStruct((3 * slots,), jnp.float32),
        ),
        in_specs=[SMEM] + [VMEM] * (len(given) - 1 + len(payloads)),
        out_specs=(VMEM, VMEM, SMEM, SMEM),
        scratch_shapes=[
            pltpu.VMEM((8, LANES), jnp.int32),
            pltpu.SMEM((8, LANES), jnp.int32),
            pltpu.VMEM((rows, LANES), jnp.float32),
            pltpu.VMEM((rows, LANES), jnp.float32),
            pltpu.SemaphoreType.DMA,
        ],
        compiler_params=PARAMS,
        cost_estimate=cost(1, 1),
    )(*given, *payloads)


def last_call(chunks, qblocks, wide, slots, numbers, packed, totals, payload):
    half = jax.ShapeDtypeStruct((2 * qblocks, LANES), jnp.float32)
    return pl.pallas_call(
        functools.partial(last_kernel, chunks, wide),
        out_shape=(half, half),
        in_specs=[SMEM] * 2 + [VMEM] * 3,
        out_specs=(VMEM, VMEM),
        scratch_shapes=[pltpu.VMEM(totals.shape, jnp.float32)],
        compiler_params=PARAMS,
        cost_estimate=cost(1, 1),
    )(slots, numbers, packed, totals, payload)


def per_device(
    queries,
    query_block_cluster,
    block_count,
    references,
    ref_cluster,
    ref_rows,
    cluster_beta,
    cluster_member_count,
):
    nblk, nhelper = lax.axis_size("blk"), lax.axis_size("helper")
    helper = lax.axis_index("helper").astype(jnp.int32)
    qblocks = query_block_cluster.shape[0]
    rows, width = references.shape
    tiles = rows // LANES
    chunks = tiles // nhelper
    sources = nblk // 2

    q_partner = swap(queries, "blk")
    by_chunk = references.reshape(chunks, nhelper, LANES, width)
    own = lax.dynamic_index_in_dim(by_chunk, helper, 1, keepdims=False)
    own = pl.pallas_call(
        functools.partial(pack_kernel, nhelper),
        out_shape=jax.ShapeDtypeStruct((chunks * LANES + TABLE, width), jnp.bfloat16),
        in_specs=[SMEM] * 2 + [VMEM] * 2,
        out_specs=VMEM,
        compiler_params=PARAMS,
        cost_estimate=cost(1, 1),
    )(
        helper[None],
        ref_rows,
        ref_cluster.reshape(tiles, LANES),
        own.reshape(chunks * LANES, width),
    )

    held, mask = [own], sources - 1
    while mask:
        held = held + [trade(x, 2 * mask) for x in held]
        mask //= 2
    q_helper = swap(queries, "helper")

    beta = cluster_beta.reshape(1, -1)
    staged, beta = pl.pallas_call(
        stage_kernel,
        out_shape=[jax.ShapeDtypeStruct(x.shape, x.dtype) for x in (queries, beta)],
        in_specs=[VMEM] * 2,
        out_specs=[VMEM] * 2,
        compiler_params=PARAMS,
        cost_estimate=cost(1, 1),
    )(queries, beta)
    table = pl.pallas_call(
        table_kernel,
        out_shape=jax.ShapeDtypeStruct((8, LANES), jnp.int32),
        in_specs=[SMEM] * 2,
        out_specs=VMEM,
        compiler_params=PARAMS,
        cost_estimate=cost(1, 1),
    )(after(query_block_cluster, own, staged), block_count)
    q_tables = (table, swap(table, "helper"), swap(table, "blk"), swap_both(table))
    q_partner = after(q_partner, staged, *held[1:-1], *q_tables)
    half = qblocks // 2 * LANES
    q_both = [swap(q_partner[:half], "helper"), swap(q_partner[half:], "helper")]
    queries = (staged, q_helper, q_partner, *q_both)
    pieces = (1, 1, 1, 2)

    given = (beta, *queries, *q_tables)
    totals, packed, *plan = first_call(chunks, qblocks, pieces, 4, given, held[:-1])
    keep, give = last_call(chunks, qblocks, 4, *plan, packed, totals, held[-1])
    keep = keep + swap(give, "helper")
    total = keep[:qblocks] + swap(keep, "blk")[qblocks:]
    columns = jnp.arange(cluster_member_count.shape[0], dtype=jnp.int32)
    onehot = query_block_cluster[:, None] == columns[None, :]
    sizes = jnp.sum(jnp.where(onehot, cluster_member_count[None, :], 0), axis=1)
    density = jnp.log1p(total / sizes.astype(jnp.float32)[:, None])
    return density.reshape(qblocks * LANES)


def solution(mesh):
    in_specs = (
        P(("parts", "blk", "helper"), None),
        P(("parts", "blk", "helper")),
        P(("parts", "blk", "helper")),
        P(("parts", "blk"), None),
        P(("parts", "blk")),
        P(("parts", "blk")),
        P("parts"),
        P("parts"),
    )
    out_specs = P(("parts", "blk", "helper"))
    return jax.shard_map(
        per_device, mesh=mesh, in_specs=in_specs, out_specs=out_specs, check_vma=False
    )
```

```python
import functools
import math

import jax
import jax.numpy as jnp
from jax import lax
from jax.experimental import pallas as pl
from jax.experimental.pallas import tpu as pltpu
from jax.sharding import PartitionSpec as P

LANES = 128
TABLE = 16
LOG2E = 1.4426950408889634
DEAD = -1.0e30
SMEM = pl.BlockSpec(memory_space=pltpu.SMEM)
VMEM = pl.BlockSpec(memory_space=pltpu.VMEM)
PARAMS = pltpu.CompilerParams(vmem_limit_bytes=24 * 1024 * 1024)


def trade(value, mask):
    length = lax.axis_size("blk")
    return lax.ppermute(value, "blk", [(i, i ^ mask) for i in range(length)])


def swap(value, axis):
    length = lax.axis_size(axis)
    return lax.ppermute(value, axis, [(i, i ^ 1) for i in range(length)])


def swap_both(value):
    nblk, nhelper = lax.axis_size("blk"), lax.axis_size("helper")
    pairs = [(i, (i ^ nhelper) ^ 1) for i in range(nblk * nhelper)]
    return lax.ppermute(value, ("blk", "helper"), pairs)


def after(value, *others):
    return lax.optimization_barrier((value, *others))[0]


def cost(flops, moved):
    return pl.CostEstimate(flops=flops, bytes_accessed=moved, transcendentals=0)


def rows_of(index, count=1):
    return pl.ds(pl.multiple_of(index * LANES, LANES), count * LANES)


def pack_kernel(nhelper, helper_ref, live_ref, ids_ref, r_ref, out_ref):
    lane = lax.broadcasted_iota(jnp.int32, (TABLE, LANES), 1)
    row = lax.broadcasted_iota(jnp.int32, (TABLE, LANES), 0)
    table = jnp.full((TABLE, LANES), -1, jnp.int32)
    height = r_ref.shape[0]
    for c in range(height // LANES):
        tile = helper_ref[0] + nhelper * c
        ids = ids_ref[pl.ds(tile, 1), :]
        table = jnp.where(row == c, jnp.where(tile * LANES + lane < live_ref[0], ids, -1), table)
    out_ref[pl.ds(0, height), :] = r_ref[...]
    out_ref[pl.ds(height, TABLE), pl.ds(0, LANES)] = table.astype(jnp.float32).astype(jnp.bfloat16)


def table_kernel(clusters_ref, count_ref, out_ref):
    lane = lax.broadcasted_iota(jnp.int32, out_ref.shape, 1)
    qblocks = clusters_ref.shape[0]
    row = jnp.where(lane == qblocks, count_ref[0], 0)
    for k in range(qblocks):
        row = jnp.where(lane == k, clusters_ref[k], row)
    out_ref[...] = row


def stage_kernel(*refs):
    half = len(refs) // 2
    for source, out in zip(refs[:half], refs[half:]):
        out[...] = source[...]


def first_kernel(chunks, qblocks, pieces, wide, beta_ref, *refs):
    *given, out_ref, qv, slot_ref, number_ref, info_v, info, ids_ref, other_ref, info_sem = refs
    q_refs = []
    for n in pieces:
        q_refs.append(given[:n])
        given = given[n:]
    t_refs, r_refs = given[:4], given[4:]
    width = qv.shape[1]
    height = chunks * LANES
    slots = 4 * qblocks
    for s, t_ref in enumerate(t_refs):
        info_v[s : s + 1, :] = t_ref[0:1, :]
    copy = pltpu.make_async_copy(info_v, info, info_sem)
    copy.start()

    for s, r_ref in enumerate(r_refs):
        table = r_ref[pl.ds(height, TABLE), pl.ds(0, LANES)].astype(jnp.float32)
        for c in range(chunks):
            ids = jnp.broadcast_to(table[c : c + 1, :], (LANES, LANES)).T
            rows = pl.ds(s * height + c * LANES, LANES)
            ids_ref[rows, :] = ids
            other_ref[rows, :] = jnp.where(ids < 0.0, DEAD, -4.0)

    copy.wait()
    factor = LOG2E / math.sqrt(width)
    q_count = jnp.int32(0)
    for source in range(4):
        blocks = info[source, qblocks]

        def enter(block, carry, source=source, q_count=q_count):
            entry = q_count + block
            cluster = info[source, block]
            beta = beta_ref[0, cluster]
            slot_ref[entry] = source * qblocks + block
            number_ref[3 * entry] = cluster.astype(jnp.float32)
            number_ref[3 * entry + 1] = beta * factor
            number_ref[3 * entry + 2] = beta * beta * (0.5 * LOG2E)
            return carry

        lax.fori_loop(0, blocks, enter, 0)
        start = 0
        for piece in q_refs[source]:
            each = piece.shape[0] // LANES

            def move(block, carry, place=q_count + start, piece=piece):
                qv[rows_of(place + block), :] = piece[rows_of(block), :]
                return carry

            lax.fori_loop(0, jnp.clip(blocks - start, 0, each), move, 0)
            start += each
        q_count = q_count + blocks

    def spare(entry, carry):
        slot_ref[entry] = slots
        for i in range(3):
            number_ref[3 * entry + i] = 0.0
        return carry

    lax.fori_loop(q_count, slots, spare, 0)
    slot_ref[slots] = q_count
    out_ref[...] = jnp.zeros_like(out_ref)

    def query_blocks(group, carry):
        sides = [wide * group + side for side in range(wide)]
        numbers = [[number_ref[3 * entry + i] for i in range(3)] for entry in sides]
        accs = [jnp.zeros((8, LANES), jnp.float32) for _ in range(wide)]
        for s, r_ref in enumerate(r_refs):
            tile = r_ref[pl.ds(0, height), :]
            rows = pl.ds(s * height, height)
            for pair in range(wide // 2):
                score = lax.dot_general(
                    tile,
                    qv[rows_of(wide * group + 2 * pair, 2), :],
                    (((1,), (1,)), ((), ())),
                    preferred_element_type=jnp.float32,
                )
                for half in range(2):
                    side = 2 * pair + half
                    cluster, scale, offset = numbers[side]
                    part = score[:, half * LANES : (half + 1) * LANES]
                    weight = jnp.where(ids_ref[rows, :] == cluster, 0.0, other_ref[rows, :])
                    value = jnp.exp2((part * scale - offset) + weight)
                    accs[side] += jnp.sum(value.reshape(height // 8, 8, LANES), axis=0)
        for entry, acc in zip(sides, accs):
            row = pl.ds(slot_ref[entry], 1)
            out_ref[row, :] = out_ref[row, :] + jnp.sum(acc, axis=0, keepdims=True)
        return carry

    lax.fori_loop(0, (q_count + wide - 1) // wide, query_blocks, 0)


def last_kernel(chunks, wide, slot_ref, number_ref, qv, prev_ref, r_ref, out_ref):
    height = chunks * LANES
    table = r_ref[pl.ds(height, TABLE), pl.ds(0, LANES)].astype(jnp.float32)
    ids = [table[c : c + 1, :] for c in range(chunks)]
    other = [jnp.where(row < 0.0, DEAD, -4.0) for row in ids]
    out_ref[...] = prev_ref[...]

    for group in range(number_ref.shape[0] // (3 * wide)):
        score = lax.dot_general(
            qv[wide * group * LANES : wide * (group + 1) * LANES, :],
            r_ref[pl.ds(0, height), :],
            (((1,), (1,)), ((), ())),
            preferred_element_type=jnp.float32,
        )
        for side in range(wide):
            entry = wide * group + side
            cluster, scale, offset = (number_ref[3 * entry + i] for i in range(3))
            acc = jnp.zeros((LANES, LANES), jnp.float32)
            for c in range(chunks):
                part = score[side * LANES : (side + 1) * LANES, c * LANES : (c + 1) * LANES]
                bias = jnp.where(ids[c] == cluster, 0.0, other[c]) - offset
                acc = acc + jnp.exp2(part * scale + bias)
            row = pl.ds(slot_ref[entry], 1)
            out_ref[row, :] = out_ref[row, :] + jnp.sum(acc.T, axis=0, keepdims=True)


def first_call(chunks, qblocks, pieces, wide, given, payloads):
    width = payloads[0].shape[1]
    slots = 4 * qblocks
    rows = len(payloads) * chunks * LANES
    return pl.pallas_call(
        functools.partial(first_kernel, chunks, qblocks, pieces, wide),
        out_shape=(
            jax.ShapeDtypeStruct((slots + 8, LANES), jnp.float32),
            jax.ShapeDtypeStruct((slots * LANES, width), jnp.bfloat16),
            jax.ShapeDtypeStruct((slots + 8,), jnp.int32),
            jax.ShapeDtypeStruct((3 * slots,), jnp.float32),
        ),
        in_specs=[SMEM] + [VMEM] * (len(given) - 1 + len(payloads)),
        out_specs=(VMEM, VMEM, SMEM, SMEM),
        scratch_shapes=[
            pltpu.VMEM((8, LANES), jnp.int32),
            pltpu.SMEM((8, LANES), jnp.int32),
            pltpu.VMEM((rows, LANES), jnp.float32),
            pltpu.VMEM((rows, LANES), jnp.float32),
            pltpu.SemaphoreType.DMA,
        ],
        compiler_params=PARAMS,
        cost_estimate=cost(1, 1),
    )(*given, *payloads)


def last_call(chunks, wide, slots, numbers, packed, totals, payload):
    return pl.pallas_call(
        functools.partial(last_kernel, chunks, wide),
        out_shape=jax.ShapeDtypeStruct(totals.shape, jnp.float32),
        in_specs=[SMEM] * 2 + [VMEM] * 3,
        out_specs=VMEM,
        compiler_params=PARAMS,
        cost_estimate=cost(1, 1),
    )(slots, numbers, packed, totals, payload)


def per_device(
    queries,
    query_block_cluster,
    block_count,
    references,
    ref_cluster,
    ref_rows,
    cluster_beta,
    cluster_member_count,
):
    nblk, nhelper = lax.axis_size("blk"), lax.axis_size("helper")
    helper = lax.axis_index("helper").astype(jnp.int32)
    qblocks = query_block_cluster.shape[0]
    rows, width = references.shape
    tiles = rows // LANES
    chunks = tiles // nhelper
    sources = nblk // 2

    q_partner = swap(queries, "blk")
    by_chunk = references.reshape(chunks, nhelper, LANES, width)
    own = lax.dynamic_index_in_dim(by_chunk, helper, 1, keepdims=False)
    own = pl.pallas_call(
        functools.partial(pack_kernel, nhelper),
        out_shape=jax.ShapeDtypeStruct((chunks * LANES + TABLE, width), jnp.bfloat16),
        in_specs=[SMEM] * 2 + [VMEM] * 2,
        out_specs=VMEM,
        compiler_params=PARAMS,
        cost_estimate=cost(1, 1),
    )(
        helper[None],
        ref_rows,
        ref_cluster.reshape(tiles, LANES),
        own.reshape(chunks * LANES, width),
    )

    held, mask = [own], sources - 1
    while mask:
        held = held + [trade(x, 2 * mask) for x in held]
        mask //= 2
    q_helper = swap(queries, "helper")

    beta = cluster_beta.reshape(1, -1)
    staged, beta = pl.pallas_call(
        stage_kernel,
        out_shape=[jax.ShapeDtypeStruct(x.shape, x.dtype) for x in (queries, beta)],
        in_specs=[VMEM] * 2,
        out_specs=[VMEM] * 2,
        compiler_params=PARAMS,
        cost_estimate=cost(1, 1),
    )(queries, beta)
    table = pl.pallas_call(
        table_kernel,
        out_shape=jax.ShapeDtypeStruct((8, LANES), jnp.int32),
        in_specs=[SMEM] * 2,
        out_specs=VMEM,
        compiler_params=PARAMS,
        cost_estimate=cost(1, 1),
    )(after(query_block_cluster, own, staged), block_count)
    q_tables = (table, swap(table, "helper"), swap(table, "blk"), swap_both(table))
    q_partner = after(q_partner, staged, *held[1:-1], *q_tables)
    half = qblocks // 2 * LANES
    q_both = [swap(q_partner[:half], "helper"), swap(q_partner[half:], "helper")]
    queries = (staged, q_helper, q_partner, *q_both)
    pieces = (1, 1, 1, 2)

    given = (beta, *queries, *q_tables)
    totals, packed, *plan = first_call(chunks, qblocks, pieces, 4, given, held[:-1])
    totals = last_call(chunks, 4, *plan, packed, totals, held[-1])
    totals = totals[: 4 * qblocks]
    totals = totals.reshape(4, qblocks, LANES)
    total = totals[0] + swap(totals[1], "helper") + swap(totals[2], "blk") + swap_both(totals[3])
    columns = jnp.arange(cluster_member_count.shape[0], dtype=jnp.int32)
    onehot = query_block_cluster[:, None] == columns[None, :]
    sizes = jnp.sum(jnp.where(onehot, cluster_member_count[None, :], 0), axis=1)
    density = jnp.log1p(total / sizes.astype(jnp.float32)[:, None])
    return density.reshape(qblocks * LANES)


def solution(mesh):
    in_specs = (
        P(("parts", "blk", "helper"), None),
        P(("parts", "blk", "helper")),
        P(("parts", "blk", "helper")),
        P(("parts", "blk"), None),
        P(("parts", "blk")),
        P(("parts", "blk")),
        P("parts"),
        P("parts"),
    )
    out_specs = P(("parts", "blk", "helper"))
    return jax.shard_map(
        per_device, mesh=mesh, in_specs=in_specs, out_specs=out_specs, check_vma=False
    )
```

```python
import functools
import math

import jax
import jax.numpy as jnp
from jax import lax
from jax.experimental import pallas as pl
from jax.experimental.pallas import tpu as pltpu
from jax.sharding import PartitionSpec as P

LANES = 128
TABLE = 16
LOG2E = 1.4426950408889634
DEAD = -1.0e30
SMEM = pl.BlockSpec(memory_space=pltpu.SMEM)
VMEM = pl.BlockSpec(memory_space=pltpu.VMEM)
PARAMS = pltpu.CompilerParams(vmem_limit_bytes=24 * 1024 * 1024)


def trade(value, mask):
    length = lax.axis_size("blk")
    return lax.ppermute(value, "blk", [(i, i ^ mask) for i in range(length)])


def swap(value, axis):
    length = lax.axis_size(axis)
    return lax.ppermute(value, axis, [(i, i ^ 1) for i in range(length)])


def swap_both(value):
    nblk, nhelper = lax.axis_size("blk"), lax.axis_size("helper")
    pairs = [(i, (i ^ nhelper) ^ 1) for i in range(nblk * nhelper)]
    return lax.ppermute(value, ("blk", "helper"), pairs)


def after(value, *others):
    return lax.optimization_barrier((value, *others))[0]


def cost(flops, moved):
    return pl.CostEstimate(flops=flops, bytes_accessed=moved, transcendentals=0)


def rows_of(index, count=1):
    return pl.ds(pl.multiple_of(index * LANES, LANES), count * LANES)


def unfolded(payload_ref, height):
    blocks = payload_ref.shape[0] // height
    return jnp.concatenate([payload_ref[pl.ds(b * height, height), :] for b in range(blocks)], axis=1)


def table_of(payload_ref):
    return payload_ref[pl.ds(payload_ref.shape[0] - TABLE, TABLE), :].astype(jnp.float32)


def pack_kernel(nhelper, helper_ref, live_ref, ids_ref, r_ref, out_ref):
    lane = lax.broadcasted_iota(jnp.int32, (TABLE, LANES), 1)
    row = lax.broadcasted_iota(jnp.int32, (TABLE, LANES), 0)
    table = jnp.full((TABLE, LANES), -1, jnp.int32)
    height = r_ref.shape[0]
    for c in range(height // LANES):
        tile = helper_ref[0] + nhelper * c
        ids = ids_ref[pl.ds(tile, 1), :]
        table = jnp.where(row == c, jnp.where(tile * LANES + lane < live_ref[0], ids, -1), table)
    blocks = r_ref.shape[1] // LANES
    for b in range(blocks):
        out_ref[pl.ds(b * height, height), :] = r_ref[:, pl.ds(b * LANES, LANES)]
    out_ref[pl.ds(blocks * height, TABLE), :] = table.astype(jnp.float32).astype(jnp.bfloat16)


def table_kernel(clusters_ref, count_ref, out_ref):
    lane = lax.broadcasted_iota(jnp.int32, out_ref.shape, 1)
    qblocks = clusters_ref.shape[0]
    row = jnp.where(lane == qblocks, count_ref[0], 0)
    for k in range(qblocks):
        row = jnp.where(lane == k, clusters_ref[k], row)
    out_ref[...] = row


def stage_kernel(*refs):
    half = len(refs) // 2
    for source, out in zip(refs[:half], refs[half:]):
        out[...] = source[...]


def first_kernel(chunks, qblocks, pieces, wide, beta_ref, *refs):
    *given, out_ref, qv, slot_ref, number_ref, info_v, info, ids_ref, other_ref, info_sem = refs
    q_refs = []
    for n in pieces:
        q_refs.append(given[:n])
        given = given[n:]
    t_refs, r_refs = given[:4], given[4:]
    width = qv.shape[1]
    height = chunks * LANES
    slots = 4 * qblocks
    for s, t_ref in enumerate(t_refs):
        info_v[s : s + 1, :] = t_ref[0:1, :]
    copy = pltpu.make_async_copy(info_v, info, info_sem)
    copy.start()

    for s, r_ref in enumerate(r_refs):
        table = table_of(r_ref)
        for c in range(chunks):
            ids = jnp.broadcast_to(table[c : c + 1, :], (LANES, LANES)).T
            rows = pl.ds(s * height + c * LANES, LANES)
            ids_ref[rows, :] = ids
            other_ref[rows, :] = jnp.where(ids < 0.0, DEAD, -4.0)

    copy.wait()
    factor = LOG2E / math.sqrt(width)
    q_count = jnp.int32(0)
    for source in range(4):
        blocks = info[source, qblocks]

        def enter(block, carry, source=source, q_count=q_count):
            entry = q_count + block
            cluster = info[source, block]
            beta = beta_ref[0, cluster]
            slot_ref[entry] = source * qblocks + block
            number_ref[3 * entry] = cluster.astype(jnp.float32)
            number_ref[3 * entry + 1] = beta * factor
            number_ref[3 * entry + 2] = beta * beta * (0.5 * LOG2E)
            return carry

        lax.fori_loop(0, blocks, enter, 0)
        start = 0
        for piece in q_refs[source]:
            each = piece.shape[0] // LANES

            def move(block, carry, place=q_count + start, piece=piece):
                qv[rows_of(place + block), :] = piece[rows_of(block), :]
                return carry

            lax.fori_loop(0, jnp.clip(blocks - start, 0, each), move, 0)
            start += each
        q_count = q_count + blocks

    def spare(entry, carry):
        slot_ref[entry] = slots
        for i in range(3):
            number_ref[3 * entry + i] = 0.0
        return carry

    lax.fori_loop(q_count, slots, spare, 0)
    slot_ref[slots] = q_count
    out_ref[...] = jnp.zeros_like(out_ref)

    def query_blocks(group, carry):
        sides = [wide * group + side for side in range(wide)]
        numbers = [[number_ref[3 * entry + i] for i in range(3)] for entry in sides]
        accs = [jnp.zeros((8, LANES), jnp.float32) for _ in range(wide)]
        for s, r_ref in enumerate(r_refs):
            tile = unfolded(r_ref, height)
            rows = pl.ds(s * height, height)
            for pair in range(wide // 2):
                score = lax.dot_general(
                    tile,
                    qv[rows_of(wide * group + 2 * pair, 2), :],
                    (((1,), (1,)), ((), ())),
                    preferred_element_type=jnp.float32,
                )
                for half in range(2):
                    side = 2 * pair + half
                    cluster, scale, offset = numbers[side]
                    part = score[:, half * LANES : (half + 1) * LANES]
                    weight = jnp.where(ids_ref[rows, :] == cluster, 0.0, other_ref[rows, :])
                    value = jnp.exp2((part * scale - offset) + weight)
                    accs[side] += jnp.sum(value.reshape(height // 8, 8, LANES), axis=0)
        for entry, acc in zip(sides, accs):
            row = pl.ds(slot_ref[entry], 1)
            out_ref[row, :] = out_ref[row, :] + jnp.sum(acc, axis=0, keepdims=True)
        return carry

    lax.fori_loop(0, (q_count + wide - 1) // wide, query_blocks, 0)


def last_kernel(chunks, wide, slot_ref, number_ref, qv, prev_ref, r_ref, out_ref):
    height = chunks * LANES
    table = table_of(r_ref)
    ids = [table[c : c + 1, :] for c in range(chunks)]
    other = [jnp.where(row < 0.0, DEAD, -4.0) for row in ids]
    tile = unfolded(r_ref, height)
    out_ref[...] = prev_ref[...]

    for group in range(number_ref.shape[0] // (3 * wide)):
        score = lax.dot_general(
            qv[wide * group * LANES : wide * (group + 1) * LANES, :],
            tile,
            (((1,), (1,)), ((), ())),
            preferred_element_type=jnp.float32,
        )
        for side in range(wide):
            entry = wide * group + side
            cluster, scale, offset = (number_ref[3 * entry + i] for i in range(3))
            acc = jnp.zeros((LANES, LANES), jnp.float32)
            for c in range(chunks):
                part = score[side * LANES : (side + 1) * LANES, c * LANES : (c + 1) * LANES]
                bias = jnp.where(ids[c] == cluster, 0.0, other[c]) - offset
                acc = acc + jnp.exp2(part * scale + bias)
            row = pl.ds(slot_ref[entry], 1)
            out_ref[row, :] = out_ref[row, :] + jnp.sum(acc.T, axis=0, keepdims=True)


def first_call(chunks, qblocks, pieces, wide, given, payloads):
    width = given[1].shape[1]
    slots = 4 * qblocks
    rows = len(payloads) * chunks * LANES
    return pl.pallas_call(
        functools.partial(first_kernel, chunks, qblocks, pieces, wide),
        out_shape=(
            jax.ShapeDtypeStruct((slots + 8, LANES), jnp.float32),
            jax.ShapeDtypeStruct((slots * LANES, width), jnp.bfloat16),
            jax.ShapeDtypeStruct((slots + 8,), jnp.int32),
            jax.ShapeDtypeStruct((3 * slots,), jnp.float32),
        ),
        in_specs=[SMEM] + [VMEM] * (len(given) - 1 + len(payloads)),
        out_specs=(VMEM, VMEM, SMEM, SMEM),
        scratch_shapes=[
            pltpu.VMEM((8, LANES), jnp.int32),
            pltpu.SMEM((8, LANES), jnp.int32),
            pltpu.VMEM((rows, LANES), jnp.float32),
            pltpu.VMEM((rows, LANES), jnp.float32),
            pltpu.SemaphoreType.DMA,
        ],
        compiler_params=PARAMS,
        cost_estimate=cost(1, 1),
    )(*given, *payloads)


def last_call(chunks, wide, slots, numbers, packed, totals, payload):
    return pl.pallas_call(
        functools.partial(last_kernel, chunks, wide),
        out_shape=jax.ShapeDtypeStruct(totals.shape, jnp.float32),
        in_specs=[SMEM] * 2 + [VMEM] * 3,
        out_specs=VMEM,
        compiler_params=PARAMS,
        cost_estimate=cost(1, 1),
    )(slots, numbers, packed, totals, payload)


def per_device(
    queries,
    query_block_cluster,
    block_count,
    references,
    ref_cluster,
    ref_rows,
    cluster_beta,
    cluster_member_count,
):
    nblk, nhelper = lax.axis_size("blk"), lax.axis_size("helper")
    helper = lax.axis_index("helper").astype(jnp.int32)
    qblocks = query_block_cluster.shape[0]
    rows, width = references.shape
    tiles = rows // LANES
    chunks = tiles // nhelper
    sources = nblk // 2

    q_partner = swap(queries, "blk")
    by_chunk = references.reshape(chunks, nhelper, LANES, width)
    own = lax.dynamic_index_in_dim(by_chunk, helper, 1, keepdims=False)
    own = pl.pallas_call(
        functools.partial(pack_kernel, nhelper),
        out_shape=jax.ShapeDtypeStruct((width // LANES * chunks * LANES + TABLE, LANES), jnp.bfloat16),
        in_specs=[SMEM] * 2 + [VMEM] * 2,
        out_specs=VMEM,
        compiler_params=PARAMS,
        cost_estimate=cost(1, 1),
    )(
        helper[None],
        ref_rows,
        ref_cluster.reshape(tiles, LANES),
        own.reshape(chunks * LANES, width),
    )

    held, mask = [own], sources - 1
    while mask:
        held = held + [trade(x, 2 * mask) for x in held]
        mask //= 2
    q_helper = swap(queries, "helper")

    beta = cluster_beta.reshape(1, -1)
    staged, beta = pl.pallas_call(
        stage_kernel,
        out_shape=[jax.ShapeDtypeStruct(x.shape, x.dtype) for x in (queries, beta)],
        in_specs=[VMEM] * 2,
        out_specs=[VMEM] * 2,
        compiler_params=PARAMS,
        cost_estimate=cost(1, 1),
    )(queries, beta)
    table = pl.pallas_call(
        table_kernel,
        out_shape=jax.ShapeDtypeStruct((8, LANES), jnp.int32),
        in_specs=[SMEM] * 2,
        out_specs=VMEM,
        compiler_params=PARAMS,
        cost_estimate=cost(1, 1),
    )(after(query_block_cluster, own, staged), block_count)
    q_tables = (table, swap(table, "helper"), swap(table, "blk"), swap_both(table))
    q_partner = after(q_partner, staged, *held[1:-1], *q_tables)
    half = qblocks // 2 * LANES
    q_both = [swap(q_partner[:half], "helper"), swap(q_partner[half:], "helper")]
    queries = (staged, q_helper, q_partner, *q_both)
    pieces = (1, 1, 1, 2)

    given = (beta, *queries, *q_tables)
    totals, packed, *plan = first_call(chunks, qblocks, pieces, 4, given, held[:-1])
    totals = last_call(chunks, 4, *plan, packed, totals, held[-1])
    totals = totals[: 4 * qblocks]
    totals = totals.reshape(4, qblocks, LANES)
    total = totals[0] + swap(totals[1], "helper") + swap(totals[2], "blk") + swap_both(totals[3])
    columns = jnp.arange(cluster_member_count.shape[0], dtype=jnp.int32)
    onehot = query_block_cluster[:, None] == columns[None, :]
    sizes = jnp.sum(jnp.where(onehot, cluster_member_count[None, :], 0), axis=1)
    density = jnp.log1p(total / sizes.astype(jnp.float32)[:, None])
    return density.reshape(qblocks * LANES)


def solution(mesh):
    in_specs = (
        P(("parts", "blk", "helper"), None),
        P(("parts", "blk", "helper")),
        P(("parts", "blk", "helper")),
        P(("parts", "blk"), None),
        P(("parts", "blk")),
        P(("parts", "blk")),
        P("parts"),
        P("parts"),
    )
    out_specs = P(("parts", "blk", "helper"))
    return jax.shard_map(
        per_device, mesh=mesh, in_specs=in_specs, out_specs=out_specs, check_vma=False
    )
```

```python
import functools
import math

import jax
import jax.numpy as jnp
from jax import lax
from jax.experimental import pallas as pl
from jax.experimental.pallas import tpu as pltpu
from jax.sharding import PartitionSpec as P

LANES = 128
TABLE = 16
LOG2E = 1.4426950408889634
DEAD = -1.0e30
SMEM = pl.BlockSpec(memory_space=pltpu.SMEM)
VMEM = pl.BlockSpec(memory_space=pltpu.VMEM)
PARAMS = pltpu.CompilerParams(vmem_limit_bytes=24 * 1024 * 1024)


def trade(value, mask):
    length = lax.axis_size("blk")
    return lax.ppermute(value, "blk", [(i, i ^ mask) for i in range(length)])


def swap(value, axis):
    length = lax.axis_size(axis)
    return lax.ppermute(value, axis, [(i, i ^ 1) for i in range(length)])


def swap_both(value):
    nblk, nhelper = lax.axis_size("blk"), lax.axis_size("helper")
    pairs = [(i, (i ^ nhelper) ^ 1) for i in range(nblk * nhelper)]
    return lax.ppermute(value, ("blk", "helper"), pairs)


def after(value, *others):
    return lax.optimization_barrier((value, *others))[0]


def cost(flops, moved):
    return pl.CostEstimate(flops=flops, bytes_accessed=moved, transcendentals=0)


def rows_of(index, count=1):
    return pl.ds(pl.multiple_of(index * LANES, LANES), count * LANES)


def unfolded(payload_ref, height):
    blocks = payload_ref.shape[0] // height
    return jnp.concatenate([payload_ref[pl.ds(b * height, height), :] for b in range(blocks)], axis=1)


def table_of(payload_ref):
    return payload_ref[pl.ds(payload_ref.shape[0] - TABLE, TABLE), :].astype(jnp.float32)


def pack_kernel(nhelper, helper_ref, live_ref, ids_ref, r_ref, out_ref):
    lane = lax.broadcasted_iota(jnp.int32, (TABLE, LANES), 1)
    row = lax.broadcasted_iota(jnp.int32, (TABLE, LANES), 0)
    table = jnp.full((TABLE, LANES), -1, jnp.int32)
    height = r_ref.shape[0]
    for c in range(height // LANES):
        tile = helper_ref[0] + nhelper * c
        ids = ids_ref[pl.ds(tile, 1), :]
        table = jnp.where(row == c, jnp.where(tile * LANES + lane < live_ref[0], ids, -1), table)
    blocks = r_ref.shape[1] // LANES
    for b in range(blocks):
        out_ref[pl.ds(b * height, height), :] = r_ref[:, pl.ds(b * LANES, LANES)]
    out_ref[pl.ds(blocks * height, TABLE), :] = table.astype(jnp.float32).astype(jnp.bfloat16)


def table_kernel(clusters_ref, count_ref, out_ref):
    lane = lax.broadcasted_iota(jnp.int32, out_ref.shape, 1)
    qblocks = clusters_ref.shape[0]
    row = jnp.where(lane == qblocks, count_ref[0], 0)
    for k in range(qblocks):
        row = jnp.where(lane == k, clusters_ref[k], row)
    out_ref[...] = row


def stage_kernel(*refs):
    half = len(refs) // 2
    for source, out in zip(refs[:half], refs[half:]):
        out[...] = source[...]


def first_kernel(chunks, qblocks, pieces, wide, beta_ref, *refs):
    *given, out_ref, qv, number_ref, info_v, info, ids_ref, other_ref, info_sem = refs
    q_refs = []
    for n in pieces:
        q_refs.append(given[:n])
        given = given[n:]
    t_refs, r_refs = given[:4], given[4:]
    width = qv.shape[1]
    height = chunks * LANES
    slots = 4 * qblocks
    for s, t_ref in enumerate(t_refs):
        info_v[s : s + 1, :] = t_ref[0:1, :]
    copy = pltpu.make_async_copy(info_v, info, info_sem)
    copy.start()

    for s, r_ref in enumerate(r_refs):
        table = table_of(r_ref)
        for c in range(chunks):
            ids = jnp.broadcast_to(table[c : c + 1, :], (LANES, LANES)).T
            rows = pl.ds(s * height + c * LANES, LANES)
            ids_ref[rows, :] = ids
            other_ref[rows, :] = jnp.where(ids < 0.0, DEAD, -4.0)

    copy.wait()
    factor = LOG2E / math.sqrt(width)
    q_count = jnp.int32(0)
    for source in range(4):
        blocks = info[source, qblocks]

        def enter(block, carry, source=source, q_count=q_count):
            entry = q_count + block
            cluster = info[source, block]
            beta = beta_ref[0, cluster]
            number_ref[4 * entry] = cluster.astype(jnp.float32)
            number_ref[4 * entry + 1] = beta * factor
            number_ref[4 * entry + 2] = beta * beta * (0.5 * LOG2E)
            number_ref[4 * entry + 3] = jnp.float32(source * qblocks) + block.astype(jnp.float32)
            return carry

        lax.fori_loop(0, blocks, enter, 0)
        start = 0
        for piece in q_refs[source]:
            each = piece.shape[0] // LANES

            def move(block, carry, place=q_count + start, piece=piece):
                qv[rows_of(place + block), :] = piece[rows_of(block), :]
                return carry

            lax.fori_loop(0, jnp.clip(blocks - start, 0, each), move, 0)
            start += each
        q_count = q_count + blocks

    def spare(entry, carry):
        number_ref[4 * entry + 3] = float(slots)
        for i in range(3):
            number_ref[4 * entry + i] = 0.0
        return carry

    lax.fori_loop(q_count, slots, spare, 0)
    out_ref[...] = jnp.zeros_like(out_ref)

    def query_blocks(group, carry):
        sides = [wide * group + side for side in range(wide)]
        numbers = [[number_ref[4 * entry + i] for i in range(3)] for entry in sides]
        accs = [jnp.zeros((8, LANES), jnp.float32) for _ in range(wide)]
        for s, r_ref in enumerate(r_refs):
            tile = unfolded(r_ref, height)
            rows = pl.ds(s * height, height)
            for pair in range(wide // 2):
                score = lax.dot_general(
                    tile,
                    qv[rows_of(wide * group + 2 * pair, 2), :],
                    (((1,), (1,)), ((), ())),
                    preferred_element_type=jnp.float32,
                )
                for half in range(2):
                    side = 2 * pair + half
                    cluster, scale, offset = numbers[side]
                    part = score[:, half * LANES : (half + 1) * LANES]
                    weight = jnp.where(ids_ref[rows, :] == cluster, 0.0, other_ref[rows, :])
                    value = jnp.exp2((part * scale - offset) + weight)
                    accs[side] += jnp.sum(value.reshape(height // 8, 8, LANES), axis=0)
        for entry, acc in zip(sides, accs):
            row = pl.ds(number_ref[4 * entry + 3].astype(jnp.int32), 1)
            out_ref[row, :] = out_ref[row, :] + jnp.sum(acc, axis=0, keepdims=True)
        return carry

    lax.fori_loop(0, (q_count + wide - 1) // wide, query_blocks, 0)


def last_kernel(chunks, wide, number_ref, qv, prev_ref, r_ref, out_ref):
    height = chunks * LANES
    table = table_of(r_ref)
    ids = [table[c : c + 1, :] for c in range(chunks)]
    other = [jnp.where(row < 0.0, DEAD, -4.0) for row in ids]
    tile = unfolded(r_ref, height)
    out_ref[...] = prev_ref[...]

    for group in range(number_ref.shape[0] // (4 * wide)):
        score = lax.dot_general(
            qv[wide * group * LANES : wide * (group + 1) * LANES, :],
            tile,
            (((1,), (1,)), ((), ())),
            preferred_element_type=jnp.float32,
        )
        for side in range(wide):
            entry = wide * group + side
            cluster, scale, offset = (number_ref[4 * entry + i] for i in range(3))
            acc = jnp.zeros((LANES, LANES), jnp.float32)
            for c in range(chunks):
                part = score[side * LANES : (side + 1) * LANES, c * LANES : (c + 1) * LANES]
                bias = jnp.where(ids[c] == cluster, 0.0, other[c]) - offset
                acc = acc + jnp.exp2(part * scale + bias)
            row = pl.ds(number_ref[4 * entry + 3].astype(jnp.int32), 1)
            out_ref[row, :] = out_ref[row, :] + jnp.sum(acc.T, axis=0, keepdims=True)


def first_call(chunks, qblocks, pieces, wide, given, payloads):
    width = given[1].shape[1]
    slots = 4 * qblocks
    rows = len(payloads) * chunks * LANES
    return pl.pallas_call(
        functools.partial(first_kernel, chunks, qblocks, pieces, wide),
        out_shape=(
            jax.ShapeDtypeStruct((slots + 8, LANES), jnp.float32),
            jax.ShapeDtypeStruct((slots * LANES, width), jnp.bfloat16),
            jax.ShapeDtypeStruct((4 * slots,), jnp.float32),
        ),
        in_specs=[SMEM] + [VMEM] * (len(given) - 1 + len(payloads)),
        out_specs=(VMEM, VMEM, SMEM),
        scratch_shapes=[
            pltpu.VMEM((8, LANES), jnp.int32),
            pltpu.SMEM((8, LANES), jnp.int32),
            pltpu.VMEM((rows, LANES), jnp.float32),
            pltpu.VMEM((rows, LANES), jnp.float32),
            pltpu.SemaphoreType.DMA,
        ],
        compiler_params=PARAMS,
        cost_estimate=cost(1, 1),
    )(*given, *payloads)


def last_call(chunks, wide, numbers, packed, totals, payload):
    return pl.pallas_call(
        functools.partial(last_kernel, chunks, wide),
        out_shape=jax.ShapeDtypeStruct(totals.shape, jnp.float32),
        in_specs=[SMEM] + [VMEM] * 3,
        out_specs=VMEM,
        compiler_params=PARAMS,
        cost_estimate=cost(1, 1),
    )(numbers, packed, totals, payload)


def per_device(
    queries,
    query_block_cluster,
    block_count,
    references,
    ref_cluster,
    ref_rows,
    cluster_beta,
    cluster_member_count,
):
    nblk, nhelper = lax.axis_size("blk"), lax.axis_size("helper")
    helper = lax.axis_index("helper").astype(jnp.int32)
    qblocks = query_block_cluster.shape[0]
    rows, width = references.shape
    tiles = rows // LANES
    chunks = tiles // nhelper
    sources = nblk // 2

    q_partner = swap(queries, "blk")
    by_chunk = references.reshape(chunks, nhelper, LANES, width)
    own = lax.dynamic_index_in_dim(by_chunk, helper, 1, keepdims=False)
    own = pl.pallas_call(
        functools.partial(pack_kernel, nhelper),
        out_shape=jax.ShapeDtypeStruct((width // LANES * chunks * LANES + TABLE, LANES), jnp.bfloat16),
        in_specs=[SMEM] * 2 + [VMEM] * 2,
        out_specs=VMEM,
        compiler_params=PARAMS,
        cost_estimate=cost(1, 1),
    )(
        helper[None],
        ref_rows,
        ref_cluster.reshape(tiles, LANES),
        own.reshape(chunks * LANES, width),
    )

    held, mask = [own], sources - 1
    while mask:
        held = held + [trade(x, 2 * mask) for x in held]
        mask //= 2
    q_helper = swap(queries, "helper")

    beta = cluster_beta.reshape(1, -1)
    staged, beta = pl.pallas_call(
        stage_kernel,
        out_shape=[jax.ShapeDtypeStruct(x.shape, x.dtype) for x in (queries, beta)],
        in_specs=[VMEM] * 2,
        out_specs=[VMEM] * 2,
        compiler_params=PARAMS,
        cost_estimate=cost(1, 1),
    )(queries, beta)
    table = pl.pallas_call(
        table_kernel,
        out_shape=jax.ShapeDtypeStruct((8, LANES), jnp.int32),
        in_specs=[SMEM] * 2,
        out_specs=VMEM,
        compiler_params=PARAMS,
        cost_estimate=cost(1, 1),
    )(after(query_block_cluster, own, staged), block_count)
    q_tables = (table, swap(table, "helper"), swap(table, "blk"), swap_both(table))
    q_partner = after(q_partner, staged, *held[1:-1], *q_tables)
    half = qblocks // 2 * LANES
    q_both = [swap(q_partner[:half], "helper"), swap(q_partner[half:], "helper")]
    queries = (staged, q_helper, q_partner, *q_both)
    pieces = (1, 1, 1, 2)

    given = (beta, *queries, *q_tables)
    totals, packed, numbers = first_call(chunks, qblocks, pieces, 4, given, held[:-1])
    totals = last_call(chunks, 8, numbers, packed, totals, held[-1])
    totals = totals[: 4 * qblocks]
    totals = totals.reshape(4, qblocks, LANES)
    total = totals[0] + swap(totals[1], "helper") + swap(totals[2], "blk") + swap_both(totals[3])
    columns = jnp.arange(cluster_member_count.shape[0], dtype=jnp.int32)
    onehot = query_block_cluster[:, None] == columns[None, :]
    sizes = jnp.sum(jnp.where(onehot, cluster_member_count[None, :], 0), axis=1)
    density = jnp.log1p(total / sizes.astype(jnp.float32)[:, None])
    return density.reshape(qblocks * LANES)


def solution(mesh):
    in_specs = (
        P(("parts", "blk", "helper"), None),
        P(("parts", "blk", "helper")),
        P(("parts", "blk", "helper")),
        P(("parts", "blk"), None),
        P(("parts", "blk")),
        P(("parts", "blk")),
        P("parts"),
        P("parts"),
    )
    out_specs = P(("parts", "blk", "helper"))
    return jax.shard_map(
        per_device, mesh=mesh, in_specs=in_specs, out_specs=out_specs, check_vma=False
    )
```

```python
import functools
import math

import jax
import jax.numpy as jnp
from jax import lax
from jax.experimental import pallas as pl
from jax.experimental.pallas import tpu as pltpu
from jax.sharding import PartitionSpec as P

LANES = 128
TABLE = 16
LOG2E = 1.4426950408889634
DEAD = -1.0e30
SMEM = pl.BlockSpec(memory_space=pltpu.SMEM)
VMEM = pl.BlockSpec(memory_space=pltpu.VMEM)
PARAMS = pltpu.CompilerParams(vmem_limit_bytes=24 * 1024 * 1024)


def trade(value, mask):
    length = lax.axis_size("blk")
    return lax.ppermute(value, "blk", [(i, i ^ mask) for i in range(length)])


def swap(value, axis):
    length = lax.axis_size(axis)
    return lax.ppermute(value, axis, [(i, i ^ 1) for i in range(length)])


def swap_both(value):
    nblk, nhelper = lax.axis_size("blk"), lax.axis_size("helper")
    pairs = [(i, (i ^ nhelper) ^ 1) for i in range(nblk * nhelper)]
    return lax.ppermute(value, ("blk", "helper"), pairs)


def after(value, *others):
    return lax.optimization_barrier((value, *others))[0]


def cost(flops, moved):
    return pl.CostEstimate(flops=flops, bytes_accessed=moved, transcendentals=0)


def rows_of(index, count=1):
    return pl.ds(pl.multiple_of(index * LANES, LANES), count * LANES)


def unfolded(payload_ref, height):
    blocks = payload_ref.shape[0] // height
    return jnp.concatenate([payload_ref[pl.ds(b * height, height), :] for b in range(blocks)], axis=1)


def table_of(payload_ref):
    return payload_ref[pl.ds(payload_ref.shape[0] - TABLE, TABLE), :].astype(jnp.float32)


def pack_kernel(nhelper, helper_ref, live_ref, ids_ref, r_ref, out_ref):
    lane = lax.broadcasted_iota(jnp.int32, (TABLE, LANES), 1)
    row = lax.broadcasted_iota(jnp.int32, (TABLE, LANES), 0)
    table = jnp.full((TABLE, LANES), -1, jnp.int32)
    height = r_ref.shape[0]
    for c in range(height // LANES):
        tile = helper_ref[0] + nhelper * c
        ids = ids_ref[pl.ds(tile, 1), :]
        table = jnp.where(row == c, jnp.where(tile * LANES + lane < live_ref[0], ids, -1), table)
    blocks = r_ref.shape[1] // LANES
    for b in range(blocks):
        out_ref[pl.ds(b * height, height), :] = r_ref[:, pl.ds(b * LANES, LANES)]
    out_ref[pl.ds(blocks * height, TABLE), :] = table.astype(jnp.float32).astype(jnp.bfloat16)


def table_kernel(clusters_ref, count_ref, out_ref):
    lane = lax.broadcasted_iota(jnp.int32, out_ref.shape, 1)
    qblocks = clusters_ref.shape[0]
    row = jnp.where(lane == qblocks, count_ref[0], 0)
    for k in range(qblocks):
        row = jnp.where(lane == k, clusters_ref[k], row)
    out_ref[...] = row


def stage_kernel(*refs):
    half = len(refs) // 2
    for source, out in zip(refs[:half], refs[half:]):
        out[...] = source[...]


def first_kernel(chunks, qblocks, pieces, wide, beta_ref, *refs):
    *given, out_ref, qv, slot_ref, number_ref, info_v, info, ids_ref, other_ref, info_sem = refs
    q_refs = []
    for n in pieces:
        q_refs.append(given[:n])
        given = given[n:]
    t_refs, r_refs = given[:4], given[4:]
    width = qv.shape[1]
    height = chunks * LANES
    slots = 4 * qblocks
    for s, t_ref in enumerate(t_refs):
        info_v[s : s + 1, :] = t_ref[0:1, :]
    copy = pltpu.make_async_copy(info_v, info, info_sem)
    copy.start()

    for s, r_ref in enumerate(r_refs):
        table = table_of(r_ref)
        for c in range(chunks):
            ids = jnp.broadcast_to(table[c : c + 1, :], (LANES, LANES)).T
            rows = pl.ds(s * height + c * LANES, LANES)
            ids_ref[rows, :] = ids
            other_ref[rows, :] = jnp.where(ids < 0.0, DEAD, -4.0)

    copy.wait()
    factor = LOG2E / math.sqrt(width)
    q_count = jnp.int32(0)
    for source in range(4):
        blocks = info[source, qblocks]

        def enter(block, carry, source=source, q_count=q_count):
            entry = q_count + block
            cluster = info[source, block]
            beta = beta_ref[0, cluster]
            slot_ref[entry] = source * qblocks + block
            number_ref[3 * entry] = cluster.astype(jnp.float32)
            number_ref[3 * entry + 1] = beta * factor
            number_ref[3 * entry + 2] = beta * beta * (0.5 * LOG2E)
            return carry

        lax.fori_loop(0, blocks, enter, 0)
        start = 0
        for piece in q_refs[source]:
            each = piece.shape[0] // LANES

            def move(block, carry, place=q_count + start, piece=piece):
                qv[rows_of(place + block), :] = piece[rows_of(block), :]
                return carry

            lax.fori_loop(0, jnp.clip(blocks - start, 0, each), move, 0)
            start += each
        q_count = q_count + blocks

    def spare(entry, carry):
        slot_ref[entry] = slots
        for i in range(3):
            number_ref[3 * entry + i] = 0.0
        return carry

    lax.fori_loop(q_count, slots, spare, 0)
    slot_ref[slots] = q_count
    out_ref[...] = jnp.zeros_like(out_ref)

    def query_blocks(group, carry):
        sides = [wide * group + side for side in range(wide)]
        numbers = [[number_ref[3 * entry + i] for i in range(3)] for entry in sides]
        accs = [jnp.zeros((8, LANES), jnp.float32) for _ in range(wide)]
        for s, r_ref in enumerate(r_refs):
            tile = unfolded(r_ref, height)
            rows = pl.ds(s * height, height)
            for pair in range(wide // 2):
                score = lax.dot_general(
                    tile,
                    qv[rows_of(wide * group + 2 * pair, 2), :],
                    (((1,), (1,)), ((), ())),
                    preferred_element_type=jnp.float32,
                )
                for half in range(2):
                    side = 2 * pair + half
                    cluster, scale, offset = numbers[side]
                    part = score[:, half * LANES : (half + 1) * LANES]
                    weight = jnp.where(ids_ref[rows, :] == cluster, 0.0, other_ref[rows, :])
                    value = jnp.exp2((part * scale - offset) + weight)
                    accs[side] += jnp.sum(value.reshape(height // 8, 8, LANES), axis=0)
        for entry, acc in zip(sides, accs):
            row = pl.ds(slot_ref[entry], 1)
            out_ref[row, :] = out_ref[row, :] + jnp.sum(acc, axis=0, keepdims=True)
        return carry

    lax.fori_loop(0, (q_count + wide - 1) // wide, query_blocks, 0)


def last_kernel(chunks, wide, slot_ref, number_ref, qv, prev_ref, r_ref, out_ref):
    height = chunks * LANES
    table = table_of(r_ref)
    ids = [table[c : c + 1, :] for c in range(chunks)]
    other = [jnp.where(row < 0.0, DEAD, -4.0) for row in ids]
    tile = unfolded(r_ref, height)
    out_ref[...] = prev_ref[...]

    sums = []
    for group in range(number_ref.shape[0] // (3 * wide)):
        score = lax.dot_general(
            qv[wide * group * LANES : wide * (group + 1) * LANES, :],
            tile,
            (((1,), (1,)), ((), ())),
            preferred_element_type=jnp.float32,
        )
        for side in range(wide):
            entry = wide * group + side
            cluster, scale, offset = (number_ref[3 * entry + i] for i in range(3))
            acc = jnp.zeros((LANES, LANES), jnp.float32)
            for c in range(chunks):
                part = score[side * LANES : (side + 1) * LANES, c * LANES : (c + 1) * LANES]
                bias = jnp.where(ids[c] == cluster, 0.0, other[c]) - offset
                acc = acc + jnp.exp2(part * scale + bias)
            sums.append(jnp.sum(acc.T, axis=0, keepdims=True))
    for entry, total in enumerate(sums):
        row = pl.ds(slot_ref[entry], 1)
        out_ref[row, :] = out_ref[row, :] + total


def first_call(chunks, qblocks, pieces, wide, given, payloads):
    width = given[1].shape[1]
    slots = 4 * qblocks
    rows = len(payloads) * chunks * LANES
    return pl.pallas_call(
        functools.partial(first_kernel, chunks, qblocks, pieces, wide),
        out_shape=(
            jax.ShapeDtypeStruct((slots + 8, LANES), jnp.float32),
            jax.ShapeDtypeStruct((slots * LANES, width), jnp.bfloat16),
            jax.ShapeDtypeStruct((slots + 8,), jnp.int32),
            jax.ShapeDtypeStruct((3 * slots,), jnp.float32),
        ),
        in_specs=[SMEM] + [VMEM] * (len(given) - 1 + len(payloads)),
        out_specs=(VMEM, VMEM, SMEM, SMEM),
        scratch_shapes=[
            pltpu.VMEM((8, LANES), jnp.int32),
            pltpu.SMEM((8, LANES), jnp.int32),
            pltpu.VMEM((rows, LANES), jnp.float32),
            pltpu.VMEM((rows, LANES), jnp.float32),
            pltpu.SemaphoreType.DMA,
        ],
        compiler_params=PARAMS,
        cost_estimate=cost(1, 1),
    )(*given, *payloads)


def last_call(chunks, wide, slots, numbers, packed, totals, payload):
    return pl.pallas_call(
        functools.partial(last_kernel, chunks, wide),
        out_shape=jax.ShapeDtypeStruct(totals.shape, jnp.float32),
        in_specs=[SMEM] * 2 + [VMEM] * 3,
        out_specs=VMEM,
        compiler_params=PARAMS,
        cost_estimate=cost(1, 1),
    )(slots, numbers, packed, totals, payload)


def per_device(
    queries,
    query_block_cluster,
    block_count,
    references,
    ref_cluster,
    ref_rows,
    cluster_beta,
    cluster_member_count,
):
    nblk, nhelper = lax.axis_size("blk"), lax.axis_size("helper")
    helper = lax.axis_index("helper").astype(jnp.int32)
    qblocks = query_block_cluster.shape[0]
    rows, width = references.shape
    tiles = rows // LANES
    chunks = tiles // nhelper
    sources = nblk // 2

    q_partner = swap(queries, "blk")
    by_chunk = references.reshape(chunks, nhelper, LANES, width)
    own = lax.dynamic_index_in_dim(by_chunk, helper, 1, keepdims=False)
    own = pl.pallas_call(
        functools.partial(pack_kernel, nhelper),
        out_shape=jax.ShapeDtypeStruct((width // LANES * chunks * LANES + TABLE, LANES), jnp.bfloat16),
        in_specs=[SMEM] * 2 + [VMEM] * 2,
        out_specs=VMEM,
        compiler_params=PARAMS,
        cost_estimate=cost(1, 1),
    )(
        helper[None],
        ref_rows,
        ref_cluster.reshape(tiles, LANES),
        own.reshape(chunks * LANES, width),
    )

    held, mask = [own], sources - 1
    while mask:
        held = held + [trade(x, 2 * mask) for x in held]
        mask //= 2
    q_helper = swap(queries, "helper")

    beta = cluster_beta.reshape(1, -1)
    staged, beta = pl.pallas_call(
        stage_kernel,
        out_shape=[jax.ShapeDtypeStruct(x.shape, x.dtype) for x in (queries, beta)],
        in_specs=[VMEM] * 2,
        out_specs=[VMEM] * 2,
        compiler_params=PARAMS,
        cost_estimate=cost(1, 1),
    )(queries, beta)
    table = pl.pallas_call(
        table_kernel,
        out_shape=jax.ShapeDtypeStruct((8, LANES), jnp.int32),
        in_specs=[SMEM] * 2,
        out_specs=VMEM,
        compiler_params=PARAMS,
        cost_estimate=cost(1, 1),
    )(after(query_block_cluster, own, staged), block_count)
    q_tables = (table, swap(table, "helper"), swap(table, "blk"), swap_both(table))
    q_partner = after(q_partner, staged, *held[1:-1], *q_tables)
    half = qblocks // 2 * LANES
    q_both = [swap(q_partner[:half], "helper"), swap(q_partner[half:], "helper")]
    queries = (staged, q_helper, q_partner, *q_both)
    pieces = (1, 1, 1, 2)

    given = (beta, *queries, *q_tables)
    totals, packed, *plan = first_call(chunks, qblocks, pieces, 4, given, held[:-1])
    totals = last_call(chunks, 2, *plan, packed, totals, held[-1])
    totals = totals[: 4 * qblocks]
    totals = totals.reshape(4, qblocks, LANES)
    total = totals[0] + swap(totals[1], "helper") + swap(totals[2], "blk") + swap_both(totals[3])
    columns = jnp.arange(cluster_member_count.shape[0], dtype=jnp.int32)
    onehot = query_block_cluster[:, None] == columns[None, :]
    sizes = jnp.sum(jnp.where(onehot, cluster_member_count[None, :], 0), axis=1)
    density = jnp.log1p(total / sizes.astype(jnp.float32)[:, None])
    return density.reshape(qblocks * LANES)


def solution(mesh):
    in_specs = (
        P(("parts", "blk", "helper"), None),
        P(("parts", "blk", "helper")),
        P(("parts", "blk", "helper")),
        P(("parts", "blk"), None),
        P(("parts", "blk")),
        P(("parts", "blk")),
        P("parts"),
        P("parts"),
    )
    out_specs = P(("parts", "blk", "helper"))
    return jax.shard_map(
        per_device, mesh=mesh, in_specs=in_specs, out_specs=out_specs, check_vma=False
    )
```

```python
import functools
import math

import jax
import jax.numpy as jnp
from jax import lax
from jax.experimental import pallas as pl
from jax.experimental.pallas import tpu as pltpu
from jax.sharding import PartitionSpec as P

LANES = 128
TABLE = 16
LOG2E = 1.4426950408889634
DEAD = -1.0e30
SMEM = pl.BlockSpec(memory_space=pltpu.SMEM)
VMEM = pl.BlockSpec(memory_space=pltpu.VMEM)
PARAMS = pltpu.CompilerParams(vmem_limit_bytes=24 * 1024 * 1024)


def trade(value, mask):
    length = lax.axis_size("blk")
    return lax.ppermute(value, "blk", [(i, i ^ mask) for i in range(length)])


def swap(value, axis):
    length = lax.axis_size(axis)
    return lax.ppermute(value, axis, [(i, i ^ 1) for i in range(length)])


def swap_both(value):
    nblk, nhelper = lax.axis_size("blk"), lax.axis_size("helper")
    pairs = [(i, (i ^ nhelper) ^ 1) for i in range(nblk * nhelper)]
    return lax.ppermute(value, ("blk", "helper"), pairs)


def after(value, *others):
    return lax.optimization_barrier((value, *others))[0]


def cost(flops, moved):
    return pl.CostEstimate(flops=flops, bytes_accessed=moved, transcendentals=0)


def rows_of(index, count=1):
    return pl.ds(pl.multiple_of(index * LANES, LANES), count * LANES)


def unfolded(payload_ref, height):
    blocks = payload_ref.shape[0] // height
    return jnp.concatenate([payload_ref[pl.ds(b * height, height), :] for b in range(blocks)], axis=1)


def table_of(payload_ref):
    return payload_ref[pl.ds(payload_ref.shape[0] - TABLE, TABLE), :].astype(jnp.float32)


def pack_kernel(nhelper, helper_ref, live_ref, ids_ref, r_ref, out_ref):
    lane = lax.broadcasted_iota(jnp.int32, (TABLE, LANES), 1)
    row = lax.broadcasted_iota(jnp.int32, (TABLE, LANES), 0)
    table = jnp.full((TABLE, LANES), -1, jnp.int32)
    height = r_ref.shape[0]
    for c in range(height // LANES):
        tile = helper_ref[0] + nhelper * c
        ids = ids_ref[pl.ds(tile, 1), :]
        table = jnp.where(row == c, jnp.where(tile * LANES + lane < live_ref[0], ids, -1), table)
    blocks = r_ref.shape[1] // LANES
    for b in range(blocks):
        out_ref[pl.ds(b * height, height), :] = r_ref[:, pl.ds(b * LANES, LANES)]
    out_ref[pl.ds(blocks * height, TABLE), :] = table.astype(jnp.float32).astype(jnp.bfloat16)


def table_kernel(clusters_ref, count_ref, out_ref):
    lane = lax.broadcasted_iota(jnp.int32, out_ref.shape, 1)
    qblocks = clusters_ref.shape[0]
    row = jnp.where(lane == qblocks, count_ref[0], 0)
    for k in range(qblocks):
        row = jnp.where(lane == k, clusters_ref[k], row)
    out_ref[...] = row


def stage_kernel(*refs):
    half = len(refs) // 2
    for source, out in zip(refs[:half], refs[half:]):
        out[...] = source[...]


def first_kernel(chunks, qblocks, pieces, wide, beta_ref, *refs):
    *given, out_ref, qv, slot_ref, number_ref, info_v, info, ids_ref, other_ref, info_sem = refs
    q_refs = []
    for n in pieces:
        q_refs.append(given[:n])
        given = given[n:]
    t_refs, r_refs = given[:4], given[4:]
    width = qv.shape[1]
    height = chunks * LANES
    slots = 4 * qblocks
    for s, t_ref in enumerate(t_refs):
        info_v[s : s + 1, :] = t_ref[0:1, :]
    copy = pltpu.make_async_copy(info_v, info, info_sem)
    copy.start()

    for s, r_ref in enumerate(r_refs):
        table = table_of(r_ref)
        for c in range(chunks):
            ids = jnp.broadcast_to(table[c : c + 1, :], (LANES, LANES)).T
            rows = pl.ds(s * height + c * LANES, LANES)
            ids_ref[rows, :] = ids
            other_ref[rows, :] = jnp.where(ids < 0.0, DEAD, -4.0)

    copy.wait()
    factor = LOG2E / math.sqrt(width)
    q_count = jnp.int32(0)
    for source in range(4):
        blocks = info[source, qblocks]

        def enter(block, carry, source=source, q_count=q_count):
            entry = q_count + block
            cluster = info[source, block]
            beta = beta_ref[0, cluster]
            slot_ref[entry] = source * qblocks + block
            number_ref[3 * entry] = cluster.astype(jnp.float32)
            number_ref[3 * entry + 1] = beta * factor
            number_ref[3 * entry + 2] = beta * beta * (0.5 * LOG2E)
            return carry

        lax.fori_loop(0, blocks, enter, 0)
        start = 0
        for piece in q_refs[source]:
            each = piece.shape[0] // LANES

            def move(block, carry, place=q_count + start, piece=piece):
                qv[rows_of(place + block), :] = piece[rows_of(block), :]
                return carry

            lax.fori_loop(0, jnp.clip(blocks - start, 0, each), move, 0)
            start += each
        q_count = q_count + blocks

    def spare(entry, carry):
        slot_ref[entry] = slots
        for i in range(3):
            number_ref[3 * entry + i] = 0.0
        return carry

    lax.fori_loop(q_count, slots, spare, 0)
    slot_ref[slots] = q_count
    out_ref[...] = jnp.zeros_like(out_ref)

    def query_blocks(group, carry):
        sides = [wide * group + side for side in range(wide)]
        numbers = [[number_ref[3 * entry + i] for i in range(3)] for entry in sides]
        accs = [jnp.zeros((8, LANES), jnp.float32) for _ in range(wide)]
        for s, r_ref in enumerate(r_refs):
            tile = unfolded(r_ref, height)
            rows = pl.ds(s * height, height)
            for pair in range(wide // 2):
                score = lax.dot_general(
                    tile,
                    qv[rows_of(wide * group + 2 * pair, 2), :],
                    (((1,), (1,)), ((), ())),
                    preferred_element_type=jnp.float32,
                )
                for half in range(2):
                    side = 2 * pair + half
                    cluster, scale, offset = numbers[side]
                    part = score[:, half * LANES : (half + 1) * LANES]
                    weight = jnp.where(ids_ref[rows, :] == cluster, 0.0, other_ref[rows, :])
                    value = jnp.exp2((part * scale - offset) + weight)
                    accs[side] += jnp.sum(value.reshape(height // 8, 8, LANES), axis=0)
        for entry, acc in zip(sides, accs):
            row = pl.ds(slot_ref[entry], 1)
            out_ref[row, :] = out_ref[row, :] + jnp.sum(acc, axis=0, keepdims=True)
        return carry

    lax.fori_loop(0, (q_count + wide - 1) // wide, query_blocks, 0)


def last_kernel(chunks, wide, slot_ref, number_ref, qv, prev_ref, r_ref, out_ref):
    height = chunks * LANES
    table = table_of(r_ref)
    ids = [table[c : c + 1, :] for c in range(chunks)]
    other = [jnp.where(row < 0.0, DEAD, -4.0) for row in ids]
    tile = unfolded(r_ref, height)
    out_ref[...] = prev_ref[...]

    for group in range(number_ref.shape[0] // (3 * wide)):
        score = lax.dot_general(
            qv[wide * group * LANES : wide * (group + 1) * LANES, :],
            tile,
            (((1,), (1,)), ((), ())),
            preferred_element_type=jnp.float32,
        )
        for side in range(wide):
            entry = wide * group + side
            cluster, scale, offset = (number_ref[3 * entry + i] for i in range(3))
            acc = jnp.zeros((LANES, LANES), jnp.float32)
            for c in range(chunks):
                part = score[side * LANES : (side + 1) * LANES, c * LANES : (c + 1) * LANES]
                bias = jnp.where(ids[c] == cluster, 0.0, other[c]) - offset
                acc = acc + jnp.exp2(part * scale + bias)
            row = pl.ds(slot_ref[entry], 1)
            out_ref[row, :] = out_ref[row, :] + jnp.sum(acc.T, axis=0, keepdims=True)


def first_call(chunks, qblocks, pieces, wide, given, payloads):
    width = given[1].shape[1]
    slots = 4 * qblocks
    rows = len(payloads) * chunks * LANES
    return pl.pallas_call(
        functools.partial(first_kernel, chunks, qblocks, pieces, wide),
        out_shape=(
            jax.ShapeDtypeStruct((slots + 8, LANES), jnp.float32),
            jax.ShapeDtypeStruct((slots * LANES, width), jnp.bfloat16),
            jax.ShapeDtypeStruct((slots + 8,), jnp.int32),
            jax.ShapeDtypeStruct((3 * slots,), jnp.float32),
        ),
        in_specs=[SMEM] + [VMEM] * (len(given) - 1 + len(payloads)),
        out_specs=(VMEM, VMEM, SMEM, SMEM),
        scratch_shapes=[
            pltpu.VMEM((8, LANES), jnp.int32),
            pltpu.SMEM((8, LANES), jnp.int32),
            pltpu.VMEM((rows, LANES), jnp.float32),
            pltpu.VMEM((rows, LANES), jnp.float32),
            pltpu.SemaphoreType.DMA,
        ],
        compiler_params=PARAMS,
        cost_estimate=cost(1, 1),
    )(*given, *payloads)


def last_call(chunks, wide, slots, numbers, packed, totals, payload):
    return pl.pallas_call(
        functools.partial(last_kernel, chunks, wide),
        out_shape=jax.ShapeDtypeStruct(totals.shape, jnp.float32),
        in_specs=[SMEM] * 2 + [VMEM] * 3,
        out_specs=VMEM,
        compiler_params=PARAMS,
        cost_estimate=cost(1, 1),
    )(slots, numbers, packed, totals, payload)


def per_device(
    queries,
    query_block_cluster,
    block_count,
    references,
    ref_cluster,
    ref_rows,
    cluster_beta,
    cluster_member_count,
):
    nblk, nhelper = lax.axis_size("blk"), lax.axis_size("helper")
    helper = lax.axis_index("helper").astype(jnp.int32)
    qblocks = query_block_cluster.shape[0]
    rows, width = references.shape
    tiles = rows // LANES
    chunks = tiles // nhelper
    sources = nblk // 2

    q_partner = swap(queries, "blk")
    by_chunk = references.reshape(chunks, nhelper, LANES, width)
    own = lax.dynamic_index_in_dim(by_chunk, helper, 1, keepdims=False)
    own = pl.pallas_call(
        functools.partial(pack_kernel, nhelper),
        out_shape=jax.ShapeDtypeStruct((width // LANES * chunks * LANES + TABLE, LANES), jnp.bfloat16),
        in_specs=[SMEM] * 2 + [VMEM] * 2,
        out_specs=VMEM,
        compiler_params=PARAMS,
        cost_estimate=cost(1, 1),
    )(
        helper[None],
        ref_rows,
        ref_cluster.reshape(tiles, LANES),
        own.reshape(chunks * LANES, width),
    )

    held, mask = [own], sources - 1
    while mask:
        held = held + [trade(x, 2 * mask) for x in held]
        mask //= 2
    q_helper = swap(queries, "helper")

    beta = cluster_beta.reshape(1, -1)
    staged, beta = pl.pallas_call(
        stage_kernel,
        out_shape=[jax.ShapeDtypeStruct(x.shape, x.dtype) for x in (queries, beta)],
        in_specs=[VMEM] * 2,
        out_specs=[VMEM] * 2,
        compiler_params=PARAMS,
        cost_estimate=cost(1, 1),
    )(queries, beta)
    table = pl.pallas_call(
        table_kernel,
        out_shape=jax.ShapeDtypeStruct((8, LANES), jnp.int32),
        in_specs=[SMEM] * 2,
        out_specs=VMEM,
        compiler_params=PARAMS,
        cost_estimate=cost(1, 1),
    )(after(query_block_cluster, own, staged), block_count)
    q_tables = (table, swap(table, "helper"), swap(table, "blk"), swap_both(table))
    q_partner = after(q_partner, staged, *held[1:-1], *q_tables)
    half = qblocks // 2 * LANES
    q_both = [swap(q_partner[:half], "helper"), swap(q_partner[half:], "helper")]
    queries = (staged, q_helper, q_partner, *q_both)
    pieces = (1, 1, 1, 2)

    given = (beta, *queries, *q_tables)
    totals, packed, *plan = first_call(chunks, qblocks, pieces, 2, given, held[:-1])
    totals = last_call(chunks, 4, *plan, packed, totals, held[-1])
    totals = totals[: 4 * qblocks]
    totals = totals.reshape(4, qblocks, LANES)
    total = totals[0] + swap(totals[1], "helper") + swap(totals[2], "blk") + swap_both(totals[3])
    columns = jnp.arange(cluster_member_count.shape[0], dtype=jnp.int32)
    onehot = query_block_cluster[:, None] == columns[None, :]
    sizes = jnp.sum(jnp.where(onehot, cluster_member_count[None, :], 0), axis=1)
    density = jnp.log1p(total / sizes.astype(jnp.float32)[:, None])
    return density.reshape(qblocks * LANES)


def solution(mesh):
    in_specs = (
        P(("parts", "blk", "helper"), None),
        P(("parts", "blk", "helper")),
        P(("parts", "blk", "helper")),
        P(("parts", "blk"), None),
        P(("parts", "blk")),
        P(("parts", "blk")),
        P("parts"),
        P("parts"),
    )
    out_specs = P(("parts", "blk", "helper"))
    return jax.shard_map(
        per_device, mesh=mesh, in_specs=in_specs, out_specs=out_specs, check_vma=False
    )
```
